256 devices in a mesh: items: 64 (over z, y, core), rep: 4 (over x).
Axes of the slice: x: 4, y: 4, z: 8, core: 2. Of those that a mesh axis runs over, the one named last changes fastest.
Arguments:
- queries: bfloat16 [131072, 256], P(('items', 'rep')), may hold values from -60 to 60
- clusters: int32 [4096, 4], P(('items', 'rep')), may hold values from 0 to 63, all different within a row; in each aligned block of 16 rows (0 to 15, 16 to 31, ...) at most 2 rows name the same one
- positives: int32 [131072], P(('items', 'rep')), may hold values from 0 to 4095
- owner_of: int32 [64], replicated, may hold values from 0 to 63, each once
- table: float32 [64, 1024, 256], P('items'), may hold values from -1.2 to 1.2
- accum: float32 [64, 1024, 256], P('items'), may hold values from 0.1 to 10
Outputs:
- losses: float32 [131072], P(('items', 'rep'))
- query_grads: float32 [131072, 256], P(('items', 'rep'))
- new_table: float32 [64, 1024, 256], P('items')
- new_accum: float32 [64, 1024, 256], P('items')
The draws below stay inside these ranges and needn't reach their ends.
Inputs may be any that keep to these rules, and one draw needn't show every extreme that they name: Each row names 4 different clusters; within the rows of one device no cluster is named more than 2 times. `owner_of`: each cluster has its own slot. `positives`: a candidate index of the query's block.
All inputs are finite; a program needn't handle non-finite values.
Results may differ from the reference program's by a relative error of at most 0.0045.
The reference program's roundings to bfloat16 on the way (of `rows16` and `coeffs`) count: a program that leaves them out, or rounds other values in their place, can miss the bound.
Values may be sent and summed in bfloat16 or wider, within the bound.
No kernel may reach another device: no remote copies, remote signals or barrier semaphores. Data moves between devices by JAX's collectives and lax.ppermute only.
A program may use at most 128 MiB of HBM per device.

```python
import math
import jax
import jax.numpy as jnp
import numpy as np
from jax import lax

E = 256
CSIZE = 1024
PICK = 4
MOST = 2
CLUSTERS = 64
QB = 16
BQ = 32
BLOCKS = 4096
QUERIES = 131072


def draw_queries(key, part):
    key = jax.random.fold_in(key, 11)
    key_base, key_scale = jax.random.split(key)
    base = jax.random.truncated_normal(key_base, -6.0, 6.0, (QUERIES, E), jnp.float32)
    scale = jnp.exp(jax.random.uniform(key_scale, (QUERIES, 1), jnp.float32, math.log(0.5), math.log(2.0)))
    return (base * scale).astype(jnp.bfloat16)


def plant(entries, key, smallest, top_value):
    shape = entries.shape
    index_at = [jax.random.randint(jax.random.fold_in(key, axis), (), 0, shape[axis]) for axis in range(len(shape))]
    entries = entries.at[tuple(index_at)].set(smallest)
    longest = shape.index(max(shape))
    index_at[longest] = (index_at[longest] + 1) % shape[longest]
    return entries.at[tuple(index_at)].set(top_value)


def block_scale(rng, extent, cuts, low, top_value):
    level, own = 1.0, jax.random.fold_in(rng, 6)
    for axis_at, parts in cuts:
        steps = jnp.exp(jax.random.uniform(jax.random.fold_in(own, axis_at), (parts,), jnp.float32, low / len(cuts), top_value / len(cuts)))
        level = level * jnp.repeat(steps, extent[axis_at] // parts).reshape([-1 if axis == axis_at else 1 for axis in range(len(extent))])
    return level


def deal_out(key, own, number, rows, number_of, top, most, slope):
    ranking = jax.random.permutation(key, number_of)
    heavy_load, ordinary = shares(number_of, rows * top, most, slope, True), shares(number_of, rows * top, most, slope, False)
    places = jnp.arange(number_of)

    def named(lengths, rotation):
        used = int((lengths > 0).sum())
        fixed = max(1, used // 4)
        passed = fixed + (places - fixed + rotation * (used - fixed)) % max(1, number_of - fixed)
        return jnp.zeros((number_of,), jnp.int32).at[ranking[jnp.where(places < fixed, places, passed)]].set(jnp.asarray(lengths, jnp.int32))

    lengths = jnp.where(number % 4 == 0, named(heavy_load, number // 4), named(ordinary, number - number // 4 - 1))
    mixed = jax.random.permutation(jax.random.fold_in(own, 3), number_of)
    giver, taker = mixed[0:number_of // 2 * 2:2], mixed[1:number_of // 2 * 2:2]
    room = jnp.minimum(lengths[giver] - 1, most - lengths[taker]) // 2
    room = jnp.where((giver == ranking[0]) | (taker == ranking[0]) | (lengths[taker] == 0), 0, jnp.maximum(room, 0))
    passed = jax.random.randint(jax.random.fold_in(own, 4), (number_of // 2,), 0, 1 << 20) % (room + 1)
    lengths = lengths.at[giver].add(-passed).at[taker].add(passed)
    items = jnp.searchsorted(jnp.cumsum(lengths), jnp.arange(rows * top), side="right").astype(jnp.int32)
    grid = items.reshape(top, rows).T
    grid = grid[jax.random.permutation(jax.random.fold_in(own, 1), rows)]
    rotation = jax.random.randint(jax.random.fold_in(own, 2), (rows, 1), 0, top)
    return jnp.take_along_axis(grid, (jnp.arange(top)[None, :] + rotation) % top, axis=1)


def shares(amount, total, reach, skew, full):
    weights = [(1 << 20) // math.isqrt(rank ** skew) + 1 for rank in range(1, amount + 1)]
    largest = reach if full else min(reach, max(-(-total // amount), total * weights[0] // sum(weights)))
    least = 1 if total - largest >= amount - 1 else 0
    holding, rest = [largest] + [least] * (amount - 1), total - largest - least * (amount - 1)
    while rest > 0:
        free = [i for i in range(1, amount) if holding[i] < largest] or [i for i in range(1, amount) if holding[i] < reach]
        pool, remaining = sum([weights[i] for i in free]), rest
        for i in free:
            extra = min(reach - holding[i], max(1, remaining * weights[i] // pool), rest)
            holding[i] = holding[i] + extra
            rest = rest - extra
    return np.array(holding)


def bell_draw(own_key, shape, scale, reach, cuts=(), held_as=jnp.bfloat16):
    array = jax.random.normal(own_key, shape, jnp.float32) * scale
    if len(cuts) > 0:
        array = block_scale(own_key, shape, cuts, -0.22, 0.18) * array
    return jnp.clip(array, min=-reach, max=reach).astype(held_as)


def setup_inputs(seed: int = 0) -> dict:
    key_list = jax.random.split(jax.random.key(seed), 7)
    queries = draw_queries(jax.random.fold_in(key_list[6], 71), 0)
    clusters_keys = jax.random.split(jax.random.fold_in(key_list[1], 1), BLOCKS // QB)
    clusters_turns = jax.random.permutation(jax.random.fold_in(key_list[1], 3), BLOCKS // QB)
    clusters = jax.vmap(lambda own, number: deal_out(jax.random.fold_in(key_list[1], 2), own, number, QB, CLUSTERS, PICK, MOST, 2))(clusters_keys, clusters_turns).reshape((BLOCKS, PICK))
    positives = plant(jax.random.randint(key_list[2], (QUERIES,), 0, PICK * CSIZE), jax.random.fold_in(key_list[2], 1), 0, (PICK * CSIZE) - 1).astype(jnp.int32)
    owner_of = jax.random.permutation(key_list[3], CLUSTERS).astype(jnp.int32)
    table = bell_draw(key_list[4], (CLUSTERS, CSIZE, E), 0.2, 1.2, ((0, 64),), jnp.float32)
    accum = jnp.clip(jnp.exp(math.log(10.0) - 4.6051702 * jax.random.uniform(key_list[5], (CLUSTERS, CSIZE, E), jnp.float32) ** block_scale(key_list[5], (CLUSTERS, CSIZE, E), ((0, 64),), -0.2, 0.2)), 0.1, 10.0)
    return dict(queries=queries, clusters=clusters, positives=positives, owner_of=owner_of, table=table, accum=accum)


def reference(queries, clusters, positives, owner_of, table, accum):
    rows16 = table.astype(jnp.bfloat16)
    query_blocks = queries.reshape(BLOCKS, BQ, E)
    target_blocks = positives.reshape(BLOCKS, BQ)
    slot_lists = owner_of[clusters].astype(jnp.int32)
    candidates = jnp.arange(PICK * CSIZE, dtype=jnp.int32)

    def one_block(grads, inputs):
        block_rows, targets, slots = inputs
        gathered = rows16[slots].reshape(PICK * CSIZE, E)
        scores = lax.dot_general(block_rows, gathered, (((1,), (1,)), ((), ())), preferred_element_type=jnp.float32)
        highest = lax.optimization_barrier(jnp.max(scores, axis=1))
        lse = highest + jnp.log(lax.optimization_barrier(jnp.sum(jnp.exp(scores - highest[:, None]), axis=1)))
        is_target = candidates[None, :] == targets[:, None]
        picked = lax.optimization_barrier(jnp.sum(jnp.where(is_target, scores, jnp.float32(0.0)), axis=1))
        loss_rows = lse - picked
        coeffs = (jnp.exp(scores - lse[:, None]) - is_target.astype(jnp.float32)).astype(jnp.bfloat16)
        grad_rows = jnp.dot(coeffs, gathered, preferred_element_type=jnp.float32)
        pieces = jnp.einsum('bkc,be->kce', coeffs.reshape(BQ, PICK, CSIZE).astype(jnp.float32), block_rows.astype(jnp.float32))
        grads = grads.at[slots].add(pieces)
        return (grads, (loss_rows, grad_rows))
    start = jnp.zeros((CLUSTERS, CSIZE, E), jnp.float32)
    item_grads, (loss_all, grad_all) = lax.scan(one_block, start, (query_blocks, target_blocks, slot_lists))
    new_accum = accum + item_grads * item_grads
    new_table = table - 0.5 * item_grads / jnp.sqrt(new_accum)
    return (loss_all.reshape(QUERIES), grad_all.reshape(QUERIES, E), new_table, new_accum)
```

```python
import jax
import jax.numpy as jnp
from jax import lax
from jax.experimental import pallas as pl
from jax.experimental.pallas import tpu as pltpu
from jax.sharding import Mesh, PartitionSpec as P

MOST = 2
EMPTY = 1e30
NEAR = (0, 1, 7, 2)
FAR = (6, 3, 5, 4)
ORDER = NEAR + FAR
PLANE = ("y", "c")
F32 = jnp.float32
BF16 = jnp.bfloat16
NT = (((1,), (1,)), ((), ()))
TN = (((0,), (0,)), ((), ()))
TILE = 256


def shift(value, axis, step):
    size = lax.axis_size(axis)
    return lax.ppermute(value, axis, [(i, (i + step) % size) for i in range(size)])


def tile_ids(start, shape):
    return lax.broadcasted_iota(jnp.int32, shape, 0) + start


def forward_kernel(blk, q0, q1, q2, q3, t_ref, tgt_ref, p_ref, stat_ref, s_ref):
    step = pl.program_id(0)
    sources = (q0, q1, q2, q3)
    block_rows = q0.shape[1]
    for slot in range(8):
        b = blk[step * 8 + slot]
        p_ref[0, pl.ds(slot * block_rows, block_rows), :] = sources[slot // MOST][b]
    q = p_ref[0]
    items = t_ref.shape[1]
    width = q.shape[0]
    tgt = tgt_ref[0]
    high = jnp.full((8, width), -jnp.inf, F32)
    pick = jnp.zeros((8, width), F32)
    for start in range(0, items, TILE):
        s = lax.dot_general(t_ref[0, pl.ds(start, TILE), :], q, NT, preferred_element_type=F32)
        s_ref[pl.ds(start, TILE), :] = s
        high = jnp.maximum(high, jnp.max(s.reshape(TILE // 8, 8, width), axis=0))
        hit = jnp.where(tile_ids(start, s.shape) == tgt, s, 0.0)
        pick = pick + jnp.sum(hit.reshape(TILE // 8, 8, width), axis=0)
    top = jnp.max(high, axis=0, keepdims=True)
    mass = jnp.zeros((8, width), F32)
    for start in range(0, items, TILE):
        e = jnp.exp(s_ref[pl.ds(start, TILE), :] - top)
        mass = mass + jnp.sum(e.reshape(TILE // 8, 8, width), axis=0)
    stat_ref[0, 0:1, :] = top + jnp.log(jnp.sum(mass, axis=0, keepdims=True))
    stat_ref[0, 1:2, :] = jnp.sum(pick, axis=0, keepdims=True)


def forward(sources, blk, targets, tables):
    planes, items, features = tables.shape
    width = targets.shape[2]
    whole = pl.BlockSpec(sources[0].shape, lambda j, blk: (0, 0, 0))
    return pl.pallas_call(
        forward_kernel,
        grid_spec=pltpu.PrefetchScalarGridSpec(
            num_scalar_prefetch=1,
            grid=(planes,),
            in_specs=[whole] * 4
            + [
                pl.BlockSpec((1, items, features), lambda j, blk: (j, 0, 0)),
                pl.BlockSpec((1, 1, width), lambda j, blk: (j, 0, 0)),
            ],
            out_specs=[
                pl.BlockSpec((1, width, features), lambda j, blk: (j, 0, 0)),
                pl.BlockSpec((1, 2, width), lambda j, blk: (j, 0, 0)),
            ],
            scratch_shapes=[pltpu.VMEM((items, width), F32)],
        ),
        out_shape=[
            jax.ShapeDtypeStruct((planes, width, features), BF16),
            jax.ShapeDtypeStruct((planes, 2, width), F32),
        ],
        compiler_params=pltpu.CompilerParams(vmem_limit_bytes=24 << 20),
        cost_estimate=pl.CostEstimate(
            flops=2 * planes * width * items * features,
            bytes_accessed=planes * items * features * 2 + 3 * planes * width * features * 2,
            transcendentals=planes * width * items,
        ),
        name="forward",
    )(blk, *sources, tables, targets)


def query_kernel(blk, p_ref, t_ref, lse_ref, tgt_ref, g0, g1, g2, g3, c_ref, acc_ref):
    step = pl.program_id(0)

    @pl.when(step == 0)
    def _():
        acc_ref[...] = jnp.zeros_like(acc_ref)

    q = p_ref[0]
    lse = lse_ref[0]
    tgt = tgt_ref[0]
    items = t_ref.shape[1]
    for start in range(0, items, TILE):
        s = lax.dot_general(t_ref[0, pl.ds(start, TILE), :], q, NT, preferred_element_type=F32)
        e = jnp.exp(s - lse)
        c = jnp.where(tile_ids(start, s.shape) == tgt, e - 1.0, e)
        c_ref[pl.ds(start, TILE), :] = c.astype(BF16)
    g = lax.dot_general(c_ref[...], t_ref[0], TN, preferred_element_type=F32)
    block_rows = g0.shape[1]
    for slot in range(8):
        b = blk[step * 8 + slot]
        acc_ref[slot // MOST, b] += g[slot * block_rows:(slot + 1) * block_rows, :]

    @pl.when(step == pl.num_programs(0) - 1)
    def _():
        for i, out in enumerate((g0, g1, g2, g3)):
            out[...] = acc_ref[i].astype(BF16)


def query_parts(packed, blk, lse, targets, tables, blocks, block_rows):
    planes, items, features = tables.shape
    width = targets.shape[2]
    line = pl.BlockSpec((1, 1, width), lambda j, blk: (j, 0, 0))
    out = jax.ShapeDtypeStruct((blocks, block_rows, features), BF16)
    return pl.pallas_call(
        query_kernel,
        grid_spec=pltpu.PrefetchScalarGridSpec(
            num_scalar_prefetch=1,
            grid=(planes,),
            in_specs=[
                pl.BlockSpec((1, width, features), lambda j, blk: (j, 0, 0)),
                pl.BlockSpec((1, items, features), lambda j, blk: (j, 0, 0)),
                line,
                line,
            ],
            out_specs=[pl.BlockSpec(out.shape, lambda j, blk: (0, 0, 0))] * 4,
            scratch_shapes=[
                pltpu.VMEM((items, width), BF16),
                pltpu.VMEM((4, blocks, block_rows, features), F32),
            ],
        ),
        out_shape=[out] * 4,
        compiler_params=pltpu.CompilerParams(vmem_limit_bytes=24 << 20),
        cost_estimate=pl.CostEstimate(
            flops=4 * planes * width * items * features,
            bytes_accessed=planes * items * features * 2 + 2 * planes * width * features * 2,
            transcendentals=planes * width * items,
        ),
        name="query_parts",
    )(blk, packed, tables, lse, targets)


def item_kernel(x_ref, a_ref, b_ref, line_ref, t_ref, w_ref):
    step = pl.program_id(0)
    quarters = w_ref.shape[0]
    rows = w_ref.shape[1]
    mine = x_ref[0]
    pairs = []
    for i, ref in enumerate((a_ref, b_ref)):
        pairs.append((ref[0], line_ref[0, 2 * i:2 * i + 1, :], line_ref[0, 2 * i + 1:2 * i + 2, :]))
    for tile in range(quarters):
        total = None
        for q, lse, tgt in pairs:
            s = lax.dot_general(
                t_ref[pl.ds(tile * rows, rows), :], q, NT, preferred_element_type=F32
            )
            e = jnp.exp(s - lse)
            ids = tile_ids(tile * rows, s.shape)
            c = jnp.where(ids == tgt.astype(jnp.int32), e - 1.0, e).astype(BF16)
            part = jnp.dot(c, q, preferred_element_type=F32)
            total = part if total is None else total + part
        place = lax.rem(tile - mine + quarters, quarters)

        @pl.when(step == 0)
        def _():
            w_ref[place] = total

        @pl.when(step > 0)
        def _():
            w_ref[place] += total


def item_parts(mine, near, far, lines, table16, quarters):
    sources, width, features = near.shape
    items = table16.shape[0]
    return pl.pallas_call(
        item_kernel,
        grid_spec=pltpu.PrefetchScalarGridSpec(
            num_scalar_prefetch=1,
            grid=(sources,),
            in_specs=[
                pl.BlockSpec((1, width, features), lambda j, x: (j, 0, 0)),
                pl.BlockSpec((1, width, features), lambda j, x: (j, 0, 0)),
                pl.BlockSpec((1, 4, width), lambda j, x: (j, 0, 0)),
                pl.BlockSpec((items, features), lambda j, x: (0, 0)),
            ],
            out_specs=pl.BlockSpec((quarters, items // quarters, features), lambda j, x: (0, 0, 0)),
        ),
        out_shape=jax.ShapeDtypeStruct((quarters, items // quarters, features), F32),
        compiler_params=pltpu.CompilerParams(vmem_limit_bytes=24 << 20),
        cost_estimate=pl.CostEstimate(
            flops=8 * sources * width * items * features,
            bytes_accessed=4 * sources * width * features + items * features * 6,
            transcendentals=2 * sources * width * items,
        ),
        name="item_parts",
    )(mine, near, far, lines, table16)


def local(queries, clusters, positives, owner_of, table, accum):
    z_size = lax.axis_size("z")
    x_size = lax.axis_size("x")
    z = lax.axis_index("z")
    x = lax.axis_index("x")
    local_rows, features = queries.shape
    block_count, picks = clusters.shape
    block_rows = local_rows // block_count
    items = table.shape[1]
    owners = owner_of.shape[0]
    plane = owners // z_size
    pair_count = block_count * picks

    table16 = table[0].astype(BF16)
    tables = lax.all_gather(table16, PLANE)

    here = queries.reshape(block_count, block_rows, features)
    half = block_count // 2
    right = [here]
    left = [here]
    for _ in range(3):
        right.append(shift(right[-1], "z", 1))
        left.append(shift(left[-1], "z", -1))
    opposite = jnp.concatenate(
        [shift(right[3][:half], "z", 1), shift(left[3][half:], "z", -1)], axis=0
    )
    by_source = {0: here, 4: opposite}
    for hop in range(1, 4):
        by_source[z_size - hop] = right[hop]
        by_source[hop] = left[hop]

    flat_lists = clusters.reshape(pair_count)
    catalog_ids = jnp.arange(owners, dtype=jnp.int32)
    lookup = flat_lists[:, None] == catalog_ids[None, :]
    destination = jnp.sum(jnp.where(lookup, owner_of[None, :], 0), axis=1)
    pair_ids = jnp.arange(pair_count, dtype=jnp.int32)
    earlier = (destination[:, None] == destination[None, :]) & (
        pair_ids[:, None] > pair_ids[None, :]
    )
    rank_in = jnp.sum(earlier.astype(jnp.int32), axis=1)
    slot_of_pair = destination * MOST + rank_in
    slot_count = owners * MOST
    matches = slot_of_pair[None, :] == jnp.arange(slot_count, dtype=jnp.int32)[:, None]
    filled = jnp.any(matches, axis=1)
    source_pair = jnp.sum(jnp.where(matches, pair_ids[None, :], 0), axis=1)
    which_block = source_pair // picks
    which_pick = source_pair % picks
    chosen = positives.reshape(block_count, block_rows)[which_block]
    inside = filled[:, None] & (chosen // items == which_pick[:, None])
    send_targets = jnp.where(inside, chosen - which_pick[:, None] * items, -1)
    meta = jnp.concatenate([send_targets, which_block[:, None]], axis=1)
    per_plane = plane * MOST
    got_meta = lax.all_to_all(
        meta.reshape(z_size, per_plane, block_rows + 1), "z", 0, 0, tiled=True
    )
    order = jnp.array(ORDER, jnp.int32)
    arrive = (z + order) % z_size
    place_of = [ORDER.index(d) for d in range(z_size)]
    leave = jnp.array(place_of, jnp.int32)[(jnp.arange(z_size) - z) % z_size]

    def to_slots(values):
        ordered = values[arrive].reshape(2, 4, plane, MOST, -1)
        return ordered.transpose(0, 2, 1, 3, 4)

    slots = to_slots(got_meta)
    width = 4 * MOST * block_rows
    targets = slots[..., :block_rows].reshape(2, plane, 1, width)
    blk = slots[..., block_rows].reshape(2, plane * 4 * MOST)

    near_q = [by_source[d] for d in NEAR]
    far_q = [by_source[d] for d in FAR]
    near_packed, near_stat = forward(near_q, blk[0], targets[0], tables)
    near_rows = lax.all_to_all(near_packed, PLANE, 0, 0, tiled=True)
    far_packed, far_stat = forward(far_q, blk[1], targets[1], tables)
    far_rows = lax.all_to_all(far_packed, PLANE, 0, 0, tiled=True)

    stats = jnp.stack([near_stat, far_stat]).reshape(2, plane, 2, 4, MOST, block_rows)
    stats = stats.transpose(0, 3, 1, 4, 2, 5).reshape(z_size, per_plane * 2 * block_rows)
    home = lax.all_to_all(stats[leave], "z", 0, 0, tiled=True)
    pair_stats = home.reshape(slot_count, 2 * block_rows)[slot_of_pair].reshape(
        block_count, picks, 2, block_rows
    )
    part = pair_stats[:, :, 0]
    top = jnp.max(part, axis=1)
    lse = top + jnp.log(jnp.sum(jnp.exp(part - top[:, None]), axis=1))
    losses = (lse - jnp.sum(pair_stats[:, :, 1], axis=1)).reshape(local_rows)
    slot_lse = jnp.where(filled[:, None], lse[which_block], F32(EMPTY))
    got_lse = lax.all_to_all(
        slot_lse.reshape(z_size, per_plane, block_rows), "z", 0, 0, tiled=True
    )
    lse_lines = to_slots(got_lse).reshape(2, plane, 1, width)
    lines = jnp.concatenate(
        [lse_lines[0], targets[0].astype(F32), lse_lines[1], targets[1].astype(F32)], axis=1
    )
    got_lines = lax.all_to_all(lines, PLANE, 0, 0, tiled=True)

    far_g = query_parts(
        far_packed, blk[1], lse_lines[1], targets[1], tables, block_count, block_rows
    )
    near_g = query_parts(
        near_packed, blk[0], lse_lines[0], targets[0], tables, block_count, block_rows
    )
    grads = dict(zip(ORDER, list(near_g) + list(far_g)))

    def add(a, b):
        return (a.astype(F32) + b.astype(F32)).astype(BF16)

    go_right = shift(grads[4][:half], "z", 1)
    go_left = shift(grads[4][half:], "z", -1)
    go_right = jnp.concatenate([add(go_right, grads[3][:half]), grads[3][half:]], axis=0)
    go_left = jnp.concatenate([grads[5][:half], add(go_left, grads[5][half:])], axis=0)
    for hop in (2, 1):
        go_right = add(shift(go_right, "z", 1), grads[hop])
        go_left = add(shift(go_left, "z", -1), grads[z_size - hop])
    go_right = shift(go_right, "z", 1)
    go_left = shift(go_left, "z", -1)
    query_grads = (
        grads[0].astype(F32) + go_right.astype(F32) + go_left.astype(F32)
    ).reshape(local_rows, features)

    parts = item_parts(x.reshape(1), near_rows, far_rows, got_lines, table16, x_size)
    summed = parts[0]
    for hop in range(1, x_size):
        summed = summed + shift(parts[hop], "x", hop)
    all_sums = jnp.stack([summed] + [shift(summed, "x", -hop) for hop in range(1, x_size)])
    summed = all_sums[(jnp.arange(x_size) - x) % x_size].reshape(items, features)
    new_accum = accum[0] + summed * summed
    new_table = table[0] - 0.5 * summed / jnp.sqrt(new_accum)
    return (losses, query_grads, new_table[None], new_accum[None])


def solution(mesh):
    axes = ("z", "y", "c", "x")
    split = Mesh(mesh.devices.reshape(8, 4, 2, 4), axes)
    placed = (
        P(axes, None),
        P(axes, None),
        P(axes),
        P(),
        P(axes[:3], None, None),
        P(axes[:3], None, None),
    )
    return jax.shard_map(
        local,
        mesh=split,
        in_specs=placed,
        out_specs=(
            P(axes),
            P(axes, None),
            P(axes[:3], None, None),
            P(axes[:3], None, None),
        ),
        check_vma=False,
    )
```

```python
import jax
import jax.numpy as jnp
from jax import lax
from jax.experimental import pallas as pl
from jax.experimental.pallas import tpu as pltpu
from jax.sharding import Mesh, PartitionSpec as P

MOST = 2
EMPTY = 1e30
NEAR = (0, 1, 7, 2)
FAR = (6, 3, 5, 4)
ORDER = NEAR + FAR
PLANE = ("y", "c")
F32 = jnp.float32
BF16 = jnp.bfloat16
NT = (((1,), (1,)), ((), ()))
TN = (((0,), (0,)), ((), ()))
TILE = 256
VMEM = 56 << 20


def shift(value, axis, step):
    size = lax.axis_size(axis)
    return lax.ppermute(value, axis, [(i, (i + step) % size) for i in range(size)])


def tile_ids(start, shape):
    return lax.broadcasted_iota(jnp.int32, shape, 0) + start


def shift_plane(value, dy, dc):
    ys, cs = lax.axis_size("y"), lax.axis_size("c")
    moves = []
    for y in range(ys):
        for c in range(cs):
            moves.append((y * cs + c, (y + dy) % ys * cs + (c + dc) % cs))
    return lax.ppermute(value, PLANE, moves)


def forward_kernel(blk, q0, q1, q2, q3, t_ref, tgt_ref, *rest):
    p_ref, stat_ref, s_ref = rest[-3:]
    step = pl.program_id(0)
    sources = (q0, q1, q2, q3)
    block_rows = q0.shape[1]
    for slot in range(8):
        b = blk[step * 8 + slot]
        p_ref[0, pl.ds(slot * block_rows, block_rows), :] = sources[slot // MOST][b]
    q = p_ref[0]
    items = t_ref.shape[1]
    width = q.shape[0]
    tgt = tgt_ref[0]
    high = jnp.full((8, width), -jnp.inf, F32)
    pick = jnp.zeros((8, width), F32)
    for start in range(0, items, TILE):
        s = lax.dot_general(t_ref[0, pl.ds(start, TILE), :], q, NT, preferred_element_type=F32)
        s_ref[pl.ds(start, TILE), :] = s
        high = jnp.maximum(high, jnp.max(s.reshape(TILE // 8, 8, width), axis=0))
        hit = jnp.where(tile_ids(start, s.shape) == tgt, s, 0.0)
        pick = pick + jnp.sum(hit.reshape(TILE // 8, 8, width), axis=0)
    top = jnp.max(high, axis=0, keepdims=True)
    mass = jnp.zeros((8, width), F32)
    for start in range(0, items, TILE):
        e = jnp.exp(s_ref[pl.ds(start, TILE), :] - top)
        mass = mass + jnp.sum(e.reshape(TILE // 8, 8, width), axis=0)
    stat_ref[0, 0, 0:1, :] = top + jnp.log(jnp.sum(mass, axis=0, keepdims=True))
    stat_ref[0, 0, 1:2, :] = jnp.sum(pick, axis=0, keepdims=True)


def forward(sources, blk, targets, tables, half, held=None):
    planes, items, features = tables.shape
    width = targets.shape[2]
    whole = pl.BlockSpec(sources[0].shape, lambda j, blk: (0, 0, 0))
    anywhere = pl.BlockSpec(memory_space=pl.ANY)
    carried = [] if held is None else list(held)
    return pl.pallas_call(
        forward_kernel,
        grid_spec=pltpu.PrefetchScalarGridSpec(
            num_scalar_prefetch=1,
            grid=(planes,),
            in_specs=[whole] * 4
            + [
                pl.BlockSpec((1, items, features), lambda j, blk: (j, 0, 0)),
                pl.BlockSpec((1, 1, width), lambda j, blk: (j, 0, 0)),
            ]
            + [anywhere] * len(carried),
            out_specs=[
                pl.BlockSpec((1, width, features), lambda j, blk: (j, half, 0)),
                pl.BlockSpec((1, 1, 2, width), lambda j, blk: (j, half, 0, 0)),
            ],
            scratch_shapes=[pltpu.VMEM((items, width), F32)],
        ),
        out_shape=[
            jax.ShapeDtypeStruct((planes, 2 * width, features), BF16),
            jax.ShapeDtypeStruct((planes, 2, 2, width), F32),
        ],
        input_output_aliases={7: 0, 8: 1} if carried else {},
        compiler_params=pltpu.CompilerParams(vmem_limit_bytes=VMEM),
        cost_estimate=pl.CostEstimate(
            flops=2 * planes * width * items * features,
            bytes_accessed=planes * items * features * 2 + 3 * planes * width * features * 2,
            transcendentals=planes * width * items,
        ),
        name="forward",
    )(blk, *sources, tables, targets, *carried)


def query_kernel(blk, p_ref, t_ref, lse_ref, tgt_ref, g0, g1, g2, g3, c_ref, acc_ref):
    step = pl.program_id(0)

    @pl.when(step == 0)
    def _():
        acc_ref[...] = jnp.zeros_like(acc_ref)

    q = p_ref[0]
    lse = lse_ref[0]
    tgt = tgt_ref[0]
    items = t_ref.shape[1]
    for start in range(0, items, TILE):
        s = lax.dot_general(t_ref[0, pl.ds(start, TILE), :], q, NT, preferred_element_type=F32)
        e = jnp.exp(s - lse)
        c = jnp.where(tile_ids(start, s.shape) == tgt, e - 1.0, e)
        c_ref[pl.ds(start, TILE), :] = c.astype(BF16)
    g = lax.dot_general(c_ref[...], t_ref[0], TN, preferred_element_type=F32)
    block_rows = g0.shape[1]
    for slot in range(8):
        b = blk[step * 8 + slot]
        acc_ref[slot // MOST, b] += g[slot * block_rows:(slot + 1) * block_rows, :]

    @pl.when(step == pl.num_programs(0) - 1)
    def _():
        for i, out in enumerate((g0, g1, g2, g3)):
            out[...] = acc_ref[i].astype(BF16)


def query_parts(packed, blk, lse, targets, tables, half, blocks, block_rows):
    planes, items, features = tables.shape
    width = targets.shape[2]
    line = pl.BlockSpec((1, 1, width), lambda j, blk: (j, 0, 0))
    out = jax.ShapeDtypeStruct((blocks, block_rows, features), BF16)
    return pl.pallas_call(
        query_kernel,
        grid_spec=pltpu.PrefetchScalarGridSpec(
            num_scalar_prefetch=1,
            grid=(planes,),
            in_specs=[
                pl.BlockSpec((1, width, features), lambda j, blk: (j, half, 0)),
                pl.BlockSpec((1, items, features), lambda j, blk: (j, 0, 0)),
                line,
                line,
            ],
            out_specs=[pl.BlockSpec(out.shape, lambda j, blk: (0, 0, 0))] * 4,
            scratch_shapes=[
                pltpu.VMEM((items, width), BF16),
                pltpu.VMEM((4, blocks, block_rows, features), F32),
            ],
        ),
        out_shape=[out] * 4,
        compiler_params=pltpu.CompilerParams(vmem_limit_bytes=VMEM),
        cost_estimate=pl.CostEstimate(
            flops=4 * planes * width * items * features,
            bytes_accessed=planes * items * features * 2 + 2 * planes * width * features * 2,
            transcendentals=planes * width * items,
        ),
        name="query_parts",
    )(blk, packed, tables, lse, targets)


def item_kernel(order_ref, q_ref, line_ref, t_ref, w_ref):
    step = pl.program_id(0)

    @pl.when(step == 0)
    def _():
        w_ref[...] = jnp.zeros_like(w_ref)

    quarters = w_ref.shape[0]
    rows = w_ref.shape[1]
    mine = order_ref[0]
    q = q_ref[0]
    lse = line_ref[0, 0:1, :]
    tgt = line_ref[0, 1:2, :].astype(jnp.int32)
    for place in range(quarters):
        start = pl.multiple_of(lax.rem(place + mine, quarters) * rows, rows)
        s = lax.dot_general(t_ref[pl.ds(start, rows), :], q, NT, preferred_element_type=F32)
        e = jnp.exp(s - lse)
        c = jnp.where(tile_ids(start, s.shape) == tgt, e - 1.0, e).astype(BF16)
        w_ref[place] += jnp.dot(c, q, preferred_element_type=F32)


def item_parts(order, rows, lines, table16, quarters):
    sources, width, features = rows.shape
    items = table16.shape[0]
    return pl.pallas_call(
        item_kernel,
        grid_spec=pltpu.PrefetchScalarGridSpec(
            num_scalar_prefetch=1,
            grid=(sources,),
            in_specs=[
                pl.BlockSpec((1, width, features), lambda j, o: (j, 0, 0)),
                pl.BlockSpec((1, 2, width), lambda j, o: (o[j + 1], 0, 0)),
                pl.BlockSpec((items, features), lambda j, o: (0, 0)),
            ],
            out_specs=pl.BlockSpec((quarters, items // quarters, features), lambda j, o: (0, 0, 0)),
        ),
        out_shape=jax.ShapeDtypeStruct((quarters, items // quarters, features), F32),
        compiler_params=pltpu.CompilerParams(vmem_limit_bytes=VMEM),
        cost_estimate=pl.CostEstimate(
            flops=4 * sources * width * items * features,
            bytes_accessed=2 * sources * width * features + items * features * 6,
            transcendentals=sources * width * items,
        ),
        name="item_parts",
    )(order, rows, lines, table16)


def local(queries, clusters, positives, owner_of, table, accum):
    z_size = lax.axis_size("z")
    y_size = lax.axis_size("y")
    c_size = lax.axis_size("c")
    x_size = lax.axis_size("x")
    z = lax.axis_index("z")
    y = lax.axis_index("y")
    c = lax.axis_index("c")
    x = lax.axis_index("x")
    local_rows, features = queries.shape
    block_count, picks = clusters.shape
    block_rows = local_rows // block_count
    items = table.shape[1]
    owners = owner_of.shape[0]
    plane = owners // z_size
    pair_count = block_count * picks

    table16 = table[0].astype(BF16)
    tables = lax.all_gather(table16, PLANE)

    here = queries.reshape(block_count, block_rows, features)
    by_source = {0: here}
    right = left = here
    for hop in range(1, z_size // 2 + 1):
        right = shift(right, "z", 1)
        by_source[z_size - hop] = right
        if hop < z_size // 2:
            left = shift(left, "z", -1)
            by_source[hop] = left

    flat_lists = clusters.reshape(pair_count)
    catalog_ids = jnp.arange(owners, dtype=jnp.int32)
    lookup = flat_lists[:, None] == catalog_ids[None, :]
    destination = jnp.sum(jnp.where(lookup, owner_of[None, :], 0), axis=1)
    pair_ids = jnp.arange(pair_count, dtype=jnp.int32)
    earlier = (destination[:, None] == destination[None, :]) & (
        pair_ids[:, None] > pair_ids[None, :]
    )
    rank_in = jnp.sum(earlier.astype(jnp.int32), axis=1)
    slot_of_pair = destination * MOST + rank_in
    slot_count = owners * MOST
    matches = slot_of_pair[None, :] == jnp.arange(slot_count, dtype=jnp.int32)[:, None]
    filled = jnp.any(matches, axis=1)
    source_pair = jnp.sum(jnp.where(matches, pair_ids[None, :], 0), axis=1)
    which_block = source_pair // picks
    which_pick = source_pair % picks
    chosen = positives.reshape(block_count, block_rows)[which_block]
    inside = filled[:, None] & (chosen // items == which_pick[:, None])
    send_targets = jnp.where(inside, chosen - which_pick[:, None] * items, -1)
    block_or_none = jnp.where(filled, which_block, -1)
    per_plane = plane * MOST
    meta = jnp.concatenate(
        [
            send_targets.reshape(z_size, per_plane * block_rows),
            block_or_none.reshape(z_size, per_plane),
            jnp.broadcast_to(slot_of_pair[None, :], (z_size, pair_count)),
        ],
        axis=1,
    )
    got = lax.all_to_all(meta, "z", 0, 0, tiled=True)
    order = jnp.array(ORDER, jnp.int32)
    got = got[(z + order) % z_size]
    width = 4 * MOST * block_rows
    cut = per_plane * block_rows
    targets = got[:, :cut].reshape(2, 4, plane, MOST, block_rows)
    targets = targets.transpose(0, 2, 1, 3, 4).reshape(2, plane, 1, width)
    named = got[:, cut:cut + per_plane].reshape(2, 4, plane, MOST).transpose(0, 2, 1, 3)
    named = named.reshape(2, plane * 4 * MOST)
    blk = jnp.maximum(named, 0)

    pair_slot = got[:, cut + per_plane:]
    pair_owner = pair_slot // MOST
    pair_from = (pair_owner // plane - z) % z_size
    pair_rel = (order[:, None] - pair_from) % z_size
    pair_place = jnp.zeros_like(pair_rel)
    for place, d in enumerate(ORDER):
        pair_place = jnp.where(pair_rel == d, place, pair_place)
    pair_row = (pair_from * plane + pair_owner % plane) * 2 + pair_place // 4
    pair_row = pair_row * 2 * 4 * MOST + pair_place % 4 * MOST + pair_slot % MOST

    near_q = [by_source[d] for d in NEAR]
    far_q = [by_source[d] for d in FAR]
    held = forward(near_q, blk[0], targets[0], tables, 0)
    packed, stats = forward(far_q, blk[1], targets[1], tables, 1, held)
    rows = lax.all_to_all(packed, PLANE, 0, 0, tiled=True)

    all_stats = jnp.stack([stats] + [shift(stats, "z", -e) for e in range(1, z_size)])
    all_stats = all_stats.reshape(-1, block_rows)
    part = all_stats[pair_row.reshape(-1)].reshape(z_size, block_count, picks, block_rows)
    pick = all_stats[pair_row[0] + 4 * MOST].reshape(block_count, picks, block_rows)
    top = jnp.max(part, axis=2)
    lse = top + jnp.log(jnp.sum(jnp.exp(part - top[:, :, None]), axis=2))
    losses = (lse[0] - jnp.sum(pick, axis=1)).reshape(local_rows)
    lse_rows = lse.reshape(z_size * block_count, block_rows)
    first = jnp.arange(z_size, dtype=jnp.int32).reshape(2, 1, 4, 1) * block_count
    lse_at = (blk.reshape(2, plane, 4, MOST) + first).reshape(-1)
    lse_slots = jnp.where(named.reshape(-1, 1) < 0, F32(EMPTY), lse_rows[lse_at])
    lse_lines = lse_slots.reshape(2, plane, 1, width)

    lines = jnp.stack(
        [
            lse_lines.transpose(1, 2, 0, 3).reshape(plane, 2 * width),
            targets.transpose(1, 2, 0, 3).reshape(plane, 2 * width).astype(F32),
        ],
        axis=1,
    )
    line_parts = []
    ranks = []
    for dy in range(y_size):
        for dc in range(c_size):
            index = (y + dy) % y_size * c_size + (c + dc) % c_size
            mine = lax.dynamic_index_in_dim(lines, index, 0, keepdims=False)
            line_parts.append(shift_plane(mine, dy, dc) if dy or dc else mine)
    sources = jnp.arange(plane, dtype=jnp.int32)
    ranks = (y - sources // c_size) % y_size * c_size + (c - sources % c_size) % c_size
    got_lines = jnp.stack(line_parts)

    far_g = query_parts(
        packed, blk[1], lse_lines[1], targets[1], tables, 1, block_count, block_rows
    )
    near_g = query_parts(
        packed, blk[0], lse_lines[0], targets[0], tables, 0, block_count, block_rows
    )
    grads = dict(zip(ORDER, list(near_g) + list(far_g)))

    def add(a, b):
        return (a.astype(F32) + b.astype(F32)).astype(BF16)

    go_right = shift(grads[4], "z", 1)
    go_right = shift(add(go_right, grads[3]), "z", 1)
    go_left = shift(grads[5], "z", -1)
    go_right = shift(add(go_right, grads[2]), "z", 1)
    go_left = shift(add(go_left, grads[6]), "z", -1)
    go_right = shift(add(go_right, grads[1]), "z", 1)
    go_left = shift(add(go_left, grads[7]), "z", -1)
    query_grads = (
        grads[0].astype(F32) + go_right.astype(F32) + go_left.astype(F32)
    ).reshape(local_rows, features)

    item_order = jnp.concatenate([x.reshape(1), ranks])
    parts = item_parts(item_order, rows, got_lines, table16, x_size)
    summed = parts[0]
    for hop in range(1, x_size):
        summed = summed + shift(parts[hop], "x", hop)
    all_sums = jnp.stack([summed] + [shift(summed, "x", -hop) for hop in range(1, x_size)])
    summed = all_sums[(jnp.arange(x_size) - x) % x_size].reshape(items, features)
    new_accum = accum[0] + summed * summed
    new_table = table[0] - 0.5 * summed / jnp.sqrt(new_accum)
    return (losses, query_grads, new_table[None], new_accum[None])


def solution(mesh):
    axes = ("z", "y", "c", "x")
    split = Mesh(mesh.devices.reshape(8, 4, 2, 4), axes)
    placed = (
        P(axes, None),
        P(axes, None),
        P(axes),
        P(),
        P(axes[:3], None, None),
        P(axes[:3], None, None),
    )
    return jax.shard_map(
        local,
        mesh=split,
        in_specs=placed,
        out_specs=(
            P(axes),
            P(axes, None),
            P(axes[:3], None, None),
            P(axes[:3], None, None),
        ),
        check_vma=False,
    )
```

```python
import functools

import jax
import jax.numpy as jnp
from jax import lax
from jax.experimental import pallas as pl
from jax.experimental.pallas import tpu as pltpu
from jax.sharding import Mesh, PartitionSpec as P

MOST = 2
EMPTY = 1e30
NEAR = (0, 1, 7, 6)
FAR = (2, 3, 4, 5)
ORDER = NEAR + FAR
PLANE = ("y", "c")
F32 = jnp.float32
BF16 = jnp.bfloat16
NT = (((1,), (1,)), ((), ()))
TN = (((0,), (0,)), ((), ()))
TILE = 256
VMEM = 24 << 20


def shift(value, axis, step):
    size = lax.axis_size(axis)
    return lax.ppermute(value, axis, [(i, (i + step) % size) for i in range(size)])


def tile_ids(start, shape):
    return lax.broadcasted_iota(jnp.int32, shape, 0) + start


def pack_kernel(blk, *refs):
    sources, p_ref = refs[:-1], refs[-1]
    step = pl.program_id(0)
    block_rows = sources[0].shape[1]
    per_step = len(sources) * MOST
    for slot in range(per_step):
        b = blk[step * per_step + slot]
        p_ref[0, pl.ds(slot * block_rows, block_rows), :] = sources[slot // MOST][b]


def pack(sources, blk, plane):
    shape = sources[0].shape
    width = len(sources) * MOST * shape[1]
    return pl.pallas_call(
        pack_kernel,
        grid_spec=pltpu.PrefetchScalarGridSpec(
            num_scalar_prefetch=1,
            grid=(plane,),
            in_specs=[pl.BlockSpec(shape, lambda j, blk: (0, 0, 0))] * len(sources),
            out_specs=pl.BlockSpec((1, width, shape[2]), lambda j, blk: (j, 0, 0)),
        ),
        out_shape=jax.ShapeDtypeStruct((plane, width, shape[2]), BF16),
        compiler_params=pltpu.CompilerParams(vmem_limit_bytes=VMEM),
        cost_estimate=pl.CostEstimate(
            flops=0, bytes_accessed=4 * plane * width * shape[2], transcendentals=0
        ),
        name="pack",
    )(blk, *sources)


def forward_kernel(p_ref, t_ref, tgt_ref, stat_ref, s_ref):
    q = p_ref[0]
    items = t_ref.shape[1]
    width = q.shape[0]
    tgt = tgt_ref[0]
    high = jnp.full((8, width), -jnp.inf, F32)
    pick = jnp.zeros((8, width), F32)
    for start in range(0, items, TILE):
        s = lax.dot_general(t_ref[0, pl.ds(start, TILE), :], q, NT, preferred_element_type=F32)
        s_ref[pl.ds(start, TILE), :] = s
        high = jnp.maximum(high, jnp.max(s.reshape(TILE // 8, 8, width), axis=0))
        hit = jnp.where(tile_ids(start, s.shape) == tgt, s, 0.0)
        pick = pick + jnp.sum(hit.reshape(TILE // 8, 8, width), axis=0)
    top = jnp.max(high, axis=0, keepdims=True)
    mass = jnp.zeros((8, width), F32)
    for start in range(0, items, TILE):
        e = jnp.exp(s_ref[pl.ds(start, TILE), :] - top)
        mass = mass + jnp.sum(e.reshape(TILE // 8, 8, width), axis=0)
    stat_ref[0, 0:1, :] = top + jnp.log(jnp.sum(mass, axis=0, keepdims=True))
    stat_ref[0, 1:2, :] = jnp.sum(pick, axis=0, keepdims=True)


def forward(packed, targets, tables):
    planes, items, features = tables.shape
    width = packed.shape[1]
    return pl.pallas_call(
        forward_kernel,
        grid=(planes,),
        in_specs=[
            pl.BlockSpec((1, width, features), lambda j: (j, 0, 0)),
            pl.BlockSpec((1, items, features), lambda j: (j, 0, 0)),
            pl.BlockSpec((1, 1, width), lambda j: (j, 0, 0)),
        ],
        out_specs=pl.BlockSpec((1, 2, width), lambda j: (j, 0, 0)),
        out_shape=jax.ShapeDtypeStruct((planes, 2, width), F32),
        scratch_shapes=[pltpu.VMEM((items, width), F32)],
        compiler_params=pltpu.CompilerParams(vmem_limit_bytes=VMEM),
        cost_estimate=pl.CostEstimate(
            flops=2 * planes * width * items * features,
            bytes_accessed=planes * items * features * 2 + planes * width * features * 2,
            transcendentals=planes * width * items,
        ),
        name="forward",
    )(packed, tables, targets)


def query_kernel(half, blk, p_ref, t_ref, line_ref, g0, g1, g2, g3, c_ref, acc_ref):
    step = pl.program_id(0)

    @pl.when(step == 0)
    def _():
        acc_ref[...] = jnp.zeros_like(acc_ref)

    q = p_ref[0]
    lse = line_ref[0, 0:1, :]
    tgt = line_ref[0, 1:2, :].astype(jnp.int32)
    items = t_ref.shape[1]
    for start in range(0, items, TILE):
        s = lax.dot_general(t_ref[0, pl.ds(start, TILE), :], q, NT, preferred_element_type=F32)
        e = jnp.exp(s - lse)
        c = jnp.where(tile_ids(start, s.shape) == tgt, e - 1.0, e)
        c_ref[pl.ds(start, TILE), :] = c.astype(BF16)
    g = lax.dot_general(c_ref[...], t_ref[0], TN, preferred_element_type=F32)
    block_rows = g0.shape[1]
    for slot in range(8):
        b = blk[step * 16 + half * 8 + slot]
        acc_ref[slot // MOST, b] += g[slot * block_rows:(slot + 1) * block_rows, :]

    @pl.when(step == pl.num_programs(0) - 1)
    def _():
        for i, out in enumerate((g0, g1, g2, g3)):
            out[...] = acc_ref[i].astype(BF16)


def query_parts(packed, blk, lines, tables, half, blocks, block_rows):
    planes, items, features = tables.shape
    width = packed.shape[1] // 2
    out = jax.ShapeDtypeStruct((blocks, block_rows, features), BF16)
    return pl.pallas_call(
        functools.partial(query_kernel, half),
        grid_spec=pltpu.PrefetchScalarGridSpec(
            num_scalar_prefetch=1,
            grid=(planes,),
            in_specs=[
                pl.BlockSpec((1, width, features), lambda j, blk: (j, half, 0)),
                pl.BlockSpec((1, items, features), lambda j, blk: (j, 0, 0)),
                pl.BlockSpec((1, 2, width), lambda j, blk: (j, 0, half)),
            ],
            out_specs=[pl.BlockSpec(out.shape, lambda j, blk: (0, 0, 0))] * 4,
            scratch_shapes=[
                pltpu.VMEM((items, width), BF16),
                pltpu.VMEM((4, blocks, block_rows, features), F32),
            ],
        ),
        out_shape=[out] * 4,
        compiler_params=pltpu.CompilerParams(vmem_limit_bytes=VMEM),
        cost_estimate=pl.CostEstimate(
            flops=4 * planes * width * items * features,
            bytes_accessed=planes * items * features * 2 + 2 * planes * width * features * 2,
            transcendentals=planes * width * items,
        ),
        name="query_parts",
    )(blk, packed, tables, lines)


def item_kernel(places, quarters, x_ref, q_ref, line_ref, t_ref, *outs):
    step = pl.program_id(0)

    @pl.when(step == 0)
    def _():
        for out in outs:
            out[...] = jnp.zeros_like(out)

    rows = t_ref.shape[0] // quarters
    mine = x_ref[0]
    q = q_ref[0]
    lse = line_ref[0, 0:1, :]
    tgt = line_ref[0, 1:2, :].astype(jnp.int32)
    per_out = len(outs) // len(places)
    for i, place in enumerate(places):
        start = pl.multiple_of(lax.rem(place + mine, quarters) * rows, rows)
        s = lax.dot_general(t_ref[pl.ds(start, rows), :], q, NT, preferred_element_type=F32)
        e = jnp.exp(s - lse)
        c = jnp.where(tile_ids(start, s.shape) == tgt, e - 1.0, e).astype(BF16)
        part = jnp.dot(c, q, preferred_element_type=F32)
        cut = rows // per_out
        for n in range(per_out):
            outs[i * per_out + n][...] += part[n * cut:(n + 1) * cut]


def item_parts(places, pieces, x, rows, lines, table16, quarters):
    sources, width, features = rows.shape
    items = table16.shape[0]
    out = jax.ShapeDtypeStruct((items // quarters // pieces, features), F32)
    share = len(places)
    return pl.pallas_call(
        functools.partial(item_kernel, places, quarters),
        grid_spec=pltpu.PrefetchScalarGridSpec(
            num_scalar_prefetch=1,
            grid=(sources,),
            in_specs=[
                pl.BlockSpec((1, width, features), lambda j, o: (j, 0, 0)),
                pl.BlockSpec((1, 2, width), lambda j, o: (j, 0, 0)),
                pl.BlockSpec((items, features), lambda j, o: (0, 0)),
            ],
            out_specs=[pl.BlockSpec(out.shape, lambda j, o: (0, 0))] * (share * pieces),
        ),
        out_shape=[out] * (share * pieces),
        compiler_params=pltpu.CompilerParams(vmem_limit_bytes=VMEM),
        cost_estimate=pl.CostEstimate(
            flops=share * sources * width * items * features,
            bytes_accessed=2 * sources * width * features + items * features * 3,
            transcendentals=share * sources * width * items // 4,
        ),
        name="item_parts",
    )(x, rows, lines, table16)


def update_kernel(x_ref, own, after, before, far_a, far_b, t_ref, a_ref, nt_ref, na_ref):
    quarters = pl.num_programs(0)
    rel = lax.rem(pl.program_id(0) - x_ref[0] + quarters, quarters)
    cut = far_a.shape[0]

    def write(start, summed):
        span = pl.ds(start, summed.shape[0])
        accum = a_ref[span, :] + summed * summed
        na_ref[span, :] = accum
        nt_ref[span, :] = t_ref[span, :] - 0.5 * summed / jnp.sqrt(accum)

    for place, ref in ((0, own), (1, after), (3, before)):

        @pl.when(rel == place)
        def _():
            write(0, ref[...])

    @pl.when(rel == 2)
    def _():
        write(0, far_a[...])
        write(cut, far_b[...])


def update(x, own, after, before, far_a, far_b, table, accum, quarters):
    items, features = table.shape
    whole = pl.BlockSpec(own.shape, lambda i, x: (0, 0))
    part = pl.BlockSpec(far_a.shape, lambda i, x: (0, 0))
    block = pl.BlockSpec((items // quarters, features), lambda i, x: (i, 0))
    return pl.pallas_call(
        update_kernel,
        grid_spec=pltpu.PrefetchScalarGridSpec(
            num_scalar_prefetch=1,
            grid=(quarters,),
            in_specs=[whole] * 3 + [part] * 2 + [block] * 2,
            out_specs=[block] * 2,
        ),
        out_shape=[jax.ShapeDtypeStruct(table.shape, F32)] * 2,
        compiler_params=pltpu.CompilerParams(vmem_limit_bytes=VMEM),
        name="update",
    )(x, own, after, before, far_a, far_b, table, accum)


def local(queries, clusters, positives, owner_of, table, accum):
    z_size = lax.axis_size("z")
    x_size = lax.axis_size("x")
    z = lax.axis_index("z")
    x = lax.axis_index("x").reshape(1)
    local_rows, features = queries.shape
    block_count, picks = clusters.shape
    block_rows = local_rows // block_count
    items = table.shape[1]
    owners = owner_of.shape[0]
    plane = owners // z_size
    pair_count = block_count * picks

    table16 = table[0].astype(BF16)
    tables = lax.all_gather(table16, PLANE)

    here = queries.reshape(block_count, block_rows, features)
    by_source = {0: here, 7: shift(here, "z", 1), 1: shift(here, "z", -1)}
    clusters, positives, by_source[7], by_source[1] = lax.optimization_barrier(
        (clusters, positives, by_source[7], by_source[1])
    )
    by_source[6] = shift(by_source[7], "z", 1)
    by_source[2] = shift(by_source[1], "z", -1)
    by_source[5] = shift(by_source[6], "z", 1)
    by_source[3] = shift(by_source[2], "z", -1)

    flat_lists = clusters.reshape(pair_count)
    catalog_ids = jnp.arange(owners, dtype=jnp.int32)
    lookup = flat_lists[:, None] == catalog_ids[None, :]
    destination = jnp.sum(jnp.where(lookup, owner_of[None, :], 0), axis=1)
    pair_ids = jnp.arange(pair_count, dtype=jnp.int32)
    earlier = (destination[:, None] == destination[None, :]) & (
        pair_ids[:, None] > pair_ids[None, :]
    )
    rank_in = jnp.sum(earlier.astype(jnp.int32), axis=1)
    slot_of_pair = destination * MOST + rank_in
    slot_count = owners * MOST
    matches = slot_of_pair[None, :] == jnp.arange(slot_count, dtype=jnp.int32)[:, None]
    filled = jnp.any(matches, axis=1)
    source_pair = jnp.sum(jnp.where(matches, pair_ids[None, :], 0), axis=1)
    which_block = source_pair // picks
    which_pick = source_pair % picks
    chosen = positives.reshape(block_count, block_rows)[which_block]
    inside = filled[:, None] & (chosen // items == which_pick[:, None])
    send_targets = jnp.where(inside, chosen - which_pick[:, None] * items, -1)
    block_or_none = jnp.where(filled, which_block, -1)
    per_plane = plane * MOST
    meta = jnp.concatenate(
        [
            send_targets.reshape(z_size, per_plane * block_rows),
            block_or_none.reshape(z_size, per_plane),
            jnp.broadcast_to(slot_of_pair[None, :], (z_size, pair_count)),
        ],
        axis=1,
    )
    got = lax.all_to_all(meta, "z", 0, 0, tiled=True)
    got, last = lax.optimization_barrier((got, by_source[5]))
    by_source[4] = shift(last, "z", 1)
    order = jnp.array(ORDER, jnp.int32)
    got = got[(z + order) % z_size]
    width = z_size * MOST * block_rows
    cut = per_plane * block_rows
    targets = got[:, :cut].reshape(z_size, plane, MOST, block_rows)
    targets = targets.transpose(1, 0, 2, 3).reshape(plane, 1, width)
    named = got[:, cut:cut + per_plane].reshape(z_size, plane, MOST).transpose(1, 0, 2)
    named = named.reshape(plane * per_plane)
    blk = jnp.maximum(named, 0)

    pair_slot = got[:, cut + per_plane:]
    pair_owner = pair_slot // MOST
    pair_from = (pair_owner // plane - z) % z_size
    pair_rel = (order[:, None] - pair_from) % z_size
    pair_place = jnp.zeros_like(pair_rel)
    for place, d in enumerate(ORDER):
        pair_place = jnp.where(pair_rel == d, place, pair_place)
    pair_row = (pair_from % 2 * 4 + pair_from // 2) * plane + pair_owner % plane
    pair_row = (pair_row * 2 * z_size + pair_place) * MOST + pair_slot % MOST

    packed = pack([by_source[d] for d in ORDER], blk, plane)
    rows = lax.all_to_all(packed, PLANE, 0, 0, tiled=True)
    stats = forward(packed, targets, tables)

    even = jnp.stack([stats] + [shift(stats, "z", -e) for e in (2, 4, 6)])
    all_stats = jnp.stack([even, shift(even, "z", -1)]).reshape(-1, block_rows)
    part = all_stats[pair_row.reshape(-1)].reshape(z_size, block_count, picks, block_rows)
    pick = all_stats[pair_row[0] + z_size * MOST].reshape(block_count, picks, block_rows)
    top = jnp.max(part, axis=2)
    lse = top + jnp.log(jnp.sum(jnp.exp(part - top[:, :, None]), axis=2))
    losses = (lse[0] - jnp.sum(pick, axis=1)).reshape(local_rows)
    lse_rows = lse.reshape(z_size * block_count, block_rows)
    first = jnp.arange(z_size, dtype=jnp.int32).reshape(1, z_size, 1) * block_count
    lse_at = (blk.reshape(plane, z_size, MOST) + first).reshape(-1)
    lse_slots = jnp.where(named[:, None] < 0, F32(EMPTY), lse_rows[lse_at])
    lines = jnp.concatenate(
        [lse_slots.reshape(plane, 1, width), targets.astype(F32)], axis=1
    )
    got_lines = lax.all_to_all(lines, PLANE, 0, 0, tiled=True)

    far_g = query_parts(packed, blk, lines, tables, 1, block_count, block_rows)
    near_g = query_parts(packed, blk, lines, tables, 0, block_count, block_rows)
    grads = dict(zip(ORDER, list(near_g) + list(far_g)))

    def add(a, b):
        return (a.astype(F32) + b.astype(F32)).astype(BF16)

    go_right = shift(grads[4], "z", 1)
    go_right = shift(add(go_right, grads[3]), "z", 1)
    go_right = shift(add(go_right, grads[2]), "z", 1)
    go_right = shift(add(go_right, grads[1]), "z", 1)
    go_left = shift(grads[5], "z", -1)
    go_left = shift(add(go_left, grads[6]), "z", -1)
    go_left = shift(add(go_left, grads[7]), "z", -1)
    query_grads = (
        grads[0].astype(F32) + go_right.astype(F32) + go_left.astype(F32)
    ).reshape(local_rows, features)

    far_a, far_b = item_parts((2,), 2, x, rows, got_lines, table16, x_size)
    own, after, before = item_parts((0, 1, 3), 1, x, rows, got_lines, table16, x_size)
    half = far_a.shape[0]
    far_a = shift(far_a, "x", 1)
    far_b = shift(far_b, "x", -1)
    after = shift(jnp.concatenate([after[:half] + far_a, after[half:]]), "x", 1)
    before = shift(jnp.concatenate([before[:half], before[half:] + far_b]), "x", -1)
    own = own + after + before
    before = shift(own, "x", 1)
    after = shift(own, "x", -1)
    far_a = shift(before[:half], "x", 1)
    far_b = shift(after[half:], "x", -1)
    new_table, new_accum = update(
        x, own, after, before, far_a, far_b, table[0], accum[0], x_size
    )
    return (losses, query_grads, new_table[None], new_accum[None])


def solution(mesh):
    axes = ("z", "y", "c", "x")
    split = Mesh(mesh.devices.reshape(8, 4, 2, 4), axes)
    placed = (
        P(axes, None),
        P(axes, None),
        P(axes),
        P(),
        P(axes[:3], None, None),
        P(axes[:3], None, None),
    )
    return jax.shard_map(
        local,
        mesh=split,
        in_specs=placed,
        out_specs=(
            P(axes),
            P(axes, None),
            P(axes[:3], None, None),
            P(axes[:3], None, None),
        ),
        check_vma=False,
    )
```

```python
import functools

import jax
import jax.numpy as jnp
from jax import lax
from jax.experimental import pallas as pl
from jax.experimental.pallas import tpu as pltpu
from jax.sharding import Mesh, PartitionSpec as P

MOST = 2
EMPTY = 1e30
NEAR = (0, 1, 7, 6)
FAR = (2, 3, 4, 5)
ORDER = NEAR + FAR
PLANE = ("y", "c")
F32 = jnp.float32
BF16 = jnp.bfloat16
NT = (((1,), (1,)), ((), ()))
TN = (((0,), (0,)), ((), ()))
TILE = 256
VMEM = 24 << 20


def shift(value, axis, step):
    size = lax.axis_size(axis)
    return lax.ppermute(value, axis, [(i, (i + step) % size) for i in range(size)])


def tile_ids(start, shape):
    return lax.broadcasted_iota(jnp.int32, shape, 0) + start


def shift_plane(value, dy, dc):
    ys, cs = lax.axis_size("y"), lax.axis_size("c")
    moves = []
    for y in range(ys):
        for c in range(cs):
            moves.append((y * cs + c, (y + dy) % ys * cs + (c + dc) % cs))
    return lax.ppermute(value, PLANE, moves)


def pack_kernel(count, blk, *refs):
    sources, p_ref, outs = refs[:count], refs[count], refs[count + 1:]
    block_rows = sources[0].shape[1]
    per_peer = count * MOST
    for peer, out in enumerate(outs):
        j = blk[len(outs) * per_peer + peer]
        for slot in range(per_peer):
            rows = sources[slot // MOST][blk[j * per_peer + slot]]
            span = pl.ds(slot * block_rows, block_rows)
            out[span, :] = rows
            p_ref[j, span, :] = rows


def pack(sources, blk, peers):
    shape = sources[0].shape
    plane = peers.shape[0]
    width = len(sources) * MOST * shape[1]
    out = jax.ShapeDtypeStruct((width, shape[2]), BF16)
    return pl.pallas_call(
        functools.partial(pack_kernel, len(sources)),
        grid_spec=pltpu.PrefetchScalarGridSpec(
            num_scalar_prefetch=1,
            grid=(1,),
            in_specs=[pl.BlockSpec(shape, lambda j, blk: (0, 0, 0))] * len(sources),
            out_specs=[pl.BlockSpec((plane, width, shape[2]), lambda j, blk: (0, 0, 0))]
            + [pl.BlockSpec(out.shape, lambda j, blk: (0, 0))] * plane,
        ),
        out_shape=[jax.ShapeDtypeStruct((plane, width, shape[2]), BF16)] + [out] * plane,
        compiler_params=pltpu.CompilerParams(vmem_limit_bytes=VMEM),
        cost_estimate=pl.CostEstimate(
            flops=0, bytes_accessed=6 * plane * width * shape[2], transcendentals=0
        ),
        name="pack",
    )(jnp.concatenate([blk, peers]), *sources)


def forward_kernel(p_ref, t_ref, tgt_ref, stat_ref, s_ref):
    q = p_ref[0]
    items = t_ref.shape[1]
    width = q.shape[0]
    tgt = tgt_ref[0]
    high = jnp.full((8, width), -jnp.inf, F32)
    pick = jnp.zeros((8, width), F32)
    for start in range(0, items, TILE):
        s = lax.dot_general(t_ref[0, pl.ds(start, TILE), :], q, NT, preferred_element_type=F32)
        s_ref[pl.ds(start, TILE), :] = s
        high = jnp.maximum(high, jnp.max(s.reshape(TILE // 8, 8, width), axis=0))
        hit = jnp.where(tile_ids(start, s.shape) == tgt, s, 0.0)
        pick = pick + jnp.sum(hit.reshape(TILE // 8, 8, width), axis=0)
    top = jnp.max(high, axis=0, keepdims=True)
    mass = jnp.zeros((8, width), F32)
    for start in range(0, items, TILE):
        e = jnp.exp(s_ref[pl.ds(start, TILE), :] - top)
        mass = mass + jnp.sum(e.reshape(TILE // 8, 8, width), axis=0)
    stat_ref[0, 0:1, :] = top + jnp.log(jnp.sum(mass, axis=0, keepdims=True))
    stat_ref[0, 1:2, :] = jnp.sum(pick, axis=0, keepdims=True)


def forward(packed, targets, tables):
    planes, items, features = tables.shape
    width = packed.shape[1]
    return pl.pallas_call(
        forward_kernel,
        grid=(planes,),
        in_specs=[
            pl.BlockSpec((1, width, features), lambda j: (j, 0, 0)),
            pl.BlockSpec((1, items, features), lambda j: (j, 0, 0)),
            pl.BlockSpec((1, 1, width), lambda j: (j, 0, 0)),
        ],
        out_specs=pl.BlockSpec((1, 2, width), lambda j: (j, 0, 0)),
        out_shape=jax.ShapeDtypeStruct((planes, 2, width), F32),
        scratch_shapes=[pltpu.VMEM((items, width), F32)],
        compiler_params=pltpu.CompilerParams(vmem_limit_bytes=VMEM),
        cost_estimate=pl.CostEstimate(
            flops=2 * planes * width * items * features,
            bytes_accessed=planes * items * features * 2 + planes * width * features * 2,
            transcendentals=planes * width * items,
        ),
        name="forward",
    )(packed, tables, targets)


def query_kernel(half, blk, p_ref, t_ref, line_ref, g0, g1, g2, g3, c_ref, acc_ref):
    step = pl.program_id(0)

    @pl.when(step == 0)
    def _():
        acc_ref[...] = jnp.zeros_like(acc_ref)

    q = p_ref[0]
    lse = line_ref[0, 0:1, :]
    tgt = line_ref[0, 1:2, :].astype(jnp.int32)
    items = t_ref.shape[1]
    for start in range(0, items, TILE):
        s = lax.dot_general(t_ref[0, pl.ds(start, TILE), :], q, NT, preferred_element_type=F32)
        e = jnp.exp(s - lse)
        c = jnp.where(tile_ids(start, s.shape) == tgt, e - 1.0, e)
        c_ref[pl.ds(start, TILE), :] = c.astype(BF16)
    g = lax.dot_general(c_ref[...], t_ref[0], TN, preferred_element_type=F32)
    block_rows = g0.shape[1]
    for slot in range(8):
        b = blk[step * 16 + half * 8 + slot]
        acc_ref[slot // MOST, b] += g[slot * block_rows:(slot + 1) * block_rows, :]

    @pl.when(step == pl.num_programs(0) - 1)
    def _():
        for i, out in enumerate((g0, g1, g2, g3)):
            out[...] = acc_ref[i].astype(BF16)


def query_parts(packed, blk, lines, tables, half, blocks, block_rows):
    planes, items, features = tables.shape
    width = packed.shape[1] // 2
    out = jax.ShapeDtypeStruct((blocks, block_rows, features), BF16)
    return pl.pallas_call(
        functools.partial(query_kernel, half),
        grid_spec=pltpu.PrefetchScalarGridSpec(
            num_scalar_prefetch=1,
            grid=(planes,),
            in_specs=[
                pl.BlockSpec((1, width, features), lambda j, blk: (j, half, 0)),
                pl.BlockSpec((1, items, features), lambda j, blk: (j, 0, 0)),
                pl.BlockSpec((1, 2, width), lambda j, blk: (j, 0, half)),
            ],
            out_specs=[pl.BlockSpec(out.shape, lambda j, blk: (0, 0, 0))] * 4,
            scratch_shapes=[
                pltpu.VMEM((items, width), BF16),
                pltpu.VMEM((4, blocks, block_rows, features), F32),
            ],
        ),
        out_shape=[out] * 4,
        compiler_params=pltpu.CompilerParams(vmem_limit_bytes=VMEM),
        cost_estimate=pl.CostEstimate(
            flops=4 * planes * width * items * features,
            bytes_accessed=planes * items * features * 2 + 2 * planes * width * features * 2,
            transcendentals=planes * width * items,
        ),
        name="query_parts",
    )(blk, packed, tables, lines)


def item_kernel(count, where, *refs):
    rows_in, line_ref, t_ref, outs = refs[:count], refs[count], refs[count + 1], refs[count + 2:]
    start = where[pl.program_id(0)] * t_ref.shape[0]
    first = pl.num_programs(0)
    total = None
    for i, ref in enumerate(rows_in):
        source = where[first + i]
        q = ref[...]
        line = line_ref[source]
        lse = line[0:1, :]
        tgt = line[1:2, :].astype(jnp.int32)
        s = lax.dot_general(t_ref[...], q, NT, preferred_element_type=F32)
        e = jnp.exp(s - lse)
        c = jnp.where(tile_ids(start, s.shape) == tgt, e - 1.0, e).astype(BF16)
        part = jnp.dot(c, q, preferred_element_type=F32)
        total = part if total is None else total + part
    cut = t_ref.shape[0] // len(outs)
    for n, out in enumerate(outs):
        out[0] = total[n * cut:(n + 1) * cut]


def item_parts(places, pieces, x, origin, rows, lines, table16, quarters):
    width, features = rows[0].shape
    count = len(rows)
    span = table16.shape[0] // quarters
    share = len(places)
    where = jnp.concatenate([(jnp.array(places, jnp.int32) + x) % quarters, origin])
    out = jax.ShapeDtypeStruct((share, span // pieces, features), F32)
    return pl.pallas_call(
        functools.partial(item_kernel, count),
        grid_spec=pltpu.PrefetchScalarGridSpec(
            num_scalar_prefetch=1,
            grid=(share,),
            in_specs=[pl.BlockSpec((width, features), lambda i, o: (0, 0))] * count
            + [
                pl.BlockSpec(lines.shape, lambda i, o: (0, 0, 0)),
                pl.BlockSpec((span, features), lambda i, o: (o[i], 0)),
            ],
            out_specs=[pl.BlockSpec((1,) + out.shape[1:], lambda i, o: (i, 0, 0))] * pieces,
        ),
        out_shape=[out] * pieces,
        compiler_params=pltpu.CompilerParams(vmem_limit_bytes=VMEM),
        cost_estimate=pl.CostEstimate(
            flops=4 * share * span * count * width * features,
            bytes_accessed=2 * count * width * features + share * span * features * 6,
            transcendentals=share * span * count * width,
        ),
        name="item_parts",
    )(where, *rows, lines, table16)


def update_kernel(x_ref, own, after, before, far_a, far_b, t_ref, a_ref, nt_ref, na_ref):
    quarters = pl.num_programs(0)
    rel = lax.rem(pl.program_id(0) - x_ref[0] + quarters, quarters)
    cut = far_a.shape[0]

    def write(start, summed):
        span = pl.ds(start, summed.shape[0])
        accum = a_ref[span, :] + summed * summed
        na_ref[span, :] = accum
        nt_ref[span, :] = t_ref[span, :] - 0.5 * summed / jnp.sqrt(accum)

    for place, ref in ((0, own), (1, after), (3, before)):

        @pl.when(rel == place)
        def _():
            write(0, ref[...])

    @pl.when(rel == 2)
    def _():
        write(0, far_a[...])
        write(cut, far_b[...])


def update(x, own, after, before, far_a, far_b, table, accum, quarters):
    items, features = table.shape
    whole = pl.BlockSpec(own.shape, lambda i, x: (0, 0))
    part = pl.BlockSpec(far_a.shape, lambda i, x: (0, 0))
    block = pl.BlockSpec((items // quarters, features), lambda i, x: (i, 0))
    return pl.pallas_call(
        update_kernel,
        grid_spec=pltpu.PrefetchScalarGridSpec(
            num_scalar_prefetch=1,
            grid=(quarters,),
            in_specs=[whole] * 3 + [part] * 2 + [block] * 2,
            out_specs=[block] * 2,
        ),
        out_shape=[jax.ShapeDtypeStruct(table.shape, F32)] * 2,
        compiler_params=pltpu.CompilerParams(vmem_limit_bytes=VMEM),
        name="update",
    )(x, own, after, before, far_a, far_b, table, accum)


def local(queries, clusters, positives, owner_of, table, accum):
    z_size = lax.axis_size("z")
    x_size = lax.axis_size("x")
    y_size = lax.axis_size("y")
    c_size = lax.axis_size("c")
    z = lax.axis_index("z")
    y = lax.axis_index("y")
    c = lax.axis_index("c")
    x = lax.axis_index("x").reshape(1)
    local_rows, features = queries.shape
    block_count, picks = clusters.shape
    block_rows = local_rows // block_count
    items = table.shape[1]
    owners = owner_of.shape[0]
    plane = owners // z_size
    pair_count = block_count * picks

    table16 = table[0].astype(BF16)
    tables = lax.all_gather(table16, PLANE)

    here = queries.reshape(block_count, block_rows, features)
    by_source = {0: here, 7: shift(here, "z", 1), 1: shift(here, "z", -1)}
    clusters, positives, by_source[7], by_source[1] = lax.optimization_barrier(
        (clusters, positives, by_source[7], by_source[1])
    )
    by_source[6] = shift(by_source[7], "z", 1)
    by_source[2] = shift(by_source[1], "z", -1)
    by_source[5] = shift(by_source[6], "z", 1)
    by_source[3] = shift(by_source[2], "z", -1)

    flat_lists = clusters.reshape(pair_count)
    catalog_ids = jnp.arange(owners, dtype=jnp.int32)
    lookup = flat_lists[:, None] == catalog_ids[None, :]
    destination = jnp.sum(jnp.where(lookup, owner_of[None, :], 0), axis=1)
    pair_ids = jnp.arange(pair_count, dtype=jnp.int32)
    earlier = (destination[:, None] == destination[None, :]) & (
        pair_ids[:, None] > pair_ids[None, :]
    )
    rank_in = jnp.sum(earlier.astype(jnp.int32), axis=1)
    slot_of_pair = destination * MOST + rank_in
    slot_count = owners * MOST
    matches = slot_of_pair[None, :] == jnp.arange(slot_count, dtype=jnp.int32)[:, None]
    filled = jnp.any(matches, axis=1)
    source_pair = jnp.sum(jnp.where(matches, pair_ids[None, :], 0), axis=1)
    which_block = source_pair // picks
    which_pick = source_pair % picks
    chosen = positives.reshape(block_count, block_rows)[which_block]
    inside = filled[:, None] & (chosen // items == which_pick[:, None])
    send_targets = jnp.where(inside, chosen - which_pick[:, None] * items, -1)
    block_or_none = jnp.where(filled, which_block, -1)
    per_plane = plane * MOST
    meta = jnp.concatenate(
        [
            send_targets.reshape(z_size, per_plane * block_rows),
            block_or_none.reshape(z_size, per_plane),
            jnp.broadcast_to(slot_of_pair[None, :], (z_size, pair_count)),
        ],
        axis=1,
    )
    got = lax.all_to_all(meta, "z", 0, 0, tiled=True)
    by_source[4] = shift(by_source[5], "z", 1)
    order = jnp.array(ORDER, jnp.int32)
    got = got[(z + order) % z_size]
    width = z_size * MOST * block_rows
    cut = per_plane * block_rows
    targets = got[:, :cut].reshape(z_size, plane, MOST, block_rows)
    targets = targets.transpose(1, 0, 2, 3).reshape(plane, 1, width)
    named = got[:, cut:cut + per_plane].reshape(z_size, plane, MOST).transpose(1, 0, 2)
    named = named.reshape(plane * per_plane)
    blk = jnp.maximum(named, 0)

    pair_slot = got[:, cut + per_plane:]
    pair_owner = pair_slot // MOST
    pair_from = (pair_owner // plane - z) % z_size
    pair_rel = (order[:, None] - pair_from) % z_size
    pair_place = jnp.zeros_like(pair_rel)
    for place, d in enumerate(ORDER):
        pair_place = jnp.where(pair_rel == d, place, pair_place)
    pair_row = (pair_owner * 2 * z_size + pair_place) * MOST + pair_slot % MOST

    hops = jnp.arange(plane, dtype=jnp.int32)
    peers = (y + hops // c_size) % y_size * c_size + (c + hops % c_size) % c_size
    origin = (y - hops // c_size) % y_size * c_size + (c - hops % c_size) % c_size
    packed, *outgoing = pack([by_source[d] for d in ORDER], blk, peers)
    rows = [
        shift_plane(value, hop // c_size, hop % c_size) if hop else value
        for hop, value in enumerate(outgoing)
    ]
    stats = forward(packed, targets, tables)

    spread = jnp.broadcast_to(stats[None], (z_size,) + stats.shape)
    all_stats = lax.all_to_all(spread, "z", 0, 0, tiled=True).reshape(-1, block_rows)
    part = all_stats[pair_row.reshape(-1)].reshape(z_size, block_count, picks, block_rows)
    pick = all_stats[pair_row[0] + z_size * MOST].reshape(block_count, picks, block_rows)
    top = jnp.max(part, axis=2)
    lse = top + jnp.log(jnp.sum(jnp.exp(part - top[:, :, None]), axis=2))
    losses = (lse[0] - jnp.sum(pick, axis=1)).reshape(local_rows)
    lse_rows = lse.reshape(z_size * block_count, block_rows)
    first = jnp.arange(z_size, dtype=jnp.int32).reshape(1, z_size, 1) * block_count
    lse_at = (blk.reshape(plane, z_size, MOST) + first).reshape(-1)
    lse_slots = jnp.where(named[:, None] < 0, F32(EMPTY), lse_rows[lse_at])
    lines = jnp.concatenate(
        [lse_slots.reshape(plane, 1, width), targets.astype(F32)], axis=1
    )
    got_lines = lax.all_to_all(lines, PLANE, 0, 0, tiled=True)

    far_g = query_parts(packed, blk, lines, tables, 1, block_count, block_rows)
    far_a, far_b = item_parts((2,), 2, x, origin, rows, got_lines, table16, x_size)
    (rest,) = item_parts((0, 1, 3), 1, x, origin, rows, got_lines, table16, x_size)
    rest, late = lax.optimization_barrier((rest, blk))
    near_g = query_parts(packed, late, lines, tables, 0, block_count, block_rows)
    grads = dict(zip(ORDER, list(near_g) + list(far_g)))

    def add(a, b):
        return (a.astype(F32) + b.astype(F32)).astype(BF16)

    go_right = shift(grads[4], "z", 1)
    go_right = shift(add(go_right, grads[3]), "z", 1)
    go_right = shift(add(go_right, grads[2]), "z", 1)
    go_right = shift(add(go_right, grads[1]), "z", 1)
    go_left = shift(grads[5], "z", -1)
    go_left = shift(add(go_left, grads[6]), "z", -1)
    go_left = shift(add(go_left, grads[7]), "z", -1)
    query_grads = (
        grads[0].astype(F32) + go_right.astype(F32) + go_left.astype(F32)
    ).reshape(local_rows, features)

    far_a, far_b = far_a[0], far_b[0]
    own, after, before = rest[0], rest[1], rest[2]
    half = far_a.shape[0]
    far_a = shift(far_a, "x", 1)
    far_b = shift(far_b, "x", -1)
    after = shift(jnp.concatenate([after[:half] + far_a, after[half:]]), "x", 1)
    before = shift(jnp.concatenate([before[:half], before[half:] + far_b]), "x", -1)
    own, losses = lax.optimization_barrier((own + after + before, losses))
    before = shift(own, "x", 1)
    after = shift(own, "x", -1)
    far_a = shift(before[:half], "x", 1)
    far_b = shift(after[half:], "x", -1)
    new_table, new_accum = update(
        x, own, after, before, far_a, far_b, table[0], accum[0], x_size
    )
    return (losses, query_grads, new_table[None], new_accum[None])


def solution(mesh):
    axes = ("z", "y", "c", "x")
    split = Mesh(mesh.devices.reshape(8, 4, 2, 4), axes)
    placed = (
        P(axes, None),
        P(axes, None),
        P(axes),
        P(),
        P(axes[:3], None, None),
        P(axes[:3], None, None),
    )
    return jax.shard_map(
        local,
        mesh=split,
        in_specs=placed,
        out_specs=(
            P(axes),
            P(axes, None),
            P(axes[:3], None, None),
            P(axes[:3], None, None),
        ),
        check_vma=False,
    )
```

```python
import functools

import jax
import jax.numpy as jnp
from jax import lax
from jax.experimental import pallas as pl
from jax.experimental.pallas import tpu as pltpu
from jax.sharding import Mesh, PartitionSpec as P

MOST = 2
EMPTY = 1e30
PLANE = ("y", "c")
F32 = jnp.float32
BF16 = jnp.bfloat16
NT = (((1,), (1,)), ((), ()))
TN = (((0,), (0,)), ((), ()))
TILE = 256
LARGE = 56 << 20
SMALL = 20 << 20


def shift(value, axis, step):
    size = lax.axis_size(axis)
    return lax.ppermute(value, axis, [(i, (i + step) % size) for i in range(size)])


def tile_ids(start, shape):
    return lax.broadcasted_iota(jnp.int32, shape, 0) + start


def shift_plane(value, dy, dc):
    ys, cs = lax.axis_size("y"), lax.axis_size("c")
    moves = []
    for y in range(ys):
        for c in range(cs):
            moves.append((y * cs + c, (y + dy) % ys * cs + (c + dc) % cs))
    return lax.ppermute(value, PLANE, moves)


def pack_kernel(count, blk, *refs):
    sources, p_ref, outs = refs[:count], refs[count], refs[count + 1:]
    block_rows = sources[0].shape[1]
    per_peer = count * MOST
    for peer, out in enumerate(outs):
        j = blk[len(outs) * per_peer + peer]
        for slot in range(per_peer):
            rows = sources[slot // MOST][blk[j * per_peer + slot]]
            span = pl.ds(slot * block_rows, block_rows)
            out[span, :] = rows
            p_ref[j, span, :] = rows


def pack(sources, blk, peers):
    shape = sources[0].shape
    plane = peers.shape[0]
    width = len(sources) * MOST * shape[1]
    out = jax.ShapeDtypeStruct((width, shape[2]), BF16)
    return pl.pallas_call(
        functools.partial(pack_kernel, len(sources)),
        grid_spec=pltpu.PrefetchScalarGridSpec(
            num_scalar_prefetch=1,
            grid=(1,),
            in_specs=[pl.BlockSpec(shape, lambda j, blk: (0, 0, 0))] * len(sources),
            out_specs=[pl.BlockSpec((plane, width, shape[2]), lambda j, blk: (0, 0, 0))]
            + [pl.BlockSpec(out.shape, lambda j, blk: (0, 0))] * plane,
        ),
        out_shape=[jax.ShapeDtypeStruct((plane, width, shape[2]), BF16)] + [out] * plane,
        compiler_params=pltpu.CompilerParams(vmem_limit_bytes=LARGE),
        cost_estimate=pl.CostEstimate(
            flops=0, bytes_accessed=6 * plane * width * shape[2], transcendentals=0
        ),
        name="pack",
    )(jnp.concatenate([blk, peers]), *sources)


def fetch_table(t_hbm, t_all, sems):
    step = pl.program_id(0)

    @pl.when(step == 0)
    def _():
        for j in range(t_all.shape[0]):
            pltpu.make_async_copy(t_hbm.at[j], t_all.at[j], sems.at[j]).start()

    pltpu.make_async_copy(t_hbm.at[step], t_all.at[step], sems.at[step]).wait()
    return t_all.at[step]


def forward_kernel(p_ref, t_hbm, tgt_ref, stat_ref, s_ref, t_all, sems):
    t_ref = fetch_table(t_hbm, t_all, sems)
    q = p_ref[0]
    items = t_ref.shape[0]
    width = q.shape[0]
    tgt = tgt_ref[0]
    high = jnp.full((8, width), -jnp.inf, F32)
    pick = jnp.zeros((8, width), F32)
    for start in range(0, items, TILE):
        s = lax.dot_general(t_ref[pl.ds(start, TILE), :], q, NT, preferred_element_type=F32)
        s_ref[pl.ds(start, TILE), :] = s
        high = jnp.maximum(high, jnp.max(s.reshape(TILE // 8, 8, width), axis=0))
        hit = jnp.where(tile_ids(start, s.shape) == tgt, s, 0.0)
        pick = pick + jnp.sum(hit.reshape(TILE // 8, 8, width), axis=0)
    top = jnp.max(high, axis=0, keepdims=True)
    mass = jnp.zeros((8, width), F32)
    for start in range(0, items, TILE):
        e = jnp.exp(s_ref[pl.ds(start, TILE), :] - top)
        mass = mass + jnp.sum(e.reshape(TILE // 8, 8, width), axis=0)
    stat_ref[0, 0:1, :] = top + jnp.log(jnp.sum(mass, axis=0, keepdims=True))
    stat_ref[0, 1:2, :] = jnp.sum(pick, axis=0, keepdims=True)


def forward(packed, targets, tables):
    planes, items, features = tables.shape
    width = packed.shape[1]
    return pl.pallas_call(
        forward_kernel,
        grid=(planes,),
        in_specs=[
            pl.BlockSpec((1, width, features), lambda j: (j, 0, 0)),
            pl.BlockSpec(memory_space=pl.ANY),
            pl.BlockSpec((1, 1, width), lambda j: (j, 0, 0)),
        ],
        out_specs=pl.BlockSpec((1, 2, width), lambda j: (j, 0, 0)),
        out_shape=jax.ShapeDtypeStruct((planes, 2, width), F32),
        scratch_shapes=[
            pltpu.VMEM((items, width), F32),
            pltpu.VMEM(tables.shape, BF16),
            pltpu.SemaphoreType.DMA((planes,)),
        ],
        compiler_params=pltpu.CompilerParams(vmem_limit_bytes=LARGE),
        cost_estimate=pl.CostEstimate(
            flops=2 * planes * width * items * features,
            bytes_accessed=planes * items * features * 2 + planes * width * features * 2,
            transcendentals=planes * width * items,
        ),
        name="forward",
    )(packed, tables, targets)


def combine_kernel(addr, named, a_ref, tgt_ref, line_ref, loss_ref, part_ref, lse_ref):
    picks = part_ref.shape[0]
    blocks = lse_ref.shape[0]
    own_blocks = loss_ref.shape[0]
    slots = line_ref.shape[2] // 32

    def fetch(pair, kind):
        a = addr[pair]
        group = pl.multiple_of(lax.shift_right_logical(a, 2) % 4 * 128, 128)
        row = a_ref[lax.shift_right_logical(a, 4), pl.ds(kind, 1), pl.ds(group, 128)]
        return pltpu.roll(row, (4 - a % 4) % 4 * 32, 1)

    def gather(i, carry):
        for p in range(picks):
            part_ref[p, pl.ds(i, 1), :] = fetch(i * picks + p, 0)
        return carry

    lax.fori_loop(0, blocks, gather, 0, unroll=4)
    part = part_ref[...]
    top = jnp.max(part, axis=0)
    lse_ref[...] = top + jnp.log(jnp.sum(jnp.exp(part - top[None]), axis=0))

    def loss(i, carry):
        total = lse_ref[pl.ds(i, 1), :]
        for p in range(picks):
            total = total - fetch(i * picks + p, 1)
        loss_ref[pl.ds(i, 1), :] = total
        return carry

    lax.fori_loop(0, own_blocks, loss, 0, unroll=4)
    lane = lax.broadcasted_iota(jnp.int32, (1, 128), 1)

    def lines(j, carry):
        for group in range(slots // 4):
            value = jnp.full((1, 128), EMPTY, F32)
            for m in range(4):
                slot = group * 4 + m
                b = named[j * slots + slot]
                row = lse_ref[pl.ds(slot // MOST * own_blocks + jnp.maximum(b, 0), 1), :]
                if m:
                    row = pltpu.roll(row, m * 32, 1)
                keep = (lane >= m * 32) & (lane < m * 32 + 32) & (jnp.full((1, 128), b) >= 0)
                value = jnp.where(keep, row, value)
            line_ref[j, 0:1, group * 128:(group + 1) * 128] = value
        line_ref[j, 1:2, :] = tgt_ref[j].astype(F32)
        return carry

    lax.fori_loop(0, line_ref.shape[0], lines, 0)


def combine(addr, named, all_stats, targets, block_count, picks):
    blocks = addr.shape[0] // picks
    plane, _, width = targets.shape
    whole = lambda shape: pl.BlockSpec(shape, lambda i, a, b: (0,) * len(shape))
    lines = jax.ShapeDtypeStruct((plane, 2, width), F32)
    loss = jax.ShapeDtypeStruct((block_count, 128), F32)
    return pl.pallas_call(
        combine_kernel,
        grid_spec=pltpu.PrefetchScalarGridSpec(
            num_scalar_prefetch=2,
            grid=(1,),
            in_specs=[whole(all_stats.shape), whole(targets.shape)],
            out_specs=[whole(lines.shape), whole(loss.shape)],
            scratch_shapes=[pltpu.VMEM((picks, blocks, 128), F32), pltpu.VMEM((blocks, 128), F32)],
        ),
        out_shape=[lines, loss],
        compiler_params=pltpu.CompilerParams(vmem_limit_bytes=SMALL),
        name="combine",
    )(addr, named, all_stats, targets)


def query_kernel(blk, p_ref, t_hbm, line_ref, g_ref, c_ref, acc_ref, t_all, sems):
    step = pl.program_id(0)
    t_ref = fetch_table(t_hbm, t_all, sems)
    sources, blocks, block_rows, _ = acc_ref.shape

    @pl.when(step == 0)
    def _():
        acc_ref[...] = jnp.zeros_like(acc_ref)

    q = p_ref[0]
    lse = line_ref[0, 0:1, :]
    tgt = line_ref[0, 1:2, :].astype(jnp.int32)
    items = t_ref.shape[0]
    for start in range(0, items, TILE):
        s = lax.dot_general(t_ref[pl.ds(start, TILE), :], q, NT, preferred_element_type=F32)
        e = jnp.exp(s - lse)
        c = jnp.where(tile_ids(start, s.shape) == tgt, e - 1.0, e)
        c_ref[pl.ds(start, TILE), :] = c.astype(BF16)
    g = lax.dot_general(c_ref[...], t_ref[...], TN, preferred_element_type=F32)
    slots = sources * MOST
    for slot in range(slots):
        b = blk[step * slots + slot]
        acc_ref[slot // MOST, b] += g[slot * block_rows:(slot + 1) * block_rows, :]

    @pl.when(step == pl.num_programs(0) - 1)
    def _():
        z = blk[pl.num_programs(0) * slots]
        for i in range(sources):
            g_ref[lax.rem(z + i, sources)] = acc_ref[i].astype(BF16)


def query_parts(packed, blk, lines, tables, sources, blocks, block_rows):
    planes, items, features = tables.shape
    width = packed.shape[1]
    out = jax.ShapeDtypeStruct((sources, blocks, block_rows, features), BF16)
    return pl.pallas_call(
        query_kernel,
        grid_spec=pltpu.PrefetchScalarGridSpec(
            num_scalar_prefetch=1,
            grid=(planes,),
            in_specs=[
                pl.BlockSpec((1, width, features), lambda j, blk: (j, 0, 0)),
                pl.BlockSpec(memory_space=pl.ANY),
                pl.BlockSpec((1, 2, width), lambda j, blk: (j, 0, 0)),
            ],
            out_specs=pl.BlockSpec(out.shape, lambda j, blk: (0, 0, 0, 0)),
            scratch_shapes=[
                pltpu.VMEM((items, width), BF16),
                pltpu.VMEM(out.shape, F32),
                pltpu.VMEM(tables.shape, BF16),
                pltpu.SemaphoreType.DMA((planes,)),
            ],
        ),
        out_shape=out,
        compiler_params=pltpu.CompilerParams(vmem_limit_bytes=LARGE),
        cost_estimate=pl.CostEstimate(
            flops=4 * planes * width * items * features,
            bytes_accessed=planes * items * features * 2 + 2 * planes * width * features * 2,
            transcendentals=planes * width * items,
        ),
        name="query_parts",
    )(blk, packed, tables, lines)


def item_kernel(count, where, *refs):
    rows_in, line_ref, t_ref, outs = refs[:count], refs[count], refs[count + 1], refs[count + 2:]
    start = where[pl.program_id(0)] * t_ref.shape[0]
    first = pl.num_programs(0)
    total = None
    for i, ref in enumerate(rows_in):
        source = where[first + i]
        q = ref[...]
        line = line_ref[source]
        lse = line[0:1, :]
        tgt = line[1:2, :].astype(jnp.int32)
        s = lax.dot_general(t_ref[...], q, NT, preferred_element_type=F32)
        e = jnp.exp(s - lse)
        c = jnp.where(tile_ids(start, s.shape) == tgt, e - 1.0, e).astype(BF16)
        part = jnp.dot(c, q, preferred_element_type=F32)
        total = part if total is None else total + part
    cut = t_ref.shape[0] // len(outs)
    for n, out in enumerate(outs):
        out[0] = total[n * cut:(n + 1) * cut]


def item_parts(places, pieces, x, origin, rows, lines, table16, quarters):
    width, features = rows[0].shape
    count = len(rows)
    span = table16.shape[0] // quarters
    share = len(places)
    where = jnp.concatenate([(jnp.array(places, jnp.int32) + x) % quarters, origin])
    out = jax.ShapeDtypeStruct((share, span // pieces, features), F32)
    return pl.pallas_call(
        functools.partial(item_kernel, count),
        grid_spec=pltpu.PrefetchScalarGridSpec(
            num_scalar_prefetch=1,
            grid=(share,),
            in_specs=[pl.BlockSpec((width, features), lambda i, o: (0, 0))] * count
            + [
                pl.BlockSpec(lines.shape, lambda i, o: (0, 0, 0)),
                pl.BlockSpec((span, features), lambda i, o: (o[i], 0)),
            ],
            out_specs=[pl.BlockSpec((1,) + out.shape[1:], lambda i, o: (i, 0, 0))] * pieces,
        ),
        out_shape=[out] * pieces,
        compiler_params=pltpu.CompilerParams(vmem_limit_bytes=SMALL),
        cost_estimate=pl.CostEstimate(
            flops=4 * share * span * count * width * features,
            bytes_accessed=2 * count * width * features + share * span * features * 6,
            transcendentals=share * span * count * width,
        ),
        name="item_parts",
    )(where, *rows, lines, table16)


def update_kernel(x_ref, own, after, before, far_a, far_b, t_ref, a_ref, nt_ref, na_ref):
    quarters = pl.num_programs(0)
    rel = lax.rem(pl.program_id(0) - x_ref[0] + quarters, quarters)
    cut = far_a.shape[0]

    def write(start, summed):
        span = pl.ds(start, summed.shape[0])
        accum = a_ref[span, :] + summed * summed
        na_ref[span, :] = accum
        nt_ref[span, :] = t_ref[span, :] - 0.5 * summed / jnp.sqrt(accum)

    for place, ref in ((0, own), (1, after), (3, before)):

        @pl.when(rel == place)
        def _():
            write(0, ref[...])

    @pl.when(rel == 2)
    def _():
        write(0, far_a[...])
        write(cut, far_b[...])


def update(x, own, after, before, far_a, far_b, table, accum, quarters):
    items, features = table.shape
    whole = pl.BlockSpec(own.shape, lambda i, x: (0, 0))
    part = pl.BlockSpec(far_a.shape, lambda i, x: (0, 0))
    block = pl.BlockSpec((items // quarters, features), lambda i, x: (i, 0))
    return pl.pallas_call(
        update_kernel,
        grid_spec=pltpu.PrefetchScalarGridSpec(
            num_scalar_prefetch=1,
            grid=(quarters,),
            in_specs=[whole] * 3 + [part] * 2 + [block] * 2,
            out_specs=[block] * 2,
        ),
        out_shape=[jax.ShapeDtypeStruct(table.shape, F32)] * 2,
        compiler_params=pltpu.CompilerParams(vmem_limit_bytes=SMALL),
        name="update",
    )(x, own, after, before, far_a, far_b, table, accum)


def local(queries, clusters, positives, owner_of, table, accum):
    z_size = lax.axis_size("z")
    x_size = lax.axis_size("x")
    y_size = lax.axis_size("y")
    c_size = lax.axis_size("c")
    z = lax.axis_index("z")
    y = lax.axis_index("y")
    c = lax.axis_index("c")
    x = lax.axis_index("x").reshape(1)
    local_rows, features = queries.shape
    block_count, picks = clusters.shape
    block_rows = local_rows // block_count
    items = table.shape[1]
    owners = owner_of.shape[0]
    plane = owners // z_size
    pair_count = block_count * picks

    table16 = table[0].astype(BF16)
    tables = lax.all_gather(table16, PLANE)

    here = queries.reshape(block_count, block_rows, features)
    by_source = {0: here, 7: shift(here, "z", 1), 1: shift(here, "z", -1)}
    clusters, positives, by_source[7], by_source[1] = lax.optimization_barrier(
        (clusters, positives, by_source[7], by_source[1])
    )
    by_source[6] = shift(by_source[7], "z", 1)
    by_source[2] = shift(by_source[1], "z", -1)
    by_source[5] = shift(by_source[6], "z", 1)
    by_source[3] = shift(by_source[2], "z", -1)

    flat_lists = clusters.reshape(pair_count)
    catalog_ids = jnp.arange(owners, dtype=jnp.int32)
    lookup = flat_lists[:, None] == catalog_ids[None, :]
    destination = jnp.sum(jnp.where(lookup, owner_of[None, :], 0), axis=1)
    pair_ids = jnp.arange(pair_count, dtype=jnp.int32)
    earlier = (destination[:, None] == destination[None, :]) & (
        pair_ids[:, None] > pair_ids[None, :]
    )
    rank_in = jnp.sum(earlier.astype(jnp.int32), axis=1)
    slot_of_pair = destination * MOST + rank_in
    slot_count = owners * MOST
    matches = slot_of_pair[None, :] == jnp.arange(slot_count, dtype=jnp.int32)[:, None]
    filled = jnp.any(matches, axis=1)
    source_pair = jnp.sum(jnp.where(matches, pair_ids[None, :], 0), axis=1)
    which_block = source_pair // picks
    which_pick = source_pair % picks
    chosen = positives.reshape(block_count, block_rows)[which_block]
    inside = filled[:, None] & (chosen // items == which_pick[:, None])
    send_targets = jnp.where(inside, chosen - which_pick[:, None] * items, -1)
    block_or_none = jnp.where(filled, which_block, -1)
    per_plane = plane * MOST
    meta = jnp.concatenate(
        [
            send_targets.reshape(z_size, per_plane * block_rows),
            block_or_none.reshape(z_size, per_plane),
            jnp.broadcast_to(slot_of_pair[None, :], (z_size, pair_count)),
        ],
        axis=1,
    )
    got = lax.all_to_all(meta, "z", 0, 0, tiled=True)
    by_source[4] = shift(by_source[5], "z", 1)
    order = jnp.arange(z_size, dtype=jnp.int32)
    got = got[(z + order) % z_size]
    width = z_size * MOST * block_rows
    cut = per_plane * block_rows
    targets = got[:, :cut].reshape(z_size, plane, MOST, block_rows)
    targets = targets.transpose(1, 0, 2, 3).reshape(plane, 1, width)
    named = got[:, cut:cut + per_plane].reshape(z_size, plane, MOST).transpose(1, 0, 2)
    named = named.reshape(plane * per_plane)
    blk = jnp.maximum(named, 0)

    pair_slot = got[:, cut + per_plane:]
    pair_owner = pair_slot // MOST
    pair_from = (pair_owner // plane - z) % z_size
    pair_place = (order[:, None] - pair_from) % z_size
    pair_row = (pair_owner * z_size + pair_place) * MOST + pair_slot % MOST

    hops = jnp.arange(plane, dtype=jnp.int32)
    peers = (y + hops // c_size) % y_size * c_size + (c + hops % c_size) % c_size
    origin = (y - hops // c_size) % y_size * c_size + (c - hops % c_size) % c_size
    packed, *outgoing = pack([by_source[d] for d in range(z_size)], blk, peers)
    rows = [
        shift_plane(value, hop // c_size, hop % c_size) if hop else value
        for hop, value in enumerate(outgoing)
    ]
    stats = forward(packed, targets, tables)

    spread = jnp.broadcast_to(stats[None], (z_size,) + stats.shape)
    all_stats = lax.all_to_all(spread, "z", 0, 0, tiled=True)
    all_stats = all_stats.reshape(owners, 2, width)
    lines, losses = combine(
        pair_row.reshape(-1), named, all_stats, targets, block_count, picks
    )
    losses = losses[:, :block_rows].reshape(local_rows)
    got_lines = lax.all_to_all(lines, PLANE, 0, 0, tiled=True)

    grads = query_parts(
        packed, jnp.concatenate([blk, z.reshape(1)]), lines, tables, z_size, block_count, block_rows
    )
    grads, got_lines = lax.optimization_barrier((grads, got_lines))
    query_grads = lax.psum_scatter(grads, "z").astype(F32).reshape(local_rows, features)

    far_a, far_b = item_parts((2,), 2, x, origin, rows, got_lines, table16, x_size)
    far_a, far_b, got_lines = lax.optimization_barrier((far_a, far_b, got_lines))
    (rest,) = item_parts((0, 1, 3), 1, x, origin, rows, got_lines, table16, x_size)
    far_a, far_b = far_a[0], far_b[0]
    own, after, before = rest[0], rest[1], rest[2]
    half = far_a.shape[0]
    far_a = shift(far_a, "x", 1)
    far_b = shift(far_b, "x", -1)
    after = shift(jnp.concatenate([after[:half] + far_a, after[half:]]), "x", 1)
    before = shift(jnp.concatenate([before[:half], before[half:] + far_b]), "x", -1)
    own, losses = lax.optimization_barrier((own + after + before, losses))
    before = shift(own, "x", 1)
    after = shift(own, "x", -1)
    far_a = shift(before[:half], "x", 1)
    far_b = shift(after[half:], "x", -1)
    new_table, new_accum = update(
        x, own, after, before, far_a, far_b, table[0], accum[0], x_size
    )
    return (losses, query_grads, new_table[None], new_accum[None])


def solution(mesh):
    axes = ("z", "y", "c", "x")
    split = Mesh(mesh.devices.reshape(8, 4, 2, 4), axes)
    placed = (
        P(axes, None),
        P(axes, None),
        P(axes),
        P(),
        P(axes[:3], None, None),
        P(axes[:3], None, None),
    )
    return jax.shard_map(
        local,
        mesh=split,
        in_specs=placed,
        out_specs=(
            P(axes),
            P(axes, None),
            P(axes[:3], None, None),
            P(axes[:3], None, None),
        ),
        check_vma=False,
    )
```

```python
import functools

import jax
import jax.numpy as jnp
from jax import lax
from jax.experimental import pallas as pl
from jax.experimental.pallas import tpu as pltpu
from jax.sharding import Mesh, PartitionSpec as P

MOST = 2
EMPTY = 1e30
PLANE = ("y", "c")
F32 = jnp.float32
BF16 = jnp.bfloat16
NT = (((1,), (1,)), ((), ()))
TN = (((0,), (0,)), ((), ()))
TILE = 256
LARGE = 56 << 20
SMALL = 20 << 20


def shift(value, axis, step):
    size = lax.axis_size(axis)
    return lax.ppermute(value, axis, [(i, (i + step) % size) for i in range(size)])


def tile_ids(start, shape):
    return lax.broadcasted_iota(jnp.int32, shape, 0) + start


def pack_kernel(count, blk, *refs):
    sources, p_ref = refs[:2 * count], refs[2 * count]
    half, block_rows = sources[0].shape[:2]
    per_peer = count * MOST
    for j in range(p_ref.shape[0]):
        for slot in range(per_peer):
            b = blk[j * per_peer + slot]
            place = lax.rem(b, half)
            low = sources[slot // MOST * 2][place]
            high = sources[slot // MOST * 2 + 1][place]
            first = jnp.full(low.shape, b, jnp.int32) < half
            p_ref[j, pl.ds(slot * block_rows, block_rows), :] = jnp.where(first, low, high)


def pack(sources, blk, plane):
    shape = sources[0].shape
    count = len(sources) // 2
    width = count * MOST * shape[1]
    out = jax.ShapeDtypeStruct((plane, width, shape[2]), BF16)
    return pl.pallas_call(
        functools.partial(pack_kernel, count),
        grid_spec=pltpu.PrefetchScalarGridSpec(
            num_scalar_prefetch=1,
            grid=(1,),
            in_specs=[pl.BlockSpec(shape, lambda j, blk: (0, 0, 0))] * len(sources),
            out_specs=pl.BlockSpec(out.shape, lambda j, blk: (0, 0, 0)),
        ),
        out_shape=out,
        compiler_params=pltpu.CompilerParams(vmem_limit_bytes=SMALL),
        cost_estimate=pl.CostEstimate(
            flops=0, bytes_accessed=4 * plane * width * shape[2], transcendentals=0
        ),
        name="pack",
    )(blk, *sources)


def fetch_table(t_hbm, t_all, sems):
    step = pl.program_id(0)

    @pl.when(step == 0)
    def _():
        for j in range(t_all.shape[0]):
            pltpu.make_async_copy(t_hbm.at[j], t_all.at[j], sems.at[j]).start()

    pltpu.make_async_copy(t_hbm.at[step], t_all.at[step], sems.at[step]).wait()
    return t_all.at[step]


def forward_kernel(p_ref, t_hbm, tgt_ref, stat_ref, s_ref, t_all, sems):
    t_ref = fetch_table(t_hbm, t_all, sems)
    q = p_ref[0]
    items = t_ref.shape[0]
    width = q.shape[0]
    tgt = tgt_ref[0]
    high = jnp.full((8, width), -jnp.inf, F32)
    pick = jnp.zeros((8, width), F32)
    for start in range(0, items, TILE):
        s = lax.dot_general(t_ref[pl.ds(start, TILE), :], q, NT, preferred_element_type=F32)
        s_ref[pl.ds(start, TILE), :] = s
        high = jnp.maximum(high, jnp.max(s.reshape(TILE // 8, 8, width), axis=0))
        hit = jnp.where(tile_ids(start, s.shape) == tgt, s, 0.0)
        pick = pick + jnp.sum(hit.reshape(TILE // 8, 8, width), axis=0)
    top = jnp.max(high, axis=0, keepdims=True)
    mass = jnp.zeros((8, width), F32)
    for start in range(0, items, TILE):
        e = jnp.exp(s_ref[pl.ds(start, TILE), :] - top)
        mass = mass + jnp.sum(e.reshape(TILE // 8, 8, width), axis=0)
    stat_ref[0, 0:1, :] = top + jnp.log(jnp.sum(mass, axis=0, keepdims=True))
    stat_ref[0, 1:2, :] = jnp.sum(pick, axis=0, keepdims=True)


def forward(packed, targets, tables):
    planes, items, features = tables.shape
    width = packed.shape[1]
    return pl.pallas_call(
        forward_kernel,
        grid=(planes,),
        in_specs=[
            pl.BlockSpec((1, width, features), lambda j: (j, 0, 0)),
            pl.BlockSpec(memory_space=pl.ANY),
            pl.BlockSpec((1, 1, width), lambda j: (j, 0, 0)),
        ],
        out_specs=pl.BlockSpec((1, 2, width), lambda j: (j, 0, 0)),
        out_shape=jax.ShapeDtypeStruct((planes, 2, width), F32),
        scratch_shapes=[
            pltpu.VMEM((items, width), F32),
            pltpu.VMEM(tables.shape, BF16),
            pltpu.SemaphoreType.DMA((planes,)),
        ],
        compiler_params=pltpu.CompilerParams(vmem_limit_bytes=LARGE),
        cost_estimate=pl.CostEstimate(
            flops=2 * planes * width * items * features,
            bytes_accessed=planes * items * features * 2 + planes * width * features * 2,
            transcendentals=planes * width * items,
        ),
        name="forward",
    )(packed, tables, targets)


def query_kernel(blk, p_ref, t_hbm, line_ref, g_ref, c_ref, acc_ref, t_all, sems):
    step = pl.program_id(0)
    t_ref = fetch_table(t_hbm, t_all, sems)
    sources, blocks, block_rows, _ = acc_ref.shape

    @pl.when(step == 0)
    def _():
        acc_ref[...] = jnp.zeros_like(acc_ref)

    q = p_ref[0]
    lse = line_ref[0, 0:1, :]
    tgt = line_ref[0, 1:2, :].astype(jnp.int32)
    items = t_ref.shape[0]
    for start in range(0, items, TILE):
        s = lax.dot_general(t_ref[pl.ds(start, TILE), :], q, NT, preferred_element_type=F32)
        e = jnp.exp(s - lse)
        c = jnp.where(tile_ids(start, s.shape) == tgt, e - 1.0, e)
        c_ref[pl.ds(start, TILE), :] = c.astype(BF16)
    g = lax.dot_general(c_ref[...], t_ref[...], TN, preferred_element_type=F32)
    slots = sources * MOST
    for slot in range(slots):
        b = blk[step * slots + slot]
        acc_ref[slot // MOST, b] += g[slot * block_rows:(slot + 1) * block_rows, :]

    @pl.when(step == pl.num_programs(0) - 1)
    def _():
        z = blk[pl.num_programs(0) * slots]
        for i in range(sources):
            g_ref[lax.rem(z + i, sources)] = acc_ref[i].astype(BF16)


def query_parts(packed, blk, lines, tables, sources, blocks, block_rows):
    planes, items, features = tables.shape
    width = packed.shape[1]
    out = jax.ShapeDtypeStruct((sources, blocks, block_rows, features), BF16)
    return pl.pallas_call(
        query_kernel,
        grid_spec=pltpu.PrefetchScalarGridSpec(
            num_scalar_prefetch=1,
            grid=(planes,),
            in_specs=[
                pl.BlockSpec((1, width, features), lambda j, blk: (j, 0, 0)),
                pl.BlockSpec(memory_space=pl.ANY),
                pl.BlockSpec((1, 2, width), lambda j, blk: (j, 0, 0)),
            ],
            out_specs=pl.BlockSpec(out.shape, lambda j, blk: (0, 0, 0, 0)),
            scratch_shapes=[
                pltpu.VMEM((items, width), BF16),
                pltpu.VMEM(out.shape, F32),
                pltpu.VMEM(tables.shape, BF16),
                pltpu.SemaphoreType.DMA((planes,)),
            ],
        ),
        out_shape=out,
        compiler_params=pltpu.CompilerParams(vmem_limit_bytes=LARGE),
        cost_estimate=pl.CostEstimate(
            flops=4 * planes * width * items * features,
            bytes_accessed=planes * items * features * 2 + 2 * planes * width * features * 2,
            transcendentals=planes * width * items,
        ),
        name="query_parts",
    )(blk, packed, tables, lines)


def item_kernel(where, q_ref, line_ref, t_ref, *outs):
    start = where[pl.program_id(0)] * t_ref.shape[0]
    total = None
    for source in range(q_ref.shape[0]):
        q = q_ref[source]
        line = line_ref[source]
        lse = line[0:1, :]
        tgt = line[1:2, :].astype(jnp.int32)
        s = lax.dot_general(t_ref[...], q, NT, preferred_element_type=F32)
        e = jnp.exp(s - lse)
        c = jnp.where(tile_ids(start, s.shape) == tgt, e - 1.0, e).astype(BF16)
        part = jnp.dot(c, q, preferred_element_type=F32)
        total = part if total is None else total + part
    cut = t_ref.shape[0] // len(outs)
    for n, out in enumerate(outs):
        out[0] = total[n * cut:(n + 1) * cut]


def item_parts(places, pieces, x, rows, lines, table16, quarters):
    count, width, features = rows.shape
    span = table16.shape[0] // quarters
    share = len(places)
    out = jax.ShapeDtypeStruct((share, span // pieces, features), F32)
    return pl.pallas_call(
        item_kernel,
        grid_spec=pltpu.PrefetchScalarGridSpec(
            num_scalar_prefetch=1,
            grid=(share,),
            in_specs=[
                pl.BlockSpec(rows.shape, lambda i, o: (0, 0, 0)),
                pl.BlockSpec(lines.shape, lambda i, o: (0, 0, 0)),
                pl.BlockSpec((span, features), lambda i, o: (o[i], 0)),
            ],
            out_specs=[pl.BlockSpec((1,) + out.shape[1:], lambda i, o: (i, 0, 0))] * pieces,
        ),
        out_shape=[out] * pieces,
        compiler_params=pltpu.CompilerParams(vmem_limit_bytes=SMALL),
        cost_estimate=pl.CostEstimate(
            flops=4 * share * span * count * width * features,
            bytes_accessed=2 * count * width * features + share * span * features * 6,
            transcendentals=share * span * count * width,
        ),
        name="item_parts",
    )((jnp.array(places, jnp.int32) + x) % quarters, rows, lines, table16)


def update_kernel(x_ref, own, after, before, far_a, far_b, t_ref, a_ref, nt_ref, na_ref):
    quarters = pl.num_programs(0)
    rel = lax.rem(pl.program_id(0) - x_ref[0] + quarters, quarters)
    cut = far_a.shape[0]

    def write(start, summed):
        span = pl.ds(start, summed.shape[0])
        accum = a_ref[span, :] + summed * summed
        na_ref[span, :] = accum
        nt_ref[span, :] = t_ref[span, :] - 0.5 * summed / jnp.sqrt(accum)

    for place, ref in ((0, own), (1, after), (3, before)):

        @pl.when(rel == place)
        def _():
            write(0, ref[...])

    @pl.when(rel == 2)
    def _():
        write(0, far_a[...])
        write(cut, far_b[...])


def update(x, own, after, before, far_a, far_b, table, accum, quarters):
    items, features = table.shape
    whole = pl.BlockSpec(own.shape, lambda i, x: (0, 0))
    part = pl.BlockSpec(far_a.shape, lambda i, x: (0, 0))
    block = pl.BlockSpec((items // quarters, features), lambda i, x: (i, 0))
    return pl.pallas_call(
        update_kernel,
        grid_spec=pltpu.PrefetchScalarGridSpec(
            num_scalar_prefetch=1,
            grid=(quarters,),
            in_specs=[whole] * 3 + [part] * 2 + [block] * 2,
            out_specs=[block] * 2,
        ),
        out_shape=[jax.ShapeDtypeStruct(table.shape, F32)] * 2,
        compiler_params=pltpu.CompilerParams(vmem_limit_bytes=SMALL),
        name="update",
    )(x, own, after, before, far_a, far_b, table, accum)


def local(queries, clusters, positives, owner_of, table, accum):
    z_size = lax.axis_size("z")
    x_size = lax.axis_size("x")
    z = lax.axis_index("z")
    x = lax.axis_index("x").reshape(1)
    local_rows, features = queries.shape
    block_count, picks = clusters.shape
    block_rows = local_rows // block_count
    items = table.shape[1]
    owners = owner_of.shape[0]
    plane = owners // z_size
    pair_count = block_count * picks

    table16 = table[0].astype(BF16)
    tables = lax.all_gather(table16, PLANE)

    here = queries.reshape(2, block_count // 2, block_rows, features)
    by_source = [[None] * 2 for _ in range(z_size)]
    for half in range(2):
        right = left = by_source[0][half] = here[half]
        for hop in range(1, z_size // 2 + 1):
            right = by_source[z_size - hop][half] = shift(right, "z", 1)
            if hop < z_size // 2:
                left = by_source[hop][half] = shift(left, "z", -1)

    flat_lists = clusters.reshape(pair_count)
    catalog_ids = jnp.arange(owners, dtype=jnp.int32)
    lookup = flat_lists[:, None] == catalog_ids[None, :]
    destination = jnp.sum(jnp.where(lookup, owner_of[None, :], 0), axis=1)
    pair_ids = jnp.arange(pair_count, dtype=jnp.int32)
    earlier = (destination[:, None] == destination[None, :]) & (
        pair_ids[:, None] > pair_ids[None, :]
    )
    rank_in = jnp.sum(earlier.astype(jnp.int32), axis=1)
    slot_of_pair = destination * MOST + rank_in
    slot_count = owners * MOST
    matches = slot_of_pair[None, :] == jnp.arange(slot_count, dtype=jnp.int32)[:, None]
    filled = jnp.any(matches, axis=1)
    source_pair = jnp.sum(jnp.where(matches, pair_ids[None, :], 0), axis=1)
    which_block = source_pair // picks
    which_pick = source_pair % picks
    chosen = positives.reshape(block_count, block_rows)[which_block]
    inside = filled[:, None] & (chosen // items == which_pick[:, None])
    send_targets = jnp.where(inside, chosen - which_pick[:, None] * items, -1)
    block_or_none = jnp.where(filled, which_block, -1)
    per_plane = plane * MOST
    meta = jnp.concatenate(
        [
            send_targets.reshape(z_size, per_plane * block_rows),
            block_or_none.reshape(z_size, per_plane),
            jnp.broadcast_to(slot_of_pair[None, :], (z_size, pair_count)),
        ],
        axis=1,
    )
    got = lax.all_to_all(meta, "z", 0, 0, tiled=True)
    order = jnp.arange(z_size, dtype=jnp.int32)
    got = got[(z + order) % z_size]
    width = z_size * MOST * block_rows
    cut = per_plane * block_rows
    targets = got[:, :cut].reshape(z_size, plane, MOST, block_rows)
    targets = targets.transpose(1, 0, 2, 3).reshape(plane, 1, width)
    named = got[:, cut:cut + per_plane].reshape(z_size, plane, MOST).transpose(1, 0, 2)
    named = named.reshape(plane * per_plane)
    blk = jnp.maximum(named, 0)

    pair_slot = got[:, cut + per_plane:]
    pair_owner = pair_slot // MOST
    pair_from = (pair_owner // plane - z) % z_size
    pair_place = (order[:, None] - pair_from) % z_size
    pair_row = (pair_from % 2 * 4 + pair_from // 2) * plane + pair_owner % plane
    pair_row = (pair_row * 2 * z_size + pair_place) * MOST + pair_slot % MOST

    packed = pack([part for pair in by_source for part in pair], blk, plane)
    rows = lax.all_to_all(packed, PLANE, 0, 0, tiled=True)
    stats = forward(packed, targets, tables)

    even = jnp.stack([stats] + [shift(stats, "z", -e) for e in (2, 4, 6)])
    all_stats = jnp.stack([even, shift(even, "z", -1)]).reshape(-1, block_rows)
    part = all_stats[pair_row.reshape(-1)].reshape(z_size, block_count, picks, block_rows)
    pick = all_stats[pair_row[0] + z_size * MOST].reshape(block_count, picks, block_rows)
    top = jnp.max(part, axis=2)
    lse = top + jnp.log(jnp.sum(jnp.exp(part - top[:, :, None]), axis=2))
    losses = (lse[0] - jnp.sum(pick, axis=1)).reshape(local_rows)
    lse_rows = lse.reshape(z_size * block_count, block_rows)
    first = jnp.arange(z_size, dtype=jnp.int32).reshape(1, z_size, 1) * block_count
    lse_at = (blk.reshape(plane, z_size, MOST) + first).reshape(-1)
    lse_slots = jnp.where(named[:, None] < 0, F32(EMPTY), lse_rows[lse_at])
    lines = jnp.concatenate(
        [lse_slots.reshape(plane, 1, width), targets.astype(F32)], axis=1
    )

    grads = query_parts(
        packed, jnp.concatenate([blk, z.reshape(1)]), lines, tables, z_size, block_count, block_rows
    )
    grads, lines, rows = lax.optimization_barrier((grads, lines, rows))
    query_grads = lax.psum_scatter(grads, "z").astype(F32).reshape(local_rows, features)
    got_lines = lax.all_to_all(lines, PLANE, 0, 0, tiled=True)

    far_a, far_b = item_parts((2,), 2, x, rows, got_lines, table16, x_size)
    far_a, far_b, got_lines = lax.optimization_barrier((far_a, far_b, got_lines))
    (rest,) = item_parts((0, 1, 3), 1, x, rows, got_lines, table16, x_size)
    far_a, far_b = far_a[0], far_b[0]
    own, after, before = rest[0], rest[1], rest[2]
    half = far_a.shape[0]
    far_a = shift(far_a, "x", 1)
    far_b = shift(far_b, "x", -1)
    after = shift(jnp.concatenate([after[:half] + far_a, after[half:]]), "x", 1)
    before = shift(jnp.concatenate([before[:half], before[half:] + far_b]), "x", -1)
    own, losses = lax.optimization_barrier((own + after + before, losses))
    before = shift(own, "x", 1)
    after = shift(own, "x", -1)
    far_a = shift(before[:half], "x", 1)
    far_b = shift(after[half:], "x", -1)
    new_table, new_accum = update(
        x, own, after, before, far_a, far_b, table[0], accum[0], x_size
    )
    return (losses, query_grads, new_table[None], new_accum[None])


def solution(mesh):
    axes = ("z", "y", "c", "x")
    split = Mesh(mesh.devices.reshape(8, 4, 2, 4), axes)
    placed = (
        P(axes, None),
        P(axes, None),
        P(axes),
        P(),
        P(axes[:3], None, None),
        P(axes[:3], None, None),
    )
    return jax.shard_map(
        local,
        mesh=split,
        in_specs=placed,
        out_specs=(
            P(axes),
            P(axes, None),
            P(axes[:3], None, None),
            P(axes[:3], None, None),
        ),
        check_vma=False,
    )
```

```python
import functools

import jax
import jax.numpy as jnp
from jax import lax
from jax.experimental import pallas as pl
from jax.experimental.pallas import tpu as pltpu
from jax.sharding import Mesh, PartitionSpec as P

MOST = 2
EMPTY = 1e30
PLANE = ("y", "c")
F32 = jnp.float32
BF16 = jnp.bfloat16
NT = (((1,), (1,)), ((), ()))
TN = (((0,), (0,)), ((), ()))
TILE = 256
LARGE = 56 << 20
SMALL = 20 << 20


def shift(value, axis, step):
    size = lax.axis_size(axis)
    return lax.ppermute(value, axis, [(i, (i + step) % size) for i in range(size)])


def tile_ids(start, shape):
    return lax.broadcasted_iota(jnp.int32, shape, 0) + start


def pack_kernel(count, blk, *refs):
    sources, p_ref = refs[:2 * count], refs[2 * count]
    half, block_rows = sources[0].shape[:2]
    per_peer = count * MOST
    for j in range(p_ref.shape[0]):
        for slot in range(per_peer):
            b = blk[j * per_peer + slot]
            place = lax.rem(b, half)
            low = sources[slot // MOST * 2][place]
            high = sources[slot // MOST * 2 + 1][place]
            first = jnp.full(low.shape, b, jnp.int32) < half
            p_ref[j, pl.ds(slot * block_rows, block_rows), :] = jnp.where(first, low, high)


def pack(sources, blk, plane):
    shape = sources[0].shape
    count = len(sources) // 2
    width = count * MOST * shape[1]
    out = jax.ShapeDtypeStruct((plane, width, shape[2]), BF16)
    return pl.pallas_call(
        functools.partial(pack_kernel, count),
        grid_spec=pltpu.PrefetchScalarGridSpec(
            num_scalar_prefetch=1,
            grid=(1,),
            in_specs=[pl.BlockSpec(shape, lambda j, blk: (0, 0, 0))] * len(sources),
            out_specs=pl.BlockSpec(out.shape, lambda j, blk: (0, 0, 0)),
        ),
        out_shape=out,
        compiler_params=pltpu.CompilerParams(vmem_limit_bytes=SMALL),
        cost_estimate=pl.CostEstimate(
            flops=0, bytes_accessed=4 * plane * width * shape[2], transcendentals=0
        ),
        name="pack",
    )(blk, *sources)


def forward_kernel(p_ref, t_ref, tgt_ref, stat_ref, s_all):
    for i in range(p_ref.shape[0]):
        s_ref = s_all.at[i]
        q = p_ref[i]
        items = t_ref.shape[1]
        width = q.shape[0]
        tgt = tgt_ref[i]
        high = jnp.full((8, width), -jnp.inf, F32)
        pick = jnp.zeros((8, width), F32)
        for start in range(0, items, TILE):
            rows = t_ref[i, pl.ds(start, TILE), :]
            s = lax.dot_general(rows, q, NT, preferred_element_type=F32)
            s_ref[pl.ds(start, TILE), :] = s
            high = jnp.maximum(high, jnp.max(s.reshape(TILE // 8, 8, width), axis=0))
            hit = jnp.where(tile_ids(start, s.shape) == tgt, s, 0.0)
            pick = pick + jnp.sum(hit.reshape(TILE // 8, 8, width), axis=0)
        top = jnp.max(high, axis=0, keepdims=True)
        mass = jnp.zeros((8, width), F32)
        for start in range(0, items, TILE):
            e = jnp.exp(s_ref[pl.ds(start, TILE), :] - top)
            mass = mass + jnp.sum(e.reshape(TILE // 8, 8, width), axis=0)
        stat_ref[0, i] = top + jnp.log(jnp.sum(mass, axis=0, keepdims=True))
        stat_ref[1, i] = jnp.sum(pick, axis=0, keepdims=True)


def forward(packed, targets, tables, per=2):
    planes, items, features = tables.shape
    width = packed.shape[1]
    return pl.pallas_call(
        forward_kernel,
        grid=(planes // per,),
        in_specs=[
            pl.BlockSpec((per, width, features), lambda j: (j, 0, 0)),
            pl.BlockSpec((per, items, features), lambda j: (j, 0, 0)),
            pl.BlockSpec((per, 1, width), lambda j: (j, 0, 0)),
        ],
        out_specs=pl.BlockSpec((2, per, 1, width), lambda j: (0, j, 0, 0)),
        out_shape=jax.ShapeDtypeStruct((2, planes, 1, width), F32),
        scratch_shapes=[pltpu.VMEM((per, items, width), F32)],
        compiler_params=pltpu.CompilerParams(vmem_limit_bytes=LARGE),
        cost_estimate=pl.CostEstimate(
            flops=2 * planes * width * items * features,
            bytes_accessed=planes * items * features * 2 + planes * width * features * 2,
            transcendentals=planes * width * items,
        ),
        name="forward",
    )(packed, tables, targets)


def query_kernel(blk, p_ref, t_ref, line_ref, g_ref, c_all, acc_ref):
    step = pl.program_id(0)
    sources, _, block_rows, _ = acc_ref.shape
    per = p_ref.shape[0]
    slots = sources * MOST

    @pl.when(step == 0)
    def _():
        acc_ref[...] = jnp.zeros_like(acc_ref)

    for i in range(per):
        q = p_ref[i]
        lse = line_ref[i, 0:1, :]
        tgt = line_ref[i, 1:2, :].astype(jnp.int32)
        for start in range(0, t_ref.shape[1], TILE):
            rows = t_ref[i, pl.ds(start, TILE), :]
            s = lax.dot_general(rows, q, NT, preferred_element_type=F32)
            e = jnp.exp(s - lse)
            c = jnp.where(tile_ids(start, s.shape) == tgt, e - 1.0, e)
            c_all[i, pl.ds(start, TILE), :] = c.astype(BF16)
        g = lax.dot_general(c_all[i], t_ref[i], TN, preferred_element_type=F32)
        for slot in range(slots):
            b = blk[(step * per + i) * slots + slot]
            acc_ref[slot // MOST, b] += g[slot * block_rows:(slot + 1) * block_rows, :]

    @pl.when(step == pl.num_programs(0) - 1)
    def _():
        z = blk[pl.num_programs(0) * per * slots]
        for i in range(sources):
            g_ref[lax.rem(z + i, sources)] = acc_ref[i].astype(BF16)


def query_parts(packed, blk, lines, tables, sources, blocks, block_rows, per=4):
    planes, items, features = tables.shape
    width = packed.shape[1]
    out = jax.ShapeDtypeStruct((sources, blocks, block_rows, features), BF16)
    return pl.pallas_call(
        query_kernel,
        grid_spec=pltpu.PrefetchScalarGridSpec(
            num_scalar_prefetch=1,
            grid=(planes // per,),
            in_specs=[
                pl.BlockSpec((per, width, features), lambda j, blk: (j, 0, 0)),
                pl.BlockSpec((per, items, features), lambda j, blk: (j, 0, 0)),
                pl.BlockSpec((per, 2, width), lambda j, blk: (j, 0, 0)),
            ],
            out_specs=pl.BlockSpec(out.shape, lambda j, blk: (0, 0, 0, 0)),
            scratch_shapes=[pltpu.VMEM((per, items, width), BF16), pltpu.VMEM(out.shape, F32)],
        ),
        out_shape=out,
        compiler_params=pltpu.CompilerParams(vmem_limit_bytes=LARGE),
        cost_estimate=pl.CostEstimate(
            flops=4 * planes * width * items * features,
            bytes_accessed=planes * items * features * 2 + 2 * planes * width * features * 2,
            transcendentals=planes * width * items,
        ),
        name="query_parts",
    )(blk, packed, tables, lines)


def item_kernel(where, q_ref, line_ref, t_ref, *outs):
    start = where[pl.program_id(0)] * t_ref.shape[1]
    total = None
    for source in range(q_ref.shape[0]):
        q = q_ref[source]
        line = line_ref[source]
        lse = line[0:1, :]
        tgt = line[1:2, :].astype(jnp.int32)
        s = lax.dot_general(t_ref[0], q, NT, preferred_element_type=F32)
        e = jnp.exp(s - lse)
        c = jnp.where(tile_ids(start, s.shape) == tgt, e - 1.0, e).astype(BF16)
        part = jnp.dot(c, q, preferred_element_type=F32)
        total = part if total is None else total + part
    cut = t_ref.shape[1] // len(outs)
    for n, out in enumerate(outs):
        out[0] = total[n * cut:(n + 1) * cut]


def item_parts(places, pieces, x, mine, rows, lines, tables, quarters):
    count, width, features = rows.shape
    span = tables.shape[1] // quarters
    share = len(places)
    out = jax.ShapeDtypeStruct((share, span // pieces, features), F32)
    return pl.pallas_call(
        item_kernel,
        grid_spec=pltpu.PrefetchScalarGridSpec(
            num_scalar_prefetch=1,
            grid=(share,),
            in_specs=[
                pl.BlockSpec(rows.shape, lambda i, o: (0, 0, 0)),
                pl.BlockSpec(lines.shape, lambda i, o: (0, 0, 0)),
                pl.BlockSpec((1, span, features), lambda i, o: (o[share], o[i], 0)),
            ],
            out_specs=[pl.BlockSpec((1,) + out.shape[1:], lambda i, o: (i, 0, 0))] * pieces,
        ),
        out_shape=[out] * pieces,
        compiler_params=pltpu.CompilerParams(vmem_limit_bytes=SMALL),
        cost_estimate=pl.CostEstimate(
            flops=4 * share * span * count * width * features,
            bytes_accessed=2 * count * width * features + share * span * features * 6,
            transcendentals=share * span * count * width,
        ),
        name="item_parts",
    )(jnp.concatenate([(jnp.array(places, jnp.int32) + x) % quarters, mine]), rows, lines, tables)


def update_kernel(x_ref, own, after, before, far_a, far_b, g_ref, t_ref, a_ref, ng_ref, nt_ref, na_ref):
    quarters = pl.num_programs(0)
    rel = lax.rem(pl.program_id(0) - x_ref[0] + quarters, quarters)
    cut = far_a.shape[0]
    ng_ref[...] = g_ref[...].astype(F32)

    def write(start, summed):
        span = pl.ds(start, summed.shape[0])
        accum = a_ref[span, :] + summed * summed
        na_ref[span, :] = accum
        nt_ref[span, :] = t_ref[span, :] - 0.5 * summed / jnp.sqrt(accum)

    for place, ref in ((0, own), (1, after), (3, before)):

        @pl.when(rel == place)
        def _():
            write(0, ref[...])

    @pl.when(rel == 2)
    def _():
        write(0, far_a[...])
        write(cut, far_b[...])


def update(x, own, after, before, far_a, far_b, grads, table, accum, quarters):
    items, features = table.shape
    whole = pl.BlockSpec(own.shape, lambda i, x: (0, 0))
    part = pl.BlockSpec(far_a.shape, lambda i, x: (0, 0))
    block = pl.BlockSpec((items // quarters, features), lambda i, x: (i, 0))
    piece = pl.BlockSpec((grads.shape[0] // quarters, features), lambda i, x: (i, 0))
    return pl.pallas_call(
        update_kernel,
        grid_spec=pltpu.PrefetchScalarGridSpec(
            num_scalar_prefetch=1,
            grid=(quarters,),
            in_specs=[whole] * 3 + [part] * 2 + [piece] + [block] * 2,
            out_specs=[piece] + [block] * 2,
        ),
        out_shape=[jax.ShapeDtypeStruct(grads.shape, F32)]
        + [jax.ShapeDtypeStruct(table.shape, F32)] * 2,
        compiler_params=pltpu.CompilerParams(vmem_limit_bytes=SMALL),
        name="update",
    )(x, own, after, before, far_a, far_b, grads, table, accum)


def local(queries, clusters, positives, owner_of, table, accum):
    z_size = lax.axis_size("z")
    x_size = lax.axis_size("x")
    z = lax.axis_index("z")
    x = lax.axis_index("x").reshape(1)
    local_rows, features = queries.shape
    block_count, picks = clusters.shape
    block_rows = local_rows // block_count
    items = table.shape[1]
    owners = owner_of.shape[0]
    plane = owners // z_size
    pair_count = block_count * picks

    tables = lax.all_gather(table[0].astype(BF16), PLANE)
    mine = (lax.axis_index("y") * lax.axis_size("c") + lax.axis_index("c")).reshape(1)

    here = queries.reshape(2, block_count // 2, block_rows, features)
    by_source = [[None] * 2 for _ in range(z_size)]
    for half in range(2):
        right = left = by_source[0][half] = here[half]
        for hop in range(1, z_size // 2 + 1):
            right = by_source[z_size - hop][half] = shift(right, "z", 1)
            if hop < z_size // 2:
                left = by_source[hop][half] = shift(left, "z", -1)

    flat_lists = clusters.reshape(pair_count)
    catalog_ids = jnp.arange(owners, dtype=jnp.int32)
    lookup = flat_lists[:, None] == catalog_ids[None, :]
    destination = jnp.sum(jnp.where(lookup, owner_of[None, :], 0), axis=1)
    pair_ids = jnp.arange(pair_count, dtype=jnp.int32)
    earlier = (destination[:, None] == destination[None, :]) & (
        pair_ids[:, None] > pair_ids[None, :]
    )
    rank_in = jnp.sum(earlier.astype(jnp.int32), axis=1)
    slot_of_pair = destination * MOST + rank_in
    slot_count = owners * MOST
    matches = slot_of_pair[None, :] == jnp.arange(slot_count, dtype=jnp.int32)[:, None]
    filled = jnp.any(matches, axis=1)
    source_pair = jnp.sum(jnp.where(matches, pair_ids[None, :], 0), axis=1)
    which_block = source_pair // picks
    which_pick = source_pair % picks
    chosen = positives.reshape(block_count, block_rows)[which_block]
    inside = filled[:, None] & (chosen // items == which_pick[:, None])
    send_targets = jnp.where(inside, chosen - which_pick[:, None] * items, -1)
    block_or_none = jnp.where(filled, which_block, -1)
    per_plane = plane * MOST
    meta = jnp.concatenate(
        [
            send_targets.reshape(z_size, per_plane * block_rows),
            block_or_none.reshape(z_size, per_plane),
            jnp.broadcast_to(slot_of_pair[None, :], (z_size, pair_count)),
        ],
        axis=1,
    )
    meta, _ = lax.optimization_barrier((meta, by_source[5][0]))
    got = lax.all_to_all(meta, "z", 0, 0, tiled=True)
    order = jnp.arange(z_size, dtype=jnp.int32)
    got = got[(z + order) % z_size]
    width = z_size * MOST * block_rows
    cut = per_plane * block_rows
    targets = got[:, :cut].reshape(z_size, plane, MOST, block_rows)
    targets = targets.transpose(1, 0, 2, 3).reshape(plane, 1, width)
    named = got[:, cut:cut + per_plane].reshape(z_size, plane, MOST).transpose(1, 0, 2)
    named = named.reshape(plane * per_plane)
    blk = jnp.maximum(named, 0)

    pair_slot = got[:, cut + per_plane:]
    pair_owner = pair_slot // MOST
    pair_from = (pair_owner // plane - z) % z_size
    pair_place = (order[:, None] - pair_from) % z_size
    pair_row = (pair_from % 2 * 4 + pair_from // 2) * plane + pair_owner % plane
    pair_row = (pair_row * z_size + pair_place) * MOST + pair_slot % MOST

    packed = pack([part for pair in by_source for part in pair], blk, plane)
    rows = lax.all_to_all(packed, PLANE, 0, 0, tiled=True)
    stats = forward(packed, targets, tables)

    even = jnp.stack([stats] + [shift(stats, "z", -e) for e in (2, 4, 6)])
    all_stats = jnp.stack([even, shift(even, "z", -1)]).reshape(z_size, 2, -1)
    part = all_stats[:, 0].reshape(-1, block_rows)[pair_row.reshape(-1)]
    part = part.reshape(z_size, block_count, picks, block_rows)
    pick = all_stats[:, 1].reshape(-1, block_rows)[pair_row[0]]
    pick = pick.reshape(block_count, picks, block_rows)
    top = jnp.max(part, axis=2)
    lse = top + jnp.log(jnp.sum(jnp.exp(part - top[:, :, None]), axis=2))
    losses = (lse[0] - jnp.sum(pick, axis=1)).reshape(local_rows)
    lse_rows = lse.reshape(z_size * block_count, block_rows)
    first = jnp.arange(z_size, dtype=jnp.int32).reshape(1, z_size, 1) * block_count
    lse_at = (blk.reshape(plane, z_size, MOST) + first).reshape(-1)
    lse_slots = jnp.where(named[:, None] < 0, F32(EMPTY), lse_rows[lse_at])
    lines = jnp.concatenate(
        [lse_slots.reshape(plane, 1, width), targets.astype(F32)], axis=1
    )

    grads = query_parts(
        packed, jnp.concatenate([blk, z.reshape(1)]), lines, tables, z_size, block_count, block_rows
    )
    grads, lines, rows = lax.optimization_barrier((grads, lines, rows))
    grads = lax.psum_scatter(grads, "z").reshape(local_rows, features)
    got_lines = lax.all_to_all(lines, PLANE, 0, 0, tiled=True)

    far_a, far_b = item_parts((2,), 2, x, mine, rows, got_lines, tables, x_size)
    far_a, far_b, got_lines = lax.optimization_barrier((far_a, far_b, got_lines))
    (rest,) = item_parts((0, 1, 3), 1, x, mine, rows, got_lines, tables, x_size)
    far_a, far_b = far_a[0], far_b[0]
    own, after, before = rest[0], rest[1], rest[2]
    half = far_a.shape[0]
    far_a = shift(far_a, "x", 1)
    far_b = shift(far_b, "x", -1)
    after = shift(jnp.concatenate([after[:half] + far_a, after[half:]]), "x", 1)
    before = shift(jnp.concatenate([before[:half], before[half:] + far_b]), "x", -1)
    own, losses = lax.optimization_barrier((own + after + before, losses))
    before = shift(own, "x", 1)
    after = shift(own, "x", -1)
    far_a = shift(before[:half], "x", 1)
    far_b = shift(after[half:], "x", -1)
    query_grads, new_table, new_accum = update(
        x, own, after, before, far_a, far_b, grads, table[0], accum[0], x_size
    )
    return (losses, query_grads, new_table[None], new_accum[None])


def solution(mesh):
    axes = ("z", "y", "c", "x")
    split = Mesh(mesh.devices.reshape(8, 4, 2, 4), axes)
    placed = (
        P(axes, None),
        P(axes, None),
        P(axes),
        P(),
        P(axes[:3], None, None),
        P(axes[:3], None, None),
    )
    return jax.shard_map(
        local,
        mesh=split,
        in_specs=placed,
        out_specs=(
            P(axes),
            P(axes, None),
            P(axes[:3], None, None),
            P(axes[:3], None, None),
        ),
        check_vma=False,
    )
```

```python
import functools

import jax
import jax.numpy as jnp
from jax import lax
from jax.experimental import pallas as pl
from jax.experimental.pallas import tpu as pltpu
from jax.sharding import Mesh, PartitionSpec as P

MOST = 2
EMPTY = 1e30
PLANE = ("y", "c")
F32 = jnp.float32
BF16 = jnp.bfloat16
NT = (((1,), (1,)), ((), ()))
TN = (((0,), (0,)), ((), ()))
TILE = 256
LARGE = 56 << 20
SMALL = 20 << 20


def shift(value, axis, step):
    size = lax.axis_size(axis)
    return lax.ppermute(value, axis, [(i, (i + step) % size) for i in range(size)])


def tile_ids(start, shape):
    return lax.broadcasted_iota(jnp.int32, shape, 0) + start


def pack_kernel(count, blk, *refs):
    sources, p_ref = refs[:2 * count], refs[2 * count]
    half, block_rows = sources[0].shape[:2]
    per_peer = count * MOST
    for j in range(p_ref.shape[0]):
        for slot in range(per_peer):
            b = blk[j * per_peer + slot]
            place = lax.rem(b, half)
            low = sources[slot // MOST * 2][place]
            high = sources[slot // MOST * 2 + 1][place]
            first = jnp.full(low.shape, b, jnp.int32) < half
            p_ref[j, pl.ds(slot * block_rows, block_rows), :] = jnp.where(first, low, high)


def pack(sources, blk, plane):
    shape = sources[0].shape
    count = len(sources) // 2
    width = count * MOST * shape[1]
    out = jax.ShapeDtypeStruct((plane, width, shape[2]), BF16)
    return pl.pallas_call(
        functools.partial(pack_kernel, count),
        grid_spec=pltpu.PrefetchScalarGridSpec(
            num_scalar_prefetch=1,
            grid=(1,),
            in_specs=[pl.BlockSpec(shape, lambda j, blk: (0, 0, 0))] * len(sources),
            out_specs=pl.BlockSpec(out.shape, lambda j, blk: (0, 0, 0)),
        ),
        out_shape=out,
        compiler_params=pltpu.CompilerParams(vmem_limit_bytes=SMALL),
        cost_estimate=pl.CostEstimate(
            flops=0, bytes_accessed=4 * plane * width * shape[2], transcendentals=0
        ),
        name="pack",
    )(blk, *sources)


def forward_kernel(p_ref, t_ref, tgt_ref, stat_ref, s_all):
    for i in range(p_ref.shape[0]):
        s_ref = s_all.at[i]
        q = p_ref[i]
        items = t_ref.shape[1]
        width = q.shape[0]
        tgt = tgt_ref[i]
        high = jnp.full((8, width), -jnp.inf, F32)
        pick = jnp.zeros((8, width), F32)
        for start in range(0, items, TILE):
            rows = t_ref[i, pl.ds(start, TILE), :]
            s = lax.dot_general(rows, q, NT, preferred_element_type=F32)
            s_ref[pl.ds(start, TILE), :] = s
            high = jnp.maximum(high, jnp.max(s.reshape(TILE // 8, 8, width), axis=0))
            hit = jnp.where(tile_ids(start, s.shape) == tgt, s, 0.0)
            pick = pick + jnp.sum(hit.reshape(TILE // 8, 8, width), axis=0)
        top = jnp.max(high, axis=0, keepdims=True)
        mass = jnp.zeros((8, width), F32)
        for start in range(0, items, TILE):
            e = jnp.exp(s_ref[pl.ds(start, TILE), :] - top)
            mass = mass + jnp.sum(e.reshape(TILE // 8, 8, width), axis=0)
        stat_ref[0, i] = top + jnp.log(jnp.sum(mass, axis=0, keepdims=True))
        stat_ref[1, i] = jnp.sum(pick, axis=0, keepdims=True)


def forward(packed, targets, tables, per=2):
    planes, items, features = tables.shape
    width = packed.shape[1]
    return pl.pallas_call(
        forward_kernel,
        grid=(planes // per,),
        in_specs=[
            pl.BlockSpec((per, width, features), lambda j: (j, 0, 0)),
            pl.BlockSpec((per, items, features), lambda j: (j, 0, 0)),
            pl.BlockSpec((per, 1, width), lambda j: (j, 0, 0)),
        ],
        out_specs=pl.BlockSpec((2, per, 1, width), lambda j: (0, j, 0, 0)),
        out_shape=jax.ShapeDtypeStruct((2, planes, 1, width), F32),
        scratch_shapes=[pltpu.VMEM((per, items, width), F32)],
        compiler_params=pltpu.CompilerParams(vmem_limit_bytes=LARGE),
        cost_estimate=pl.CostEstimate(
            flops=40 * planes * width * items * features,
            bytes_accessed=planes * items * features * 2 + planes * width * features * 2,
            transcendentals=planes * width * items,
        ),
        name="forward",
    )(packed, tables, targets)


def query_kernel(blk, p_ref, t_ref, line_ref, g_ref, c_all, acc_ref):
    step = pl.program_id(0)
    sources, _, block_rows, _ = acc_ref.shape
    per = p_ref.shape[0]
    slots = sources * MOST

    @pl.when(step == 0)
    def _():
        acc_ref[...] = jnp.zeros_like(acc_ref)

    for i in range(per):
        q = p_ref[i]
        lse = line_ref[i, 0:1, :]
        tgt = line_ref[i, 1:2, :].astype(jnp.int32)
        for start in range(0, t_ref.shape[1], TILE):
            rows = t_ref[i, pl.ds(start, TILE), :]
            s = lax.dot_general(rows, q, NT, preferred_element_type=F32)
            e = jnp.exp(s - lse)
            c = jnp.where(tile_ids(start, s.shape) == tgt, e - 1.0, e)
            c_all[i, pl.ds(start, TILE), :] = c.astype(BF16)
        g = lax.dot_general(c_all[i], t_ref[i], TN, preferred_element_type=F32)
        for slot in range(slots):
            b = blk[(step * per + i) * slots + slot]
            acc_ref[slot // MOST, b] += g[slot * block_rows:(slot + 1) * block_rows, :]

    @pl.when(step == pl.num_programs(0) - 1)
    def _():
        z = blk[pl.num_programs(0) * per * slots]
        for i in range(sources):
            g_ref[lax.rem(z + i, sources)] = acc_ref[i].astype(BF16)


def query_parts(packed, blk, lines, tables, sources, blocks, block_rows, per=4):
    planes, items, features = tables.shape
    width = packed.shape[1]
    out = jax.ShapeDtypeStruct((sources, blocks, block_rows, features), BF16)
    return pl.pallas_call(
        query_kernel,
        grid_spec=pltpu.PrefetchScalarGridSpec(
            num_scalar_prefetch=1,
            grid=(planes // per,),
            in_specs=[
                pl.BlockSpec((per, width, features), lambda j, blk: (j, 0, 0)),
                pl.BlockSpec((per, items, features), lambda j, blk: (j, 0, 0)),
                pl.BlockSpec((per, 2, width), lambda j, blk: (j, 0, 0)),
            ],
            out_specs=pl.BlockSpec(out.shape, lambda j, blk: (0, 0, 0, 0)),
            scratch_shapes=[pltpu.VMEM((per, items, width), BF16), pltpu.VMEM(out.shape, F32)],
        ),
        out_shape=out,
        compiler_params=pltpu.CompilerParams(vmem_limit_bytes=LARGE),
        cost_estimate=pl.CostEstimate(flops=1 << 20, bytes_accessed=1 << 20, transcendentals=0),
        name="query_parts",
    )(blk, packed, tables, lines)


def item_kernel(where, q_ref, line_ref, t_ref, *outs):
    start = where[pl.program_id(0)] * t_ref.shape[0]
    total = None
    for source in range(q_ref.shape[0]):
        q = q_ref[source]
        line = line_ref[source]
        lse = line[0:1, :]
        tgt = line[1:2, :].astype(jnp.int32)
        s = lax.dot_general(t_ref[...], q, NT, preferred_element_type=F32)
        e = jnp.exp(s - lse)
        c = jnp.where(tile_ids(start, s.shape) == tgt, e - 1.0, e).astype(BF16)
        part = jnp.dot(c, q, preferred_element_type=F32)
        total = part if total is None else total + part
    cut = t_ref.shape[0] // len(outs)
    for n, out in enumerate(outs):
        out[0] = total[n * cut:(n + 1) * cut]


def item_parts(places, pieces, x, rows, lines, table16, quarters):
    count, width, features = rows.shape
    span = table16.shape[0] // quarters
    share = len(places)
    out = jax.ShapeDtypeStruct((share, span // pieces, features), F32)
    return pl.pallas_call(
        item_kernel,
        grid_spec=pltpu.PrefetchScalarGridSpec(
            num_scalar_prefetch=1,
            grid=(share,),
            in_specs=[
                pl.BlockSpec(rows.shape, lambda i, o: (0, 0, 0)),
                pl.BlockSpec(lines.shape, lambda i, o: (0, 0, 0)),
                pl.BlockSpec((span, features), lambda i, o: (o[i], 0)),
            ],
            out_specs=[pl.BlockSpec((1,) + out.shape[1:], lambda i, o: (i, 0, 0))] * pieces,
        ),
        out_shape=[out] * pieces,
        compiler_params=pltpu.CompilerParams(vmem_limit_bytes=SMALL),
        cost_estimate=pl.CostEstimate(
            flops=4 * share * span * count * width * features,
            bytes_accessed=2 * count * width * features + share * span * features * 6,
            transcendentals=share * span * count * width,
        ),
        name="item_parts",
    )((jnp.array(places, jnp.int32) + x) % quarters, rows, lines, table16)


def update_kernel(x_ref, own, after, before, far_a, far_b, g_ref, t_ref, a_ref, ng_ref, nt_ref, na_ref):
    quarters = pl.num_programs(0)
    rel = lax.rem(pl.program_id(0) - x_ref[0] + quarters, quarters)
    cut = far_a.shape[0]
    ng_ref[...] = g_ref[...].astype(F32)

    def write(start, summed):
        span = pl.ds(start, summed.shape[0])
        accum = a_ref[span, :] + summed * summed
        na_ref[span, :] = accum
        nt_ref[span, :] = t_ref[span, :] - 0.5 * summed / jnp.sqrt(accum)

    for place, ref in ((0, own), (1, after), (3, before)):

        @pl.when(rel == place)
        def _():
            write(0, ref[...])

    @pl.when(rel == 2)
    def _():
        write(0, far_a[...])
        write(cut, far_b[...])


def update(x, own, after, before, far_a, far_b, grads, table, accum, quarters):
    items, features = table.shape
    whole = pl.BlockSpec(own.shape, lambda i, x: (0, 0))
    part = pl.BlockSpec(far_a.shape, lambda i, x: (0, 0))
    block = pl.BlockSpec((items // quarters, features), lambda i, x: (i, 0))
    piece = pl.BlockSpec((grads.shape[0] // quarters, features), lambda i, x: (i, 0))
    return pl.pallas_call(
        update_kernel,
        grid_spec=pltpu.PrefetchScalarGridSpec(
            num_scalar_prefetch=1,
            grid=(quarters,),
            in_specs=[whole] * 3 + [part] * 2 + [piece] + [block] * 2,
            out_specs=[piece] + [block] * 2,
        ),
        out_shape=[jax.ShapeDtypeStruct(grads.shape, F32)]
        + [jax.ShapeDtypeStruct(table.shape, F32)] * 2,
        compiler_params=pltpu.CompilerParams(vmem_limit_bytes=SMALL),
        name="update",
    )(x, own, after, before, far_a, far_b, grads, table, accum)


def local(queries, clusters, positives, owner_of, table, accum):
    z_size = lax.axis_size("z")
    x_size = lax.axis_size("x")
    z = lax.axis_index("z")
    x = lax.axis_index("x").reshape(1)
    local_rows, features = queries.shape
    block_count, picks = clusters.shape
    block_rows = local_rows // block_count
    items = table.shape[1]
    owners = owner_of.shape[0]
    plane = owners // z_size
    pair_count = block_count * picks

    tables = lax.all_gather(table[0].astype(BF16), PLANE)

    here = queries.reshape(2, block_count // 2, block_rows, features)
    by_source = [[None] * 2 for _ in range(z_size)]
    for half in range(2):
        right = left = by_source[0][half] = here[half]
        for hop in range(1, z_size // 2 + 1):
            right = by_source[z_size - hop][half] = shift(right, "z", 1)
            if hop < z_size // 2:
                left = by_source[hop][half] = shift(left, "z", -1)

    flat_lists = clusters.reshape(pair_count)
    catalog_ids = jnp.arange(owners, dtype=jnp.int32)
    lookup = flat_lists[:, None] == catalog_ids[None, :]
    destination = jnp.sum(jnp.where(lookup, owner_of[None, :], 0), axis=1)
    pair_ids = jnp.arange(pair_count, dtype=jnp.int32)
    earlier = (destination[:, None] == destination[None, :]) & (
        pair_ids[:, None] > pair_ids[None, :]
    )
    rank_in = jnp.sum(earlier.astype(jnp.int32), axis=1)
    slot_of_pair = destination * MOST + rank_in
    slot_count = owners * MOST
    matches = slot_of_pair[None, :] == jnp.arange(slot_count, dtype=jnp.int32)[:, None]
    filled = jnp.any(matches, axis=1)
    source_pair = jnp.sum(jnp.where(matches, pair_ids[None, :], 0), axis=1)
    which_block = source_pair // picks
    which_pick = source_pair % picks
    chosen = positives.reshape(block_count, block_rows)[which_block]
    inside = filled[:, None] & (chosen // items == which_pick[:, None])
    send_targets = jnp.where(inside, chosen - which_pick[:, None] * items, -1)
    block_or_none = jnp.where(filled, which_block, -1)
    per_plane = plane * MOST
    meta = jnp.concatenate(
        [
            send_targets.reshape(z_size, per_plane * block_rows),
            block_or_none.reshape(z_size, per_plane),
            jnp.broadcast_to(slot_of_pair[None, :], (z_size, pair_count)),
        ],
        axis=1,
    )
    meta, _ = lax.optimization_barrier((meta, by_source[5][0]))
    got = lax.all_to_all(meta, "z", 0, 0, tiled=True)
    order = jnp.arange(z_size, dtype=jnp.int32)
    got = got[(z + order) % z_size]
    width = z_size * MOST * block_rows
    cut = per_plane * block_rows
    targets = got[:, :cut].reshape(z_size, plane, MOST, block_rows)
    targets = targets.transpose(1, 0, 2, 3).reshape(plane, 1, width)
    named = got[:, cut:cut + per_plane].reshape(z_size, plane, MOST).transpose(1, 0, 2)
    named = named.reshape(plane * per_plane)
    blk = jnp.maximum(named, 0)

    pair_slot = got[:, cut + per_plane:]
    pair_owner = pair_slot // MOST
    pair_from = (pair_owner // plane - z) % z_size
    pair_place = (order[:, None] - pair_from) % z_size
    pair_row = (pair_from % 2 * 4 + pair_from // 2) * plane + pair_owner % plane
    pair_row = (pair_row * z_size + pair_place) * MOST + pair_slot % MOST

    own_table, blk = lax.optimization_barrier((table[0], blk))
    own_table = own_table.astype(BF16)
    packed = pack([part for pair in by_source for part in pair], blk, plane)
    rows = lax.all_to_all(packed, PLANE, 0, 0, tiled=True)
    stats = forward(packed, targets, tables)

    even = jnp.stack([stats] + [shift(stats, "z", -e) for e in (2, 4, 6)])
    all_stats = jnp.stack([even, shift(even, "z", -1)]).reshape(z_size, 2, -1)
    part = all_stats[:, 0].reshape(-1, block_rows)[pair_row.reshape(-1)]
    part, rows = lax.optimization_barrier((part, rows))
    part = part.reshape(z_size, block_count, picks, block_rows)
    pick = all_stats[:, 1].reshape(-1, block_rows)[pair_row[0]]
    pick = pick.reshape(block_count, picks, block_rows)
    top = jnp.max(part, axis=2)
    lse = top + jnp.log(jnp.sum(jnp.exp(part - top[:, :, None]), axis=2))
    losses = (lse[0] - jnp.sum(pick, axis=1)).reshape(local_rows)
    lse_rows = lse.reshape(z_size * block_count, block_rows)
    first = jnp.arange(z_size, dtype=jnp.int32).reshape(1, z_size, 1) * block_count
    lse_at = (blk.reshape(plane, z_size, MOST) + first).reshape(-1)
    lse_slots = jnp.where(named[:, None] < 0, F32(EMPTY), lse_rows[lse_at])
    lines = jnp.concatenate(
        [lse_slots.reshape(plane, 1, width), targets.astype(F32)], axis=1
    )

    grads = query_parts(
        packed, jnp.concatenate([blk, z.reshape(1)]), lines, tables, z_size, block_count, block_rows
    )
    grads, lines = lax.optimization_barrier((grads, lines))
    grads = lax.psum_scatter(grads, "z").reshape(local_rows, features)
    got_lines = lax.all_to_all(lines, PLANE, 0, 0, tiled=True)

    far_a, far_b = item_parts((2,), 2, x, rows, got_lines, own_table, x_size)
    far_a, far_b, got_lines = lax.optimization_barrier((far_a, far_b, got_lines))
    (rest,) = item_parts((0, 1, 3), 1, x, rows, got_lines, own_table, x_size)
    far_a, far_b = far_a[0], far_b[0]
    own, after, before = rest[0], rest[1], rest[2]
    half = far_a.shape[0]
    far_a = shift(far_a, "x", 1)
    far_b = shift(far_b, "x", -1)
    after = shift(jnp.concatenate([after[:half] + far_a, after[half:]]), "x", 1)
    before = shift(jnp.concatenate([before[:half], before[half:] + far_b]), "x", -1)
    own, losses = lax.optimization_barrier((own + after + before, losses))
    before = shift(own, "x", 1)
    after = shift(own, "x", -1)
    far_a = shift(before[:half], "x", 1)
    far_b = shift(after[half:], "x", -1)
    query_grads, new_table, new_accum = update(
        x, own, after, before, far_a, far_b, grads, table[0], accum[0], x_size
    )
    return (losses, query_grads, new_table[None], new_accum[None])


def solution(mesh):
    axes = ("z", "y", "c", "x")
    split = Mesh(mesh.devices.reshape(8, 4, 2, 4), axes)
    placed = (
        P(axes, None),
        P(axes, None),
        P(axes),
        P(),
        P(axes[:3], None, None),
        P(axes[:3], None, None),
    )
    return jax.shard_map(
        local,
        mesh=split,
        in_specs=placed,
        out_specs=(
            P(axes),
            P(axes, None),
            P(axes[:3], None, None),
            P(axes[:3], None, None),
        ),
        check_vma=False,
    )
```

```python
import functools

import jax
import jax.numpy as jnp
from jax import lax
from jax.experimental import pallas as pl
from jax.experimental.pallas import tpu as pltpu
from jax.sharding import Mesh, PartitionSpec as P

MOST = 2
EMPTY = 1e30
PLANE = ("y", "c")
F32 = jnp.float32
BF16 = jnp.bfloat16
NT = (((1,), (1,)), ((), ()))
TN = (((0,), (0,)), ((), ()))
TILE = 256
LARGE = 56 << 20
SMALL = 20 << 20


def shift(value, axis, step):
    size = lax.axis_size(axis)
    return lax.ppermute(value, axis, [(i, (i + step) % size) for i in range(size)])


def tile_ids(start, shape):
    return lax.broadcasted_iota(jnp.int32, shape, 0) + start


def pack_kernel(count, blk, *refs):
    sources, p_ref = refs[:2 * count], refs[2 * count]
    half, block_rows = sources[0].shape[:2]
    per_peer = count * MOST
    for j in range(p_ref.shape[0]):
        for slot in range(per_peer):
            b = blk[j * per_peer + slot]
            place = lax.rem(b, half)
            low = sources[slot // MOST * 2][place]
            high = sources[slot // MOST * 2 + 1][place]
            first = jnp.full(low.shape, b, jnp.int32) < half
            p_ref[j, pl.ds(slot * block_rows, block_rows), :] = jnp.where(first, low, high)


def pack(sources, blk, plane):
    shape = sources[0].shape
    count = len(sources) // 2
    width = count * MOST * shape[1]
    out = jax.ShapeDtypeStruct((plane, width, shape[2]), BF16)
    return pl.pallas_call(
        functools.partial(pack_kernel, count),
        grid_spec=pltpu.PrefetchScalarGridSpec(
            num_scalar_prefetch=1,
            grid=(1,),
            in_specs=[pl.BlockSpec(v.shape, lambda j, blk: (0, 0, 0)) for v in sources],
            out_specs=pl.BlockSpec(out.shape, lambda j, blk: (0, 0, 0)),
        ),
        out_shape=out,
        compiler_params=pltpu.CompilerParams(vmem_limit_bytes=SMALL),
        cost_estimate=pl.CostEstimate(
            flops=0, bytes_accessed=4 * plane * width * shape[2], transcendentals=0
        ),
        name="pack",
    )(blk, *sources)


def forward_kernel(p_ref, t_ref, tgt_ref, stat_ref, s_all):
    for i in range(p_ref.shape[0]):
        s_ref = s_all.at[i]
        q = p_ref[i]
        items = t_ref.shape[1]
        width = q.shape[0]
        tgt = tgt_ref[i]
        high = jnp.full((8, width), -jnp.inf, F32)
        pick = jnp.zeros((8, width), F32)
        for start in range(0, items, TILE):
            rows = t_ref[i, pl.ds(start, TILE), :]
            s = lax.dot_general(rows, q, NT, preferred_element_type=F32)
            s_ref[pl.ds(start, TILE), :] = s
            high = jnp.maximum(high, jnp.max(s.reshape(TILE // 8, 8, width), axis=0))
            hit = jnp.where(tile_ids(start, s.shape) == tgt, s, 0.0)
            pick = pick + jnp.sum(hit.reshape(TILE // 8, 8, width), axis=0)
        top = jnp.max(high, axis=0, keepdims=True)
        mass = jnp.zeros((8, width), F32)
        for start in range(0, items, TILE):
            e = jnp.exp(s_ref[pl.ds(start, TILE), :] - top)
            mass = mass + jnp.sum(e.reshape(TILE // 8, 8, width), axis=0)
        stat_ref[0, i] = top + jnp.log(jnp.sum(mass, axis=0, keepdims=True))
        stat_ref[1, i] = jnp.sum(pick, axis=0, keepdims=True)


def forward(packed, targets, tables, per=2):
    planes, items, features = tables.shape
    width = packed.shape[1]
    return pl.pallas_call(
        forward_kernel,
        grid=(planes // per,),
        in_specs=[
            pl.BlockSpec((per, width, features), lambda j: (j, 0, 0)),
            pl.BlockSpec((per, items, features), lambda j: (j, 0, 0)),
            pl.BlockSpec((per, 1, width), lambda j: (j, 0, 0)),
        ],
        out_specs=pl.BlockSpec((2, per, 1, width), lambda j: (0, j, 0, 0)),
        out_shape=jax.ShapeDtypeStruct((2, planes, 1, width), F32),
        scratch_shapes=[pltpu.VMEM((per, items, width), F32)],
        compiler_params=pltpu.CompilerParams(vmem_limit_bytes=LARGE),
        cost_estimate=pl.CostEstimate(
            flops=40 * planes * width * items * features,
            bytes_accessed=planes * items * features * 2 + planes * width * features * 2,
            transcendentals=planes * width * items,
        ),
        name="forward",
    )(packed, tables, targets)


def query_kernel(blk, p_ref, t_ref, line_ref, g_ref, c_all, acc_ref):
    step = pl.program_id(0)
    sources, _, block_rows, _ = acc_ref.shape
    per = p_ref.shape[0]
    slots = sources * MOST

    @pl.when(step == 0)
    def _():
        acc_ref[...] = jnp.zeros_like(acc_ref)

    for i in range(per):
        q = p_ref[i]
        lse = line_ref[i, 0:1, :]
        tgt = line_ref[i, 1:2, :].astype(jnp.int32)
        for start in range(0, t_ref.shape[1], TILE):
            rows = t_ref[i, pl.ds(start, TILE), :]
            s = lax.dot_general(rows, q, NT, preferred_element_type=F32)
            e = jnp.exp(s - lse)
            c = jnp.where(tile_ids(start, s.shape) == tgt, e - 1.0, e)
            c_all[i, pl.ds(start, TILE), :] = c.astype(BF16)
        g = lax.dot_general(c_all[i], t_ref[i], TN, preferred_element_type=F32)
        for slot in range(slots):
            b = blk[(step * per + i) * slots + slot]
            acc_ref[slot // MOST, b] += g[slot * block_rows:(slot + 1) * block_rows, :]

    @pl.when(step == pl.num_programs(0) - 1)
    def _():
        z = blk[pl.num_programs(0) * per * slots]
        for i in range(sources):
            g_ref[lax.rem(z + i, sources)] = acc_ref[i].astype(BF16)


def query_parts(packed, blk, lines, tables, sources, blocks, block_rows, per=4):
    planes, items, features = tables.shape
    width = packed.shape[1]
    out = jax.ShapeDtypeStruct((sources, blocks, block_rows, features), BF16)
    return pl.pallas_call(
        query_kernel,
        grid_spec=pltpu.PrefetchScalarGridSpec(
            num_scalar_prefetch=1,
            grid=(planes // per,),
            in_specs=[
                pl.BlockSpec((per, width, features), lambda j, blk: (j, 0, 0)),
                pl.BlockSpec((per, items, features), lambda j, blk: (j, 0, 0)),
                pl.BlockSpec((per, 2, width), lambda j, blk: (j, 0, 0)),
            ],
            out_specs=pl.BlockSpec(out.shape, lambda j, blk: (0, 0, 0, 0)),
            scratch_shapes=[pltpu.VMEM((per, items, width), BF16), pltpu.VMEM(out.shape, F32)],
        ),
        out_shape=out,
        compiler_params=pltpu.CompilerParams(vmem_limit_bytes=LARGE),
        cost_estimate=pl.CostEstimate(flops=1 << 20, bytes_accessed=1 << 20, transcendentals=0),
        name="query_parts",
    )(blk, packed, tables, lines)


def item_kernel(where, q_ref, line_ref, t_ref, *outs):
    start = where[pl.program_id(0)] * t_ref.shape[0]
    total = None
    for source in range(q_ref.shape[0]):
        q = q_ref[source]
        line = line_ref[source]
        lse = line[0:1, :]
        tgt = line[1:2, :].astype(jnp.int32)
        s = lax.dot_general(t_ref[...], q, NT, preferred_element_type=F32)
        e = jnp.exp(s - lse)
        c = jnp.where(tile_ids(start, s.shape) == tgt, e - 1.0, e).astype(BF16)
        part = jnp.dot(c, q, preferred_element_type=F32)
        total = part if total is None else total + part
    pieces = t_ref.shape[0] // outs[0].shape[0]
    for place in range(len(outs) // pieces):

        @pl.when(pl.program_id(0) == place)
        def _():
            for n in range(pieces):
                out = outs[place * pieces + n]
                out[...] = total[n * out.shape[0]:(n + 1) * out.shape[0]]


def item_parts(places, pieces, x, rows, lines, table16, quarters):
    count, width, features = rows.shape
    span = table16.shape[0] // quarters
    share = len(places)
    out = jax.ShapeDtypeStruct((span // pieces, features), F32)
    return pl.pallas_call(
        item_kernel,
        grid_spec=pltpu.PrefetchScalarGridSpec(
            num_scalar_prefetch=1,
            grid=(share,),
            in_specs=[
                pl.BlockSpec(rows.shape, lambda i, o: (0, 0, 0)),
                pl.BlockSpec(lines.shape, lambda i, o: (0, 0, 0)),
                pl.BlockSpec((span, features), lambda i, o: (o[i], 0)),
            ],
            out_specs=[pl.BlockSpec(out.shape, lambda i, o: (0, 0))] * (share * pieces),
        ),
        out_shape=[out] * (share * pieces),
        compiler_params=pltpu.CompilerParams(vmem_limit_bytes=SMALL),
        cost_estimate=pl.CostEstimate(
            flops=4 * share * span * count * width * features,
            bytes_accessed=2 * count * width * features + share * span * features * 6,
            transcendentals=share * span * count * width,
        ),
        name="item_parts",
    )((jnp.array(places, jnp.int32) + x) % quarters, rows, lines, table16)


def update_kernel(x_ref, own, after, before, far_a, far_b, t_ref, a_ref, nt_ref, na_ref):
    quarters = pl.num_programs(0)
    rel = lax.rem(pl.program_id(0) - x_ref[0] + quarters, quarters)
    cut = far_a.shape[0]

    def write(start, summed):
        span = pl.ds(start, summed.shape[0])
        accum = a_ref[span, :] + summed * summed
        na_ref[span, :] = accum
        nt_ref[span, :] = t_ref[span, :] - 0.5 * summed / jnp.sqrt(accum)

    for place, ref in ((0, own), (1, after), (3, before)):

        @pl.when(rel == place)
        def _():
            write(0, ref[...])

    @pl.when(rel == 2)
    def _():
        write(0, far_a[...])
        write(cut, far_b[...])


def update(x, own, after, before, far_a, far_b, table, accum, quarters):
    items, features = table.shape
    whole = pl.BlockSpec(own.shape, lambda i, x: (0, 0))
    part = pl.BlockSpec(far_a.shape, lambda i, x: (0, 0))
    block = pl.BlockSpec((items // quarters, features), lambda i, x: (i, 0))
    return pl.pallas_call(
        update_kernel,
        grid_spec=pltpu.PrefetchScalarGridSpec(
            num_scalar_prefetch=1,
            grid=(quarters,),
            in_specs=[whole] * 3 + [part] * 2 + [block] * 2,
            out_specs=[block] * 2,
        ),
        out_shape=[jax.ShapeDtypeStruct(table.shape, F32)] * 2,
        compiler_params=pltpu.CompilerParams(vmem_limit_bytes=SMALL),
        name="update",
    )(x, own, after, before, far_a, far_b, table, accum)


def local(queries, clusters, positives, owner_of, table, accum):
    z_size = lax.axis_size("z")
    x_size = lax.axis_size("x")
    z = lax.axis_index("z")
    x = lax.axis_index("x").reshape(1)
    local_rows, features = queries.shape
    block_count, picks = clusters.shape
    block_rows = local_rows // block_count
    items = table.shape[1]
    owners = owner_of.shape[0]
    plane = owners // z_size
    pair_count = block_count * picks

    tables = lax.all_gather(table[0].astype(BF16), PLANE)

    flat_lists = clusters.reshape(pair_count)
    catalog_ids = jnp.arange(owners, dtype=jnp.int32)
    lookup = flat_lists[:, None] == catalog_ids[None, :]
    destination = jnp.sum(jnp.where(lookup, owner_of[None, :], 0), axis=1)
    pair_ids = jnp.arange(pair_count, dtype=jnp.int32)
    earlier = (destination[:, None] == destination[None, :]) & (
        pair_ids[:, None] > pair_ids[None, :]
    )
    rank_in = jnp.sum(earlier.astype(jnp.int32), axis=1)
    slot_of_pair = destination * MOST + rank_in
    digits = jnp.stack([positives // 64, positives % 64]).reshape(-1, features)
    extra = jnp.concatenate([digits, jnp.pad(slot_of_pair, (0, features - pair_count))[None]])
    digit_rows = digits.shape[0] // 2
    extra = jnp.pad(extra, ((0, block_rows - extra.shape[0]), (0, 0))).astype(BF16)
    half_rows = local_rows // 2
    halves = [queries[:half_rows], jnp.concatenate([queries[half_rows:], extra])]
    by_source = [[None] * 2 for _ in range(z_size)]
    for half in range(2):
        right = left = halves[half].reshape(-1, block_rows, features)
        by_source[0][half] = right
        for hop in range(1, z_size // 2 + 1):
            right = by_source[z_size - hop][half] = shift(right, "z", 1)
            if hop < z_size // 2:
                left = by_source[hop][half] = shift(left, "z", -1)

    carried = jnp.stack([pair[1][-1, :2 * digit_rows + 1] for pair in by_source])
    carried = carried.astype(F32).astype(jnp.int32)
    pair_slot = carried[:, 2 * digit_rows, :pair_count]
    chosen = carried[:, :digit_rows] * 64 + carried[:, digit_rows:2 * digit_rows]
    chosen = chosen.reshape(z_size * block_count, block_rows)
    order = jnp.arange(z_size, dtype=jnp.int32)
    width = z_size * MOST * block_rows
    wanted = (z * plane + jnp.arange(plane, dtype=jnp.int32)[:, None]) * MOST
    wanted = (wanted + jnp.arange(MOST, dtype=jnp.int32)[None, :]).reshape(plane, 1, MOST, 1)
    matches = pair_slot[None, :, None, :] == wanted
    pair = jnp.max(jnp.where(matches, pair_ids, -1), axis=3)
    named = jnp.where(pair < 0, -1, pair // picks)
    blk = jnp.maximum(named, 0)
    chosen = chosen[(blk + (order * block_count)[None, :, None]).reshape(-1)]
    start = (pair % picks * items).reshape(-1, 1)
    inside = (named.reshape(-1, 1) >= 0) & (chosen >= start) & (chosen < start + items)
    targets = jnp.where(inside, chosen - start, -1).reshape(plane, 1, width)
    named = named.reshape(-1)
    blk = blk.reshape(-1)

    pair_owner = pair_slot // MOST
    pair_from = (pair_owner // plane - z) % z_size
    pair_place = (order[:, None] - pair_from) % z_size
    pair_row = (pair_from % 2 * 4 + pair_from // 2) * plane + pair_owner % plane
    pair_row = (pair_row * z_size + pair_place) * MOST + pair_slot % MOST

    own_table, blk = lax.optimization_barrier((table[0], blk))
    own_table = own_table.astype(BF16)
    packed = pack([part for pair in by_source for part in pair], blk, plane)
    rows = lax.all_to_all(packed, PLANE, 0, 0, tiled=True)
    stats = forward(packed, targets, tables)

    even = jnp.stack([stats] + [shift(stats, "z", -e) for e in (2, 4, 6)])
    all_stats = jnp.stack([even, shift(even, "z", -1)]).reshape(z_size, 2, -1)
    part = all_stats[:, 0].reshape(-1, block_rows)[pair_row.reshape(-1)]
    part, rows, own_table = lax.optimization_barrier((part, rows, own_table))
    part = part.reshape(z_size, block_count, picks, block_rows)
    pick = all_stats[:, 1].reshape(-1, block_rows)[pair_row[0]]
    pick = pick.reshape(block_count, picks, block_rows)
    top = jnp.max(part, axis=2)
    lse = top + jnp.log(jnp.sum(jnp.exp(part - top[:, :, None]), axis=2))
    losses = (lse[0] - jnp.sum(pick, axis=1)).reshape(local_rows)
    lse_rows = lse.reshape(z_size * block_count, block_rows)
    first = jnp.arange(z_size, dtype=jnp.int32).reshape(1, z_size, 1) * block_count
    lse_at = (blk.reshape(plane, z_size, MOST) + first).reshape(-1)
    lse_slots = jnp.where(named[:, None] < 0, F32(EMPTY), lse_rows[lse_at])
    lines = jnp.concatenate(
        [lse_slots.reshape(plane, 1, width), targets.astype(F32)], axis=1
    )

    grads = query_parts(
        packed, jnp.concatenate([blk, z.reshape(1)]), lines, tables, z_size, block_count, block_rows
    )
    grads, lines = lax.optimization_barrier((grads, lines))
    query_grads = lax.psum_scatter(grads, "z").astype(F32).reshape(local_rows, features)
    got_lines = lax.all_to_all(lines, PLANE, 0, 0, tiled=True)

    far_a, far_b = item_parts((2,), 2, x, rows, got_lines, own_table, x_size)
    far_a, far_b, got_lines = lax.optimization_barrier((far_a, far_b, got_lines))
    own, after, before = item_parts((0, 1, 3), 1, x, rows, got_lines, own_table, x_size)
    half = far_a.shape[0]
    far_a = shift(far_a, "x", 1)
    far_b = shift(far_b, "x", -1)
    after = shift(jnp.concatenate([after[:half] + far_a, after[half:]]), "x", 1)
    before = shift(jnp.concatenate([before[:half], before[half:] + far_b]), "x", -1)
    own, losses = lax.optimization_barrier((own + after + before, losses))
    before = shift(own, "x", 1)
    after = shift(own, "x", -1)
    far_a = shift(before[:half], "x", 1)
    far_b = shift(after[half:], "x", -1)
    new_table, new_accum = update(
        x, own, after, before, far_a, far_b, table[0], accum[0], x_size
    )
    return (losses, query_grads, new_table[None], new_accum[None])


def solution(mesh):
    axes = ("z", "y", "c", "x")
    split = Mesh(mesh.devices.reshape(8, 4, 2, 4), axes)
    placed = (
        P(axes, None),
        P(axes, None),
        P(axes),
        P(),
        P(axes[:3], None, None),
        P(axes[:3], None, None),
    )
    return jax.shard_map(
        local,
        mesh=split,
        in_specs=placed,
        out_specs=(
            P(axes),
            P(axes, None),
            P(axes[:3], None, None),
            P(axes[:3], None, None),
        ),
        check_vma=False,
    )
```

```python
import functools

import jax
import jax.numpy as jnp
from jax import lax
from jax.experimental import pallas as pl
from jax.experimental.pallas import tpu as pltpu
from jax.sharding import Mesh, PartitionSpec as P

MOST = 2
EMPTY = 1e30
PLANE = ("y", "c")
F32 = jnp.float32
BF16 = jnp.bfloat16
NT = (((1,), (1,)), ((), ()))
TN = (((0,), (0,)), ((), ()))
TILE = 256
LARGE = 56 << 20
SMALL = 20 << 20


def shift(value, axis, step):
    size = lax.axis_size(axis)
    return lax.ppermute(value, axis, [(i, (i + step) % size) for i in range(size)])


def tile_ids(start, shape):
    return lax.broadcasted_iota(jnp.int32, shape, 0) + start


def pack_kernel(count, blk, *refs):
    sources, p_ref = refs[:2 * count], refs[2 * count]
    half, block_rows = sources[0].shape[:2]
    per_peer = count * MOST
    for j in range(p_ref.shape[0]):
        for slot in range(per_peer):
            b = blk[j * per_peer + slot]
            place = lax.rem(b, half)
            low = sources[slot // MOST * 2][place]
            high = sources[slot // MOST * 2 + 1][place]
            first = jnp.full(low.shape, b, jnp.int32) < half
            p_ref[j, pl.ds(slot * block_rows, block_rows), :] = jnp.where(first, low, high)


def pack(sources, blk, plane):
    shape = sources[0].shape
    count = len(sources) // 2
    width = count * MOST * shape[1]
    out = jax.ShapeDtypeStruct((plane, width, shape[2]), BF16)
    return pl.pallas_call(
        functools.partial(pack_kernel, count),
        grid_spec=pltpu.PrefetchScalarGridSpec(
            num_scalar_prefetch=1,
            grid=(1,),
            in_specs=[pl.BlockSpec(shape, lambda j, blk: (0, 0, 0))] * len(sources),
            out_specs=pl.BlockSpec(out.shape, lambda j, blk: (0, 0, 0)),
        ),
        out_shape=out,
        compiler_params=pltpu.CompilerParams(vmem_limit_bytes=SMALL),
        cost_estimate=pl.CostEstimate(
            flops=0, bytes_accessed=4 * plane * width * shape[2], transcendentals=0
        ),
        name="pack",
    )(blk, *sources)


def forward_kernel(p_ref, t_ref, tgt_ref, stat_ref, s_all):
    for i in range(p_ref.shape[0]):
        s_ref = s_all.at[i]
        q = p_ref[i]
        items = t_ref.shape[1]
        width = q.shape[0]
        tgt = tgt_ref[i]
        high = jnp.full((8, width), -jnp.inf, F32)
        pick = jnp.zeros((8, width), F32)
        for start in range(0, items, TILE):
            rows = t_ref[i, pl.ds(start, TILE), :]
            s = lax.dot_general(rows, q, NT, preferred_element_type=F32)
            s_ref[pl.ds(start, TILE), :] = s
            high = jnp.maximum(high, jnp.max(s.reshape(TILE // 8, 8, width), axis=0))
            hit = jnp.where(tile_ids(start, s.shape) == tgt, s, 0.0)
            pick = pick + jnp.sum(hit.reshape(TILE // 8, 8, width), axis=0)
        top = jnp.max(high, axis=0, keepdims=True)
        mass = jnp.zeros((8, width), F32)
        for start in range(0, items, TILE):
            e = jnp.exp(s_ref[pl.ds(start, TILE), :] - top)
            mass = mass + jnp.sum(e.reshape(TILE // 8, 8, width), axis=0)
        stat_ref[0, i] = top + jnp.log(jnp.sum(mass, axis=0, keepdims=True))
        stat_ref[1, i] = jnp.sum(pick, axis=0, keepdims=True)


def forward(packed, targets, tables, per=2):
    planes, items, features = tables.shape
    width = packed.shape[1]
    return pl.pallas_call(
        forward_kernel,
        grid=(planes // per,),
        in_specs=[
            pl.BlockSpec((per, width, features), lambda j: (j, 0, 0)),
            pl.BlockSpec((per, items, features), lambda j: (j, 0, 0)),
            pl.BlockSpec((per, 1, width), lambda j: (j, 0, 0)),
        ],
        out_specs=pl.BlockSpec((2, per, 1, width), lambda j: (0, j, 0, 0)),
        out_shape=jax.ShapeDtypeStruct((2, planes, 1, width), F32),
        scratch_shapes=[pltpu.VMEM((per, items, width), F32)],
        compiler_params=pltpu.CompilerParams(vmem_limit_bytes=LARGE),
        cost_estimate=pl.CostEstimate(
            flops=40 * planes * width * items * features,
            bytes_accessed=planes * items * features * 2 + planes * width * features * 2,
            transcendentals=planes * width * items,
        ),
        name="forward",
    )(packed, tables, targets)


def query_kernel(blk, p_ref, t_ref, line_ref, g_ref, c_all, acc_ref):
    step = pl.program_id(0)
    sources, _, block_rows, _ = acc_ref.shape
    per = p_ref.shape[0]
    slots = sources * MOST

    @pl.when(step == 0)
    def _():
        acc_ref[...] = jnp.zeros_like(acc_ref)

    for i in range(per):
        q = p_ref[i]
        lse = line_ref[i, 0:1, :]
        tgt = line_ref[i, 1:2, :].astype(jnp.int32)
        for start in range(0, t_ref.shape[1], TILE):
            rows = t_ref[i, pl.ds(start, TILE), :]
            s = lax.dot_general(rows, q, NT, preferred_element_type=F32)
            e = jnp.exp(s - lse)
            c = jnp.where(tile_ids(start, s.shape) == tgt, e - 1.0, e)
            c_all[i, pl.ds(start, TILE), :] = c.astype(BF16)
        g = lax.dot_general(c_all[i], t_ref[i], TN, preferred_element_type=F32)
        for slot in range(slots):
            b = blk[(step * per + i) * slots + slot]
            acc_ref[slot // MOST, b] += g[slot * block_rows:(slot + 1) * block_rows, :]

    @pl.when(step == pl.num_programs(0) - 1)
    def _():
        z = blk[pl.num_programs(0) * per * slots]
        for i in range(sources):
            g_ref[lax.rem(z + i, sources)] = acc_ref[i].astype(BF16)


def query_parts(packed, blk, lines, tables, sources, blocks, block_rows, per=4):
    planes, items, features = tables.shape
    width = packed.shape[1]
    out = jax.ShapeDtypeStruct((sources, blocks, block_rows, features), BF16)
    return pl.pallas_call(
        query_kernel,
        grid_spec=pltpu.PrefetchScalarGridSpec(
            num_scalar_prefetch=1,
            grid=(planes // per,),
            in_specs=[
                pl.BlockSpec((per, width, features), lambda j, blk: (j, 0, 0)),
                pl.BlockSpec((per, items, features), lambda j, blk: (j, 0, 0)),
                pl.BlockSpec((per, 2, width), lambda j, blk: (j, 0, 0)),
            ],
            out_specs=pl.BlockSpec(out.shape, lambda j, blk: (0, 0, 0, 0)),
            scratch_shapes=[pltpu.VMEM((per, items, width), BF16), pltpu.VMEM(out.shape, F32)],
        ),
        out_shape=out,
        compiler_params=pltpu.CompilerParams(vmem_limit_bytes=LARGE),
        cost_estimate=pl.CostEstimate(flops=1 << 20, bytes_accessed=1 << 20, transcendentals=0),
        name="query_parts",
    )(blk, packed, tables, lines)


def item_kernel(where, q_ref, line_ref, t_ref, *outs):
    start = where[pl.program_id(0)] * t_ref.shape[0]
    table16 = t_ref[...].astype(BF16)
    total = None
    for source in range(q_ref.shape[0]):
        q = q_ref[source]
        line = line_ref[source]
        lse = line[0:1, :]
        tgt = line[1:2, :].astype(jnp.int32)
        s = lax.dot_general(table16, q, NT, preferred_element_type=F32)
        e = jnp.exp(s - lse)
        c = jnp.where(tile_ids(start, s.shape) == tgt, e - 1.0, e).astype(BF16)
        part = jnp.dot(c, q, preferred_element_type=F32)
        total = part if total is None else total + part
    pieces = t_ref.shape[0] // outs[0].shape[0]
    for place in range(len(outs) // pieces):

        @pl.when(pl.program_id(0) == place)
        def _():
            for n in range(pieces):
                out = outs[place * pieces + n]
                out[...] = total[n * out.shape[0]:(n + 1) * out.shape[0]]


def item_parts(places, pieces, x, rows, lines, table, quarters):
    count, width, features = rows.shape
    span = table.shape[0] // quarters
    share = len(places)
    out = jax.ShapeDtypeStruct((span // pieces, features), F32)
    return pl.pallas_call(
        item_kernel,
        grid_spec=pltpu.PrefetchScalarGridSpec(
            num_scalar_prefetch=1,
            grid=(share,),
            in_specs=[
                pl.BlockSpec(rows.shape, lambda i, o: (0, 0, 0)),
                pl.BlockSpec(lines.shape, lambda i, o: (0, 0, 0)),
                pl.BlockSpec((span, features), lambda i, o: (o[i], 0)),
            ],
            out_specs=[pl.BlockSpec(out.shape, lambda i, o: (0, 0))] * (share * pieces),
        ),
        out_shape=[out] * (share * pieces),
        compiler_params=pltpu.CompilerParams(vmem_limit_bytes=SMALL),
        cost_estimate=pl.CostEstimate(
            flops=4 * share * span * count * width * features,
            bytes_accessed=2 * count * width * features + share * span * features * 6,
            transcendentals=share * span * count * width,
        ),
        name="item_parts",
    )((jnp.array(places, jnp.int32) + x) % quarters, rows, lines, table)


def update_kernel(x_ref, own, after, before, far_a, far_b, t_ref, a_ref, nt_ref, na_ref):
    quarters = pl.num_programs(0)
    rel = lax.rem(pl.program_id(0) - x_ref[0] + quarters, quarters)
    cut = far_a.shape[0]

    def write(start, summed):
        span = pl.ds(start, summed.shape[0])
        accum = a_ref[span, :] + summed * summed
        na_ref[span, :] = accum
        nt_ref[span, :] = t_ref[span, :] - 0.5 * summed / jnp.sqrt(accum)

    for place, ref in ((0, own), (1, after), (3, before)):

        @pl.when(rel == place)
        def _():
            write(0, ref[...])

    @pl.when(rel == 2)
    def _():
        write(0, far_a[...])
        write(cut, far_b[...])


def update(x, own, after, before, far_a, far_b, table, accum, quarters):
    items, features = table.shape
    whole = pl.BlockSpec(own.shape, lambda i, x: (0, 0))
    part = pl.BlockSpec(far_a.shape, lambda i, x: (0, 0))
    block = pl.BlockSpec((items // quarters, features), lambda i, x: (i, 0))
    return pl.pallas_call(
        update_kernel,
        grid_spec=pltpu.PrefetchScalarGridSpec(
            num_scalar_prefetch=1,
            grid=(quarters,),
            in_specs=[whole] * 3 + [part] * 2 + [block] * 2,
            out_specs=[block] * 2,
        ),
        out_shape=[jax.ShapeDtypeStruct(table.shape, F32)] * 2,
        compiler_params=pltpu.CompilerParams(vmem_limit_bytes=SMALL),
        name="update",
    )(x, own, after, before, far_a, far_b, table, accum)


def local(queries, clusters, positives, owner_of, table, accum):
    z_size = lax.axis_size("z")
    x_size = lax.axis_size("x")
    z = lax.axis_index("z")
    x = lax.axis_index("x").reshape(1)
    local_rows, features = queries.shape
    block_count, picks = clusters.shape
    block_rows = local_rows // block_count
    items = table.shape[1]
    owners = owner_of.shape[0]
    plane = owners // z_size
    pair_count = block_count * picks

    tables = lax.all_gather(table[0].astype(BF16), PLANE)

    here = queries.reshape(2, block_count // 2, block_rows, features)
    by_source = [[None] * 2 for _ in range(z_size)]
    for half in range(2):
        right = left = by_source[0][half] = here[half]
        for hop in range(1, z_size // 2 + 1):
            right = by_source[z_size - hop][half] = shift(right, "z", 1)
            if hop < z_size // 2:
                left = by_source[hop][half] = shift(left, "z", -1)

    flat_lists = clusters.reshape(pair_count)
    catalog_ids = jnp.arange(owners, dtype=jnp.int32)
    lookup = flat_lists[:, None] == catalog_ids[None, :]
    destination = jnp.sum(jnp.where(lookup, owner_of[None, :], 0), axis=1)
    pair_ids = jnp.arange(pair_count, dtype=jnp.int32)
    earlier = (destination[:, None] == destination[None, :]) & (
        pair_ids[:, None] > pair_ids[None, :]
    )
    rank_in = jnp.sum(earlier.astype(jnp.int32), axis=1)
    slot_of_pair = destination * MOST + rank_in
    slot_count = owners * MOST
    matches = slot_of_pair[None, :] == jnp.arange(slot_count, dtype=jnp.int32)[:, None]
    filled = jnp.any(matches, axis=1)
    source_pair = jnp.sum(jnp.where(matches, pair_ids[None, :], 0), axis=1)
    which_block = source_pair // picks
    which_pick = source_pair % picks
    chosen = positives.reshape(block_count, block_rows)[which_block]
    inside = filled[:, None] & (chosen // items == which_pick[:, None])
    send_targets = jnp.where(inside, chosen - which_pick[:, None] * items, -1)
    block_or_none = jnp.where(filled, which_block, -1)
    per_plane = plane * MOST
    meta = jnp.concatenate(
        [
            send_targets.reshape(z_size, per_plane * block_rows),
            block_or_none.reshape(z_size, per_plane),
            jnp.broadcast_to(slot_of_pair[None, :], (z_size, pair_count)),
        ],
        axis=1,
    )
    meta, _ = lax.optimization_barrier((meta, by_source[5][0]))
    got = lax.all_to_all(meta, "z", 0, 0, tiled=True)
    order = jnp.arange(z_size, dtype=jnp.int32)
    got = got[(z + order) % z_size]
    width = z_size * MOST * block_rows
    cut = per_plane * block_rows
    targets = got[:, :cut].reshape(z_size, plane, MOST, block_rows)
    targets = targets.transpose(1, 0, 2, 3).reshape(plane, 1, width)
    named = got[:, cut:cut + per_plane].reshape(z_size, plane, MOST).transpose(1, 0, 2)
    named = named.reshape(plane * per_plane)
    blk = jnp.maximum(named, 0)

    pair_slot = got[:, cut + per_plane:]
    pair_owner = pair_slot // MOST
    pair_from = (pair_owner // plane - z) % z_size
    pair_place = (order[:, None] - pair_from) % z_size
    pair_row = (pair_from % 2 * 4 + pair_from // 2) * plane + pair_owner % plane
    pair_row = (pair_row * z_size + pair_place) * MOST + pair_slot % MOST

    packed = pack([part for pair in by_source for part in pair], blk, plane)
    rows = lax.all_to_all(packed, PLANE, 0, 0, tiled=True)
    stats = forward(packed, targets, tables)

    even = jnp.stack([stats] + [shift(stats, "z", -e) for e in (2, 4, 6)])
    all_stats = jnp.stack([even, shift(even, "z", -1)]).reshape(z_size, 2, -1)
    part = all_stats[:, 0].reshape(-1, block_rows)[pair_row.reshape(-1)]
    part, rows = lax.optimization_barrier((part, rows))
    part = part.reshape(z_size, block_count, picks, block_rows)
    pick = all_stats[:, 1].reshape(-1, block_rows)[pair_row[0]]
    pick = pick.reshape(block_count, picks, block_rows)
    top = jnp.max(part, axis=2)
    lse = top + jnp.log(jnp.sum(jnp.exp(part - top[:, :, None]), axis=2))
    losses = (lse[0] - jnp.sum(pick, axis=1)).reshape(local_rows)
    lse_rows = lse.reshape(z_size * block_count, block_rows)
    first = jnp.arange(z_size, dtype=jnp.int32).reshape(1, z_size, 1) * block_count
    lse_at = (blk.reshape(plane, z_size, MOST) + first).reshape(-1)
    lse_slots = jnp.where(named[:, None] < 0, F32(EMPTY), lse_rows[lse_at])
    lines = jnp.concatenate(
        [lse_slots.reshape(plane, 1, width), targets.astype(F32)], axis=1
    )

    grads = query_parts(
        packed, jnp.concatenate([blk, z.reshape(1)]), lines, tables, z_size, block_count, block_rows
    )
    grads, lines = lax.optimization_barrier((grads, lines))
    query_grads = lax.psum_scatter(grads, "z").astype(F32).reshape(local_rows, features)
    got_lines = lax.all_to_all(lines, PLANE, 0, 0, tiled=True)

    far_a, far_b = item_parts((2,), 2, x, rows, got_lines, table[0], x_size)
    far_a, far_b, got_lines = lax.optimization_barrier((far_a, far_b, got_lines))
    after, before = item_parts((1, 3), 1, x, rows, got_lines, table[0], x_size)
    after, before, got_lines = lax.optimization_barrier((after, before, got_lines))
    (own,) = item_parts((0,), 1, x, rows, got_lines, table[0], x_size)
    half = far_a.shape[0]
    far_a = shift(far_a, "x", 1)
    far_b = shift(far_b, "x", -1)
    after = shift(jnp.concatenate([after[:half] + far_a, after[half:]]), "x", 1)
    before = shift(jnp.concatenate([before[:half], before[half:] + far_b]), "x", -1)
    own, losses = lax.optimization_barrier((own + after + before, losses))
    before = shift(own, "x", 1)
    after = shift(own, "x", -1)
    far_a = shift(before[:half], "x", 1)
    far_b = shift(after[half:], "x", -1)
    new_table, new_accum = update(
        x, own, after, before, far_a, far_b, table[0], accum[0], x_size
    )
    return (losses, query_grads, new_table[None], new_accum[None])


def solution(mesh):
    axes = ("z", "y", "c", "x")
    split = Mesh(mesh.devices.reshape(8, 4, 2, 4), axes)
    placed = (
        P(axes, None),
        P(axes, None),
        P(axes),
        P(),
        P(axes[:3], None, None),
        P(axes[:3], None, None),
    )
    return jax.shard_map(
        local,
        mesh=split,
        in_specs=placed,
        out_specs=(
            P(axes),
            P(axes, None),
            P(axes[:3], None, None),
            P(axes[:3], None, None),
        ),
        check_vma=False,
    )
```

```python
import functools

import jax
import jax.numpy as jnp
from jax import lax
from jax.experimental import pallas as pl
from jax.experimental.pallas import tpu as pltpu
from jax.sharding import Mesh, PartitionSpec as P

MOST = 2
EMPTY = 1e30
PLANE = ("y", "c")
F32 = jnp.float32
BF16 = jnp.bfloat16
NT = (((1,), (1,)), ((), ()))
TN = (((0,), (0,)), ((), ()))
TILE = 256
LARGE = 56 << 20
SMALL = 20 << 20


def shift(value, axis, step):
    size = lax.axis_size(axis)
    return lax.ppermute(value, axis, [(i, (i + step) % size) for i in range(size)])


def tile_ids(start, shape):
    return lax.broadcasted_iota(jnp.int32, shape, 0) + start


def pack_kernel(count, blk, *refs):
    sources, p_ref = refs[:2 * count], refs[2 * count]
    half, block_rows = sources[0].shape[:2]
    per_peer = count * MOST
    for i in range(p_ref.shape[0]):
        j = pl.program_id(0) * p_ref.shape[0] + i
        for slot in range(per_peer):
            b = blk[j * per_peer + slot]
            place = lax.rem(b, half)
            low = sources[slot // MOST * 2][place]
            high = sources[slot // MOST * 2 + 1][place]
            first = jnp.full(low.shape, b, jnp.int32) < half
            p_ref[i, pl.ds(slot * block_rows, block_rows), :] = jnp.where(first, low, high)


def pack(sources, blk, plane, per=4):
    shape = sources[0].shape
    count = len(sources) // 2
    width = count * MOST * shape[1]
    out = jax.ShapeDtypeStruct((plane, width, shape[2]), BF16)
    return pl.pallas_call(
        functools.partial(pack_kernel, count),
        grid_spec=pltpu.PrefetchScalarGridSpec(
            num_scalar_prefetch=1,
            grid=(plane // per,),
            in_specs=[pl.BlockSpec(shape, lambda j, blk: (0, 0, 0))] * len(sources),
            out_specs=pl.BlockSpec((per,) + out.shape[1:], lambda j, blk: (j, 0, 0)),
        ),
        out_shape=out,
        compiler_params=pltpu.CompilerParams(vmem_limit_bytes=SMALL),
        cost_estimate=pl.CostEstimate(
            flops=0, bytes_accessed=4 * plane * width * shape[2], transcendentals=0
        ),
        name="pack",
    )(blk, *sources)


def forward_kernel(p_ref, t_ref, tgt_ref, stat_ref, s_all):
    for i in range(p_ref.shape[0]):
        s_ref = s_all.at[i]
        q = p_ref[i]
        items = t_ref.shape[1]
        width = q.shape[0]
        tgt = tgt_ref[i]
        high = jnp.full((8, width), -jnp.inf, F32)
        pick = jnp.zeros((8, width), F32)
        for start in range(0, items, TILE):
            rows = t_ref[i, pl.ds(start, TILE), :]
            s = lax.dot_general(rows, q, NT, preferred_element_type=F32)
            s_ref[pl.ds(start, TILE), :] = s
            high = jnp.maximum(high, jnp.max(s.reshape(TILE // 8, 8, width), axis=0))
            hit = jnp.where(tile_ids(start, s.shape) == tgt, s, 0.0)
            pick = pick + jnp.sum(hit.reshape(TILE // 8, 8, width), axis=0)
        top = jnp.max(high, axis=0, keepdims=True)
        mass = jnp.zeros((8, width), F32)
        for start in range(0, items, TILE):
            e = jnp.exp(s_ref[pl.ds(start, TILE), :] - top)
            mass = mass + jnp.sum(e.reshape(TILE // 8, 8, width), axis=0)
        stat_ref[0, i] = top + jnp.log(jnp.sum(mass, axis=0, keepdims=True))
        stat_ref[1, i] = jnp.sum(pick, axis=0, keepdims=True)


def forward(packed, targets, tables, per=2):
    planes, items, features = tables.shape
    width = packed.shape[1]
    return pl.pallas_call(
        forward_kernel,
        grid=(planes // per,),
        in_specs=[
            pl.BlockSpec((per, width, features), lambda j: (j, 0, 0)),
            pl.BlockSpec((per, items, features), lambda j: (j, 0, 0)),
            pl.BlockSpec((per, 1, width), lambda j: (j, 0, 0)),
        ],
        out_specs=pl.BlockSpec((2, per, 1, width), lambda j: (0, j, 0, 0)),
        out_shape=jax.ShapeDtypeStruct((2, planes, 1, width), F32),
        scratch_shapes=[pltpu.VMEM((per, items, width), F32)],
        compiler_params=pltpu.CompilerParams(vmem_limit_bytes=LARGE),
        cost_estimate=pl.CostEstimate(
            flops=40 * planes * width * items * features,
            bytes_accessed=planes * items * features * 2 + planes * width * features * 2,
            transcendentals=planes * width * items,
        ),
        name="forward",
    )(packed, tables, targets)


def query_kernel(blk, p_ref, t_ref, line_ref, g_ref, c_all, acc_ref):
    step = pl.program_id(0)
    sources, _, block_rows, _ = acc_ref.shape
    per = p_ref.shape[0]
    slots = sources * MOST

    @pl.when(step == 0)
    def _():
        acc_ref[...] = jnp.zeros_like(acc_ref)

    for i in range(per):
        q = p_ref[i]
        lse = line_ref[i, 0:1, :]
        tgt = line_ref[i, 1:2, :].astype(jnp.int32)
        for start in range(0, t_ref.shape[1], TILE):
            rows = t_ref[i, pl.ds(start, TILE), :]
            s = lax.dot_general(rows, q, NT, preferred_element_type=F32)
            e = jnp.exp(s - lse)
            c = jnp.where(tile_ids(start, s.shape) == tgt, e - 1.0, e)
            c_all[i, pl.ds(start, TILE), :] = c.astype(BF16)
        g = lax.dot_general(c_all[i], t_ref[i], TN, preferred_element_type=F32)
        for slot in range(slots):
            b = blk[(step * per + i) * slots + slot]
            acc_ref[slot // MOST, b] += g[slot * block_rows:(slot + 1) * block_rows, :]

    @pl.when(step == pl.num_programs(0) - 1)
    def _():
        z = blk[pl.num_programs(0) * per * slots]
        for i in range(sources):
            g_ref[lax.rem(z + i, sources)] = acc_ref[i].astype(BF16)


def query_parts(packed, blk, lines, tables, sources, blocks, block_rows, per=4):
    planes, items, features = tables.shape
    width = packed.shape[1]
    out = jax.ShapeDtypeStruct((sources, blocks, block_rows, features), BF16)
    return pl.pallas_call(
        query_kernel,
        grid_spec=pltpu.PrefetchScalarGridSpec(
            num_scalar_prefetch=1,
            grid=(planes // per,),
            in_specs=[
                pl.BlockSpec((per, width, features), lambda j, blk: (j, 0, 0)),
                pl.BlockSpec((per, items, features), lambda j, blk: (j, 0, 0)),
                pl.BlockSpec((per, 2, width), lambda j, blk: (j, 0, 0)),
            ],
            out_specs=pl.BlockSpec(out.shape, lambda j, blk: (0, 0, 0, 0)),
            scratch_shapes=[pltpu.VMEM((per, items, width), BF16), pltpu.VMEM(out.shape, F32)],
        ),
        out_shape=out,
        compiler_params=pltpu.CompilerParams(vmem_limit_bytes=LARGE),
        cost_estimate=pl.CostEstimate(flops=1 << 20, bytes_accessed=1 << 20, transcendentals=0),
        name="query_parts",
    )(blk, packed, tables, lines)


def item_kernel(where, q_ref, line_ref, t_ref, *outs):
    start = where[pl.program_id(0)] * t_ref.shape[0]
    table16 = t_ref[...].astype(BF16)
    total = None
    for source in range(q_ref.shape[0]):
        q = q_ref[source]
        line = line_ref[source]
        lse = line[0:1, :]
        tgt = line[1:2, :].astype(jnp.int32)
        s = lax.dot_general(table16, q, NT, preferred_element_type=F32)
        e = jnp.exp(s - lse)
        c = jnp.where(tile_ids(start, s.shape) == tgt, e - 1.0, e).astype(BF16)
        part = jnp.dot(c, q, preferred_element_type=F32)
        total = part if total is None else total + part
    pieces = t_ref.shape[0] // outs[0].shape[0]
    for place in range(len(outs) // pieces):

        @pl.when(pl.program_id(0) == place)
        def _():
            for n in range(pieces):
                out = outs[place * pieces + n]
                out[...] = total[n * out.shape[0]:(n + 1) * out.shape[0]]


def item_parts(places, pieces, x, rows, lines, table, quarters):
    count, width, features = rows.shape
    span = table.shape[0] // quarters
    share = len(places)
    out = jax.ShapeDtypeStruct((span // pieces, features), F32)
    return pl.pallas_call(
        item_kernel,
        grid_spec=pltpu.PrefetchScalarGridSpec(
            num_scalar_prefetch=1,
            grid=(share,),
            in_specs=[
                pl.BlockSpec(rows.shape, lambda i, o: (0, 0, 0)),
                pl.BlockSpec(lines.shape, lambda i, o: (0, 0, 0)),
                pl.BlockSpec((span, features), lambda i, o: (o[i], 0)),
            ],
            out_specs=[pl.BlockSpec(out.shape, lambda i, o: (0, 0))] * (share * pieces),
        ),
        out_shape=[out] * (share * pieces),
        compiler_params=pltpu.CompilerParams(vmem_limit_bytes=SMALL),
        cost_estimate=pl.CostEstimate(
            flops=4 * share * span * count * width * features,
            bytes_accessed=2 * count * width * features + share * span * features * 6,
            transcendentals=share * span * count * width,
        ),
        name="item_parts",
    )((jnp.array(places, jnp.int32) + x) % quarters, rows, lines, table)


def write_rows(summed, start, t_ref, a_ref, nt_ref, na_ref):
    span = pl.ds(start, summed.shape[0])
    accum = a_ref[span, :] + summed * summed
    na_ref[span, :] = accum
    nt_ref[span, :] = t_ref[span, :] - 0.5 * summed / jnp.sqrt(accum)


def update_kernel(where, own, after, before, t_ref, a_ref, nt_ref, na_ref):
    for place, ref in enumerate((own, after, before)):

        @pl.when(pl.program_id(0) == place)
        def _():
            write_rows(ref[...], 0, t_ref, a_ref, nt_ref, na_ref)


def far_kernel(where, far_a, far_b, t_ref, a_ref, nt_in, na_in, nt_ref, na_ref):
    write_rows(far_a[...], 0, t_ref, a_ref, nt_ref, na_ref)
    write_rows(far_b[...], far_a.shape[0], t_ref, a_ref, nt_ref, na_ref)


def update(body, places, x, sums, table, accum, quarters, held=()):
    items, features = table.shape
    sizes = [pl.BlockSpec(v.shape, lambda i, o: (0, 0)) for v in sums]
    block = pl.BlockSpec((items // quarters, features), lambda i, o: (o[i], 0))
    first = 3 + len(sums)
    return pl.pallas_call(
        body,
        grid_spec=pltpu.PrefetchScalarGridSpec(
            num_scalar_prefetch=1,
            grid=(len(places),),
            in_specs=sizes + [block] * 2 + [pl.BlockSpec(memory_space=pl.ANY)] * len(held),
            out_specs=[block] * 2,
        ),
        out_shape=[jax.ShapeDtypeStruct(table.shape, F32)] * 2,
        input_output_aliases={first + i: i for i in range(len(held))},
        compiler_params=pltpu.CompilerParams(vmem_limit_bytes=SMALL),
        name="update",
    )((jnp.array(places, jnp.int32) + x) % quarters, *sums, table, accum, *held)


def cast_kernel(g_ref, out_ref):
    out_ref[...] = g_ref[...].astype(F32)


def cast_rows(grads, steps=2):
    rows, features = grads.shape
    block = pl.BlockSpec((rows // steps, features), lambda i: (i, 0))
    return pl.pallas_call(
        cast_kernel,
        grid=(steps,),
        in_specs=[block],
        out_specs=block,
        out_shape=jax.ShapeDtypeStruct(grads.shape, F32),
        compiler_params=pltpu.CompilerParams(vmem_limit_bytes=LARGE),
        name="cast_rows",
    )(grads)


def local(queries, clusters, positives, owner_of, table, accum):
    z_size = lax.axis_size("z")
    x_size = lax.axis_size("x")
    z = lax.axis_index("z")
    x = lax.axis_index("x").reshape(1)
    local_rows, features = queries.shape
    block_count, picks = clusters.shape
    block_rows = local_rows // block_count
    items = table.shape[1]
    owners = owner_of.shape[0]
    plane = owners // z_size
    pair_count = block_count * picks

    tables = lax.all_gather(table[0].astype(BF16), PLANE)

    here = queries.reshape(2, block_count // 2, block_rows, features)
    by_source = [[None] * 2 for _ in range(z_size)]
    for half in range(2):
        right = left = by_source[0][half] = here[half]
        for hop in range(1, z_size // 2 + 1):
            right = by_source[z_size - hop][half] = shift(right, "z", 1)
            if hop < z_size // 2:
                left = by_source[hop][half] = shift(left, "z", -1)

    flat_lists = clusters.reshape(pair_count)
    catalog_ids = jnp.arange(owners, dtype=jnp.int32)
    lookup = flat_lists[:, None] == catalog_ids[None, :]
    destination = jnp.sum(jnp.where(lookup, owner_of[None, :], 0), axis=1)
    pair_ids = jnp.arange(pair_count, dtype=jnp.int32)
    earlier = (destination[:, None] == destination[None, :]) & (
        pair_ids[:, None] > pair_ids[None, :]
    )
    rank_in = jnp.sum(earlier.astype(jnp.int32), axis=1)
    slot_of_pair = destination * MOST + rank_in
    slot_count = owners * MOST
    matches = slot_of_pair[None, :] == jnp.arange(slot_count, dtype=jnp.int32)[:, None]
    filled = jnp.any(matches, axis=1)
    source_pair = jnp.sum(jnp.where(matches, pair_ids[None, :], 0), axis=1)
    which_block = source_pair // picks
    which_pick = source_pair % picks
    chosen = positives.reshape(block_count, block_rows)[which_block]
    inside = filled[:, None] & (chosen // items == which_pick[:, None])
    send_targets = jnp.where(inside, chosen - which_pick[:, None] * items, -1)
    block_or_none = jnp.where(filled, which_block, -1)
    per_plane = plane * MOST
    meta = jnp.concatenate(
        [
            send_targets.reshape(z_size, per_plane * block_rows),
            block_or_none.reshape(z_size, per_plane),
            jnp.broadcast_to(slot_of_pair[None, :], (z_size, pair_count)),
        ],
        axis=1,
    )
    meta, _ = lax.optimization_barrier((meta, by_source[5][0]))
    got = lax.all_to_all(meta, "z", 0, 0, tiled=True)
    order = jnp.arange(z_size, dtype=jnp.int32)
    got = got[(z + order) % z_size]
    width = z_size * MOST * block_rows
    cut = per_plane * block_rows
    targets = got[:, :cut].reshape(z_size, plane, MOST, block_rows)
    targets = targets.transpose(1, 0, 2, 3).reshape(plane, 1, width)
    named = got[:, cut:cut + per_plane].reshape(z_size, plane, MOST).transpose(1, 0, 2)
    named = named.reshape(plane * per_plane)
    blk = jnp.maximum(named, 0)

    pair_slot = got[:, cut + per_plane:]
    pair_owner = pair_slot // MOST
    pair_from = (pair_owner // plane - z) % z_size
    pair_place = (order[:, None] - pair_from) % z_size
    pair_row = (pair_from % 2 * 4 + pair_from // 2) * plane + pair_owner % plane
    pair_row = (pair_row * z_size + pair_place) * MOST + pair_slot % MOST

    packed = pack([part for pair in by_source for part in pair], blk, plane)
    rows = lax.all_to_all(packed, PLANE, 0, 0, tiled=True)
    stats = forward(packed, targets, tables)

    even = jnp.stack([stats] + [shift(stats, "z", -e) for e in (2, 4, 6)])
    all_stats = jnp.stack([even, shift(even, "z", -1)]).reshape(z_size, 2, -1)
    part = all_stats[:, 0].reshape(-1, block_rows)[pair_row.reshape(-1)]
    part, rows = lax.optimization_barrier((part, rows))
    part = part.reshape(z_size, block_count, picks, block_rows)
    pick = all_stats[:, 1].reshape(-1, block_rows)[pair_row[0]]
    pick = pick.reshape(block_count, picks, block_rows)
    top = jnp.max(part, axis=2)
    lse = top + jnp.log(jnp.sum(jnp.exp(part - top[:, :, None]), axis=2))
    losses = (lse[0] - jnp.sum(pick, axis=1)).reshape(local_rows)
    lse_rows = lse.reshape(z_size * block_count, block_rows)
    first = jnp.arange(z_size, dtype=jnp.int32).reshape(1, z_size, 1) * block_count
    lse_at = (blk.reshape(plane, z_size, MOST) + first).reshape(-1)
    lse_slots = jnp.where(named[:, None] < 0, F32(EMPTY), lse_rows[lse_at])
    lines = jnp.concatenate(
        [lse_slots.reshape(plane, 1, width), targets.astype(F32)], axis=1
    )

    grads = query_parts(
        packed, jnp.concatenate([blk, z.reshape(1)]), lines, tables, z_size, block_count, block_rows
    )
    grads, lines = lax.optimization_barrier((grads, lines))
    query_grads = cast_rows(lax.psum_scatter(grads, "z").reshape(local_rows, features))
    got_lines = lax.all_to_all(lines, PLANE, 0, 0, tiled=True)

    far_a, far_b = item_parts((2,), 2, x, rows, got_lines, table[0], x_size)
    far_a, far_b, got_lines = lax.optimization_barrier((far_a, far_b, got_lines))
    after, before = item_parts((1, 3), 1, x, rows, got_lines, table[0], x_size)
    after, before, got_lines = lax.optimization_barrier((after, before, got_lines))
    (own,) = item_parts((0,), 1, x, rows, got_lines, table[0], x_size)
    half = far_a.shape[0]
    far_a = shift(far_a, "x", 1)
    far_b = shift(far_b, "x", -1)
    after = shift(jnp.concatenate([after[:half] + far_a, after[half:]]), "x", 1)
    before = shift(jnp.concatenate([before[:half], before[half:] + far_b]), "x", -1)
    own, losses = lax.optimization_barrier((own + after + before, losses))
    before = shift(own, "x", 1)
    after = shift(own, "x", -1)
    far_a = shift(before[:half], "x", 1)
    far_b = shift(after[half:], "x", -1)
    held = update(update_kernel, (0, 1, 3), x, (own, after, before), table[0], accum[0], x_size)
    new_table, new_accum = update(
        far_kernel, (2,), x, (far_a, far_b), table[0], accum[0], x_size, held
    )
    return (losses, query_grads, new_table[None], new_accum[None])


def solution(mesh):
    axes = ("z", "y", "c", "x")
    split = Mesh(mesh.devices.reshape(8, 4, 2, 4), axes)
    placed = (
        P(axes, None),
        P(axes, None),
        P(axes),
        P(),
        P(axes[:3], None, None),
        P(axes[:3], None, None),
    )
    return jax.shard_map(
        local,
        mesh=split,
        in_specs=placed,
        out_specs=(
            P(axes),
            P(axes, None),
            P(axes[:3], None, None),
            P(axes[:3], None, None),
        ),
        check_vma=False,
    )
```

```python
import functools

import jax
import jax.numpy as jnp
from jax import lax
from jax.experimental import pallas as pl
from jax.experimental.pallas import tpu as pltpu
from jax.sharding import Mesh, PartitionSpec as P

MOST = 2
EMPTY = 1e30
PLANE = ("y", "c")
F32 = jnp.float32
BF16 = jnp.bfloat16
NT = (((1,), (1,)), ((), ()))
TN = (((0,), (0,)), ((), ()))
TILE = 256
LARGE = 56 << 20
SMALL = 20 << 20


def shift(value, axis, step):
    size = lax.axis_size(axis)
    return lax.ppermute(value, axis, [(i, (i + step) % size) for i in range(size)])


def tile_ids(start, shape):
    return lax.broadcasted_iota(jnp.int32, shape, 0) + start


def pack_kernel(count, blk, *refs):
    sources, p_ref = refs[:2 * count], refs[2 * count]
    half, block_rows = sources[0].shape[:2]
    per_peer = count * MOST
    for i in range(p_ref.shape[0]):
        j = pl.program_id(0) * p_ref.shape[0] + i
        for slot in range(per_peer):
            b = blk[j * per_peer + slot]
            place = lax.rem(b, half)
            low = sources[slot // MOST * 2][place]
            high = sources[slot // MOST * 2 + 1][place]
            first = jnp.full(low.shape, b, jnp.int32) < half
            p_ref[i, pl.ds(slot * block_rows, block_rows), :] = jnp.where(first, low, high)


def pack(sources, blk, plane, per=4):
    shape = sources[0].shape
    count = len(sources) // 2
    width = count * MOST * shape[1]
    out = jax.ShapeDtypeStruct((plane, width, shape[2]), BF16)
    return pl.pallas_call(
        functools.partial(pack_kernel, count),
        grid_spec=pltpu.PrefetchScalarGridSpec(
            num_scalar_prefetch=1,
            grid=(plane // per,),
            in_specs=[pl.BlockSpec(shape, lambda j, blk: (0, 0, 0))] * len(sources),
            out_specs=pl.BlockSpec((per,) + out.shape[1:], lambda j, blk: (j, 0, 0)),
        ),
        out_shape=out,
        compiler_params=pltpu.CompilerParams(vmem_limit_bytes=SMALL),
        cost_estimate=pl.CostEstimate(
            flops=0, bytes_accessed=4 * plane * width * shape[2], transcendentals=0
        ),
        name="pack",
    )(blk, *sources)


def forward_kernel(p_ref, t_ref, tgt_ref, stat_ref, s_all):
    for i in range(p_ref.shape[0]):
        s_ref = s_all.at[i]
        q = p_ref[i]
        items = t_ref.shape[1]
        width = q.shape[0]
        tgt = tgt_ref[i]
        high = jnp.full((8, width), -jnp.inf, F32)
        pick = jnp.zeros((8, width), F32)
        for start in range(0, items, TILE):
            rows = t_ref[i, pl.ds(start, TILE), :]
            s = lax.dot_general(rows, q, NT, preferred_element_type=F32)
            s_ref[pl.ds(start, TILE), :] = s
            high = jnp.maximum(high, jnp.max(s.reshape(TILE // 8, 8, width), axis=0))
            hit = jnp.where(tile_ids(start, s.shape) == tgt, s, 0.0)
            pick = pick + jnp.sum(hit.reshape(TILE // 8, 8, width), axis=0)
        top = jnp.max(high, axis=0, keepdims=True)
        mass = jnp.zeros((8, width), F32)
        for start in range(0, items, TILE):
            e = jnp.exp(s_ref[pl.ds(start, TILE), :] - top)
            mass = mass + jnp.sum(e.reshape(TILE // 8, 8, width), axis=0)
        stat_ref[0, i] = top + jnp.log(jnp.sum(mass, axis=0, keepdims=True))
        stat_ref[1, i] = jnp.sum(pick, axis=0, keepdims=True)


def forward(packed, targets, tables, per=2):
    planes, items, features = tables.shape
    width = packed.shape[1]
    return pl.pallas_call(
        forward_kernel,
        grid=(planes // per,),
        in_specs=[
            pl.BlockSpec((per, width, features), lambda j: (j, 0, 0)),
            pl.BlockSpec((per, items, features), lambda j: (j, 0, 0)),
            pl.BlockSpec((per, 1, width), lambda j: (j, 0, 0)),
        ],
        out_specs=pl.BlockSpec((2, per, 1, width), lambda j: (0, j, 0, 0)),
        out_shape=jax.ShapeDtypeStruct((2, planes, 1, width), F32),
        scratch_shapes=[pltpu.VMEM((per, items, width), F32)],
        compiler_params=pltpu.CompilerParams(vmem_limit_bytes=LARGE),
        cost_estimate=pl.CostEstimate(
            flops=40 * planes * width * items * features,
            bytes_accessed=planes * items * features * 2 + planes * width * features * 2,
            transcendentals=planes * width * items,
        ),
        name="forward",
    )(packed, tables, targets)


def query_kernel(blk, p_ref, t_ref, line_ref, g_ref, c_all, acc_ref):
    step = pl.program_id(0)
    sources, _, block_rows, _ = acc_ref.shape
    per = p_ref.shape[0]
    slots = sources * MOST

    @pl.when(step == 0)
    def _():
        acc_ref[...] = jnp.zeros_like(acc_ref)

    for i in range(per):
        q = p_ref[i]
        lse = line_ref[i, 0:1, :]
        tgt = line_ref[i, 1:2, :].astype(jnp.int32)
        for start in range(0, t_ref.shape[1], TILE):
            rows = t_ref[i, pl.ds(start, TILE), :]
            s = lax.dot_general(rows, q, NT, preferred_element_type=F32)
            e = jnp.exp(s - lse)
            c = jnp.where(tile_ids(start, s.shape) == tgt, e - 1.0, e)
            c_all[i, pl.ds(start, TILE), :] = c.astype(BF16)
        g = lax.dot_general(c_all[i], t_ref[i], TN, preferred_element_type=F32)
        for slot in range(slots):
            b = blk[(step * per + i) * slots + slot]
            acc_ref[slot // MOST, b] += g[slot * block_rows:(slot + 1) * block_rows, :]

    @pl.when(step == pl.num_programs(0) - 1)
    def _():
        z = blk[pl.num_programs(0) * per * slots]
        for i in range(sources):
            g_ref[lax.rem(z + i, sources)] = acc_ref[i].astype(BF16)


def query_parts(packed, blk, lines, tables, sources, blocks, block_rows, per=4):
    planes, items, features = tables.shape
    width = packed.shape[1]
    out = jax.ShapeDtypeStruct((sources, blocks, block_rows, features), BF16)
    return pl.pallas_call(
        query_kernel,
        grid_spec=pltpu.PrefetchScalarGridSpec(
            num_scalar_prefetch=1,
            grid=(planes // per,),
            in_specs=[
                pl.BlockSpec((per, width, features), lambda j, blk: (j, 0, 0)),
                pl.BlockSpec((per, items, features), lambda j, blk: (j, 0, 0)),
                pl.BlockSpec((per, 2, width), lambda j, blk: (j, 0, 0)),
            ],
            out_specs=pl.BlockSpec(out.shape, lambda j, blk: (0, 0, 0, 0)),
            scratch_shapes=[pltpu.VMEM((per, items, width), BF16), pltpu.VMEM(out.shape, F32)],
        ),
        out_shape=out,
        compiler_params=pltpu.CompilerParams(vmem_limit_bytes=LARGE),
        cost_estimate=pl.CostEstimate(flops=1 << 20, bytes_accessed=1 << 20, transcendentals=0),
        name="query_parts",
    )(blk, packed, tables, lines)


def item_kernel(where, q_ref, line_ref, t_ref, *outs):
    start = where[pl.program_id(0)] * t_ref.shape[0]
    table16 = t_ref[...].astype(BF16)
    total = None
    for source in range(q_ref.shape[0]):
        q = q_ref[source]
        line = line_ref[source]
        lse = line[0:1, :]
        tgt = line[1:2, :].astype(jnp.int32)
        s = lax.dot_general(table16, q, NT, preferred_element_type=F32)
        e = jnp.exp(s - lse)
        c = jnp.where(tile_ids(start, s.shape) == tgt, e - 1.0, e).astype(BF16)
        part = jnp.dot(c, q, preferred_element_type=F32)
        total = part if total is None else total + part
    pieces = t_ref.shape[0] // outs[0].shape[0]
    for place in range(len(outs) // pieces):

        @pl.when(pl.program_id(0) == place)
        def _():
            for n in range(pieces):
                out = outs[place * pieces + n]
                out[...] = total[n * out.shape[0]:(n + 1) * out.shape[0]]


def item_parts(places, pieces, x, rows, lines, table, quarters):
    count, width, features = rows.shape
    span = table.shape[0] // quarters
    share = len(places)
    out = jax.ShapeDtypeStruct((span // pieces, features), F32)
    return pl.pallas_call(
        item_kernel,
        grid_spec=pltpu.PrefetchScalarGridSpec(
            num_scalar_prefetch=1,
            grid=(share,),
            in_specs=[
                pl.BlockSpec(rows.shape, lambda i, o: (0, 0, 0)),
                pl.BlockSpec(lines.shape, lambda i, o: (0, 0, 0)),
                pl.BlockSpec((span, features), lambda i, o: (o[i], 0)),
            ],
            out_specs=[pl.BlockSpec(out.shape, lambda i, o: (0, 0))] * (share * pieces),
        ),
        out_shape=[out] * (share * pieces),
        compiler_params=pltpu.CompilerParams(vmem_limit_bytes=SMALL),
        cost_estimate=pl.CostEstimate(
            flops=4 * share * span * count * width * features,
            bytes_accessed=2 * count * width * features + share * span * features * 6,
            transcendentals=share * span * count * width,
        ),
        name="item_parts",
    )((jnp.array(places, jnp.int32) + x) % quarters, rows, lines, table)


def write_rows(summed, start, t_ref, a_ref, nt_ref, na_ref):
    span = pl.ds(start, summed.shape[0])
    accum = a_ref[span, :] + summed * summed
    na_ref[span, :] = accum
    nt_ref[span, :] = t_ref[span, :] - 0.5 * summed / jnp.sqrt(accum)


def update_kernel(where, own, after, before, t_ref, a_ref, nt_ref, na_ref):
    for place, ref in enumerate((own, after, before)):

        @pl.when(pl.program_id(0) == place)
        def _():
            write_rows(ref[...], 0, t_ref, a_ref, nt_ref, na_ref)


def far_kernel(where, far_a, far_b, t_ref, a_ref, nt_in, na_in, nt_ref, na_ref):
    write_rows(far_a[...], 0, t_ref, a_ref, nt_ref, na_ref)
    write_rows(far_b[...], far_a.shape[0], t_ref, a_ref, nt_ref, na_ref)


def update(body, places, x, sums, table, accum, quarters, held=()):
    items, features = table.shape
    sizes = [pl.BlockSpec(v.shape, lambda i, o: (0, 0)) for v in sums]
    block = pl.BlockSpec((items // quarters, features), lambda i, o: (o[i], 0))
    first = 3 + len(sums)
    return pl.pallas_call(
        body,
        grid_spec=pltpu.PrefetchScalarGridSpec(
            num_scalar_prefetch=1,
            grid=(len(places),),
            in_specs=sizes + [block] * 2 + [pl.BlockSpec(memory_space=pl.ANY)] * len(held),
            out_specs=[block] * 2,
        ),
        out_shape=[jax.ShapeDtypeStruct(table.shape, F32)] * 2,
        input_output_aliases={first + i: i for i in range(len(held))},
        compiler_params=pltpu.CompilerParams(vmem_limit_bytes=SMALL),
        name="update",
    )((jnp.array(places, jnp.int32) + x) % quarters, *sums, table, accum, *held)


def cast_kernel(g_ref, out_ref):
    out_ref[...] = g_ref[...].astype(F32)


def cast_rows(grads, steps=2):
    rows, features = grads.shape
    block = pl.BlockSpec((rows // steps, features), lambda i: (i, 0))
    return pl.pallas_call(
        cast_kernel,
        grid=(steps,),
        in_specs=[block],
        out_specs=block,
        out_shape=jax.ShapeDtypeStruct(grads.shape, F32),
        compiler_params=pltpu.CompilerParams(vmem_limit_bytes=LARGE),
        name="cast_rows",
    )(grads)


def local(queries, clusters, positives, owner_of, table, accum):
    z_size = lax.axis_size("z")
    x_size = lax.axis_size("x")
    z = lax.axis_index("z")
    x = lax.axis_index("x").reshape(1)
    local_rows, features = queries.shape
    block_count, picks = clusters.shape
    block_rows = local_rows // block_count
    items = table.shape[1]
    owners = owner_of.shape[0]
    plane = owners // z_size
    pair_count = block_count * picks

    tables = lax.all_gather(table[0].astype(BF16), PLANE)

    here = queries.reshape(2, block_count // 2, block_rows, features)
    by_source = [[None] * 2 for _ in range(z_size)]
    for half in range(2):
        right = left = by_source[0][half] = here[half]
        for hop in range(1, z_size // 2 + 1):
            right = by_source[z_size - hop][half] = shift(right, "z", 1)
            if hop < z_size // 2:
                left = by_source[hop][half] = shift(left, "z", -1)

    flat_lists = clusters.reshape(pair_count)
    catalog_ids = jnp.arange(owners, dtype=jnp.int32)
    lookup = flat_lists[:, None] == catalog_ids[None, :]
    destination = jnp.sum(jnp.where(lookup, owner_of[None, :], 0), axis=1)
    pair_ids = jnp.arange(pair_count, dtype=jnp.int32)
    earlier = (destination[:, None] == destination[None, :]) & (
        pair_ids[:, None] > pair_ids[None, :]
    )
    rank_in = jnp.sum(earlier.astype(jnp.int32), axis=1)
    slot_of_pair = destination * MOST + rank_in
    slot_count = owners * MOST
    matches = slot_of_pair[None, :] == jnp.arange(slot_count, dtype=jnp.int32)[:, None]
    filled = jnp.any(matches, axis=1)
    source_pair = jnp.sum(jnp.where(matches, pair_ids[None, :], 0), axis=1)
    which_block = source_pair // picks
    which_pick = source_pair % picks
    chosen = positives.reshape(block_count, block_rows)[which_block]
    inside = filled[:, None] & (chosen // items == which_pick[:, None])
    send_targets = jnp.where(inside, chosen - which_pick[:, None] * items, -1)
    block_or_none = jnp.where(filled, which_block, -1)
    per_plane = plane * MOST
    meta = jnp.concatenate(
        [
            send_targets.reshape(z_size, per_plane * block_rows),
            block_or_none.reshape(z_size, per_plane),
            jnp.broadcast_to(slot_of_pair[None, :], (z_size, pair_count)),
        ],
        axis=1,
    )
    meta, _ = lax.optimization_barrier((meta, by_source[5][0]))
    got = lax.all_to_all(meta, "z", 0, 0, tiled=True)
    order = jnp.arange(z_size, dtype=jnp.int32)
    got = got[(z + order) % z_size]
    width = z_size * MOST * block_rows
    cut = per_plane * block_rows
    targets = got[:, :cut].reshape(z_size, plane, MOST, block_rows)
    targets = targets.transpose(1, 0, 2, 3).reshape(plane, 1, width)
    named = got[:, cut:cut + per_plane].reshape(z_size, plane, MOST).transpose(1, 0, 2)
    named = named.reshape(plane * per_plane)
    blk = jnp.maximum(named, 0)

    pair_slot = got[:, cut + per_plane:]
    pair_owner = pair_slot // MOST
    pair_from = (pair_owner // plane - z) % z_size
    pair_place = (order[:, None] - pair_from) % z_size
    pair_group = pair_from % 4
    pair_second = jnp.where(pair_group == 3, 1 - pair_from // 4, pair_from // 4)
    pair_row = (pair_group * 2 + pair_second) * plane + pair_owner % plane
    pair_row = (pair_row * z_size + pair_place) * MOST + pair_slot % MOST

    packed = pack([part for pair in by_source for part in pair], blk, plane)
    rows = lax.all_to_all(packed, PLANE, 0, 0, tiled=True)
    stats = forward(packed, targets, tables)

    both = jnp.stack([stats, shift(stats, "z", -4)])
    all_stats = jnp.stack([both] + [shift(both, "z", -e) for e in (1, 2, -1)])
    all_stats = all_stats.reshape(z_size, 2, -1)
    part = all_stats[:, 0].reshape(-1, block_rows)[pair_row.reshape(-1)]
    part, rows = lax.optimization_barrier((part, rows))
    part = part.reshape(z_size, block_count, picks, block_rows)
    pick = all_stats[:, 1].reshape(-1, block_rows)[pair_row[0]]
    pick = pick.reshape(block_count, picks, block_rows)
    top = jnp.max(part, axis=2)
    lse = top + jnp.log(jnp.sum(jnp.exp(part - top[:, :, None]), axis=2))
    losses = (lse[0] - jnp.sum(pick, axis=1)).reshape(local_rows)
    lse_rows = lse.reshape(z_size * block_count, block_rows)
    first = jnp.arange(z_size, dtype=jnp.int32).reshape(1, z_size, 1) * block_count
    lse_at = (blk.reshape(plane, z_size, MOST) + first).reshape(-1)
    lse_slots = jnp.where(named[:, None] < 0, F32(EMPTY), lse_rows[lse_at])
    lines = jnp.concatenate(
        [lse_slots.reshape(plane, 1, width), targets.astype(F32)], axis=1
    )

    grads = query_parts(
        packed, jnp.concatenate([blk, z.reshape(1)]), lines, tables, z_size, block_count, block_rows
    )
    grads, lines = lax.optimization_barrier((grads, lines))
    query_grads = cast_rows(lax.psum_scatter(grads, "z").reshape(local_rows, features))
    got_lines = lax.all_to_all(lines, PLANE, 0, 0, tiled=True)

    far_a, far_b = item_parts((2,), 2, x, rows, got_lines, table[0], x_size)
    far_a, far_b, got_lines = lax.optimization_barrier((far_a, far_b, got_lines))
    after, before = item_parts((1, 3), 1, x, rows, got_lines, table[0], x_size)
    after, before, got_lines = lax.optimization_barrier((after, before, got_lines))
    (own,) = item_parts((0,), 1, x, rows, got_lines, table[0], x_size)
    half = far_a.shape[0]
    far_a = shift(far_a, "x", 1)
    far_b = shift(far_b, "x", -1)
    after = shift(jnp.concatenate([after[:half] + far_a, after[half:]]), "x", 1)
    before = shift(jnp.concatenate([before[:half], before[half:] + far_b]), "x", -1)
    own, losses = lax.optimization_barrier((own + after + before, losses))
    before = shift(own, "x", 1)
    after = shift(own, "x", -1)
    far_a = shift(before[:half], "x", 1)
    far_b = shift(after[half:], "x", -1)
    held = update(update_kernel, (0, 1, 3), x, (own, after, before), table[0], accum[0], x_size)
    new_table, new_accum = update(
        far_kernel, (2,), x, (far_a, far_b), table[0], accum[0], x_size, held
    )
    return (losses, query_grads, new_table[None], new_accum[None])


def solution(mesh):
    axes = ("z", "y", "c", "x")
    split = Mesh(mesh.devices.reshape(8, 4, 2, 4), axes)
    placed = (
        P(axes, None),
        P(axes, None),
        P(axes),
        P(),
        P(axes[:3], None, None),
        P(axes[:3], None, None),
    )
    return jax.shard_map(
        local,
        mesh=split,
        in_specs=placed,
        out_specs=(
            P(axes),
            P(axes, None),
            P(axes[:3], None, None),
            P(axes[:3], None, None),
        ),
        check_vma=False,
    )
```
